32 devices in a mesh: groups: 2 (over y), ctx: 4 (over z), head: 2 (over x), sub: 2 (over core).
Axes of the slice: x: 2, y: 2, z: 4, core: 2. Of those that a mesh axis runs over, the one named last changes fastest.
Arguments:
- queries: bfloat16 [2048, 64, 128], P(('groups', 'ctx', 'sub'), 'head'), parts along dimension 0, may hold values from -6 to 6
- keys: bfloat16 [2048, 4, 128], P(('groups', 'ctx', 'sub'), 'head'), parts along dimension 0, may hold values from -6 to 6
- values: bfloat16 [2048, 4, 128], P(('groups', 'ctx', 'sub'), 'head'), parts along dimension 0, may hold values from -6 to 6
- grad_out: bfloat16 [2048, 64, 128], P(('groups', 'ctx', 'sub'), 'head'), parts along dimension 0, may hold values from -9 to 9
- row_lse: float32 [2048, 64], P(('groups', 'ctx', 'sub'), 'head'), parts along dimension 0, may hold values from 5.5 to 6.5
- row_delta: float32 [2048, 64], P(('groups', 'ctx', 'sub'), 'head'), parts along dimension 0, may hold values from -24 to 24
- doc_ids: int32 [2048], P(('groups', 'ctx', 'sub')), parts along dimension 0, may hold values from 0 to 3, never falling along the last dimension, each value on 1 to 512 neighbouring positions
- pairs: int32 [16, 2], P('groups'), parts along dimension 0, may hold values from 0 to 7, as said below
Outputs:
- grad_queries: float32 [2048, 64, 128], P(('groups', 'ctx', 'sub'), 'head'), parts along dimension 0
- grad_keys: float32 [2048, 4, 128], P(('groups', 'ctx', 'sub'), 'head'), parts along dimension 0
- grad_values: float32 [2048, 4, 128], P(('groups', 'ctx', 'sub'), 'head'), parts along dimension 0
The draws below stay inside these ranges and needn't reach their ends.
There are 2 independent parts, one for each index of `groups`. The reference program is written for one: setup_inputs(seed, part) draws one part's arguments, and reference() takes and returns one part's arrays. A program takes and returns all parts, laid end to end along the dimension named above; each array names one. Nothing has to cross between parts.
Inputs may be any that keep to these rules, and one draw needn't show every extreme that they name: `pairs`: row c holds two different span indices, neither equal to c. `doc_ids`: never falls along the tokens; every document appears.
All inputs are finite; a program needn't handle non-finite values.
Results may differ from the reference program's by a relative error of at most 0.0046.
Values may be sent and summed in bfloat16 or wider, within the bound.
No kernel may reach another device: no remote copies, remote signals or barrier semaphores. Data moves between devices by JAX's collectives and lax.ppermute only.
A program may use at most 64 MiB of HBM per device.

```python
import math
import jax
import jax.numpy as jnp
import numpy as np
from jax import lax

QH = 64
KVH = 4
HD = 128
TOK_DEV = 128
DOCS = 4
NCHUNK = 8
TOKENS = 1024


def draw_pairs(key, part):
    key_first, key_second = jax.random.split(jax.random.fold_in(key, 11))
    first = jax.random.randint(key_first, (NCHUNK,), 0, NCHUNK - 1)
    first = first.at[0].set(NCHUNK - 2).at[NCHUNK - 1].set(0)
    second = jax.random.randint(key_second, (NCHUNK,), 0, NCHUNK - 2)
    span_rows = jnp.arange(NCHUNK, dtype=jnp.int32)
    listed_one = (span_rows + 1 + first) % NCHUNK
    listed_two = (span_rows + 1 + (first + 1 + second) % (NCHUNK - 1)) % NCHUNK
    return jnp.stack([listed_one, listed_two], axis=1).astype(jnp.int32)


def level_of(own_key, extent, pieces, low, top_value):
    gain, own = 1.0, jax.random.fold_in(own_key, 6)
    for position, parts in pieces:
        heights = jnp.exp(jax.random.uniform(jax.random.fold_in(own, position), (parts,), jnp.float32, low / len(pieces), top_value / len(pieces)))
        gain = gain * jnp.repeat(heights, extent[position] // parts).reshape([-1 if axis == position else 1 for axis in range(len(extent))])
    return gain


def profile(number_of, total, most, lean):
    weights = [(1 << 20) // math.isqrt(standing ** lean) + 1 for standing in range(2, number_of + 1)]
    spare, given = total - most - (number_of - 1), [1] * (number_of - 1)
    while spare > 0:
        free = [i for i in range(number_of - 1) if given[i] < most]
        pool, remaining = sum([weights[i] for i in free]), spare
        for i in free:
            addition = min(most - given[i], max(1, remaining * weights[i] // pool), spare)
            given[i] = given[i] + addition
            spare = spare - addition
    return np.array([most] + given)


def ragged(rng, count, total, most, slope):
    if count == 2:
        one = jax.random.randint(rng, (), max(1, total - most), min(most, total - 1) + 1)
        return jnp.stack([one, total - one])
    lengths = jnp.asarray(profile(count, total, most, slope), jnp.int32)
    pairs = (count - 1) // 2
    donor, taker = lengths[1:1 + 2 * pairs:2], lengths[2:2 + 2 * pairs:2]
    slack = jnp.minimum(donor - 1, most - taker)
    passed = jax.random.randint(jax.random.fold_in(rng, 1), (pairs,), 0, 1 << 20) % (slack + 1)
    lengths = lengths.at[1:1 + 2 * pairs:2].set(donor - passed).at[2:2 + 2 * pairs:2].set(taker + passed)
    return lengths[jax.random.permutation(jax.random.fold_in(rng, 2), count)]


def noise(key, dims, deviation, most, pieces=(), kind=jnp.bfloat16):
    array = jax.random.normal(key, dims, jnp.float32) * deviation
    if len(pieces) > 0:
        array = level_of(key, dims, pieces, -0.22, 0.18) * array
    return jnp.clip(array, min=-most, max=most).astype(kind)


def setup_inputs(seed: int = 0, part: int = 0) -> dict:
    key_of = jax.random.split(jax.random.key(seed), 9)
    part_splits = jax.random.split(jax.random.fold_in(key_of[8], part), 9)
    return {
        "queries": noise(part_splits[0], (TOKENS, QH, HD), 1.0, 6.0, ((0, 8), (1, 2))),
        "keys": noise(part_splits[1], (TOKENS, KVH, HD), 1.0, 6.0, ((0, 8), (1, 2))),
        "values": noise(part_splits[2], (TOKENS, KVH, HD), 1.0, 6.0, ((0, 8), (1, 2))),
        "grad_out": noise(part_splits[3], (TOKENS, QH, HD), 1.5, 9.0, ((0, 8), (1, 2))),
        "row_lse": jnp.clip(5.5 + 1.0 * jax.random.uniform(part_splits[4], (TOKENS, QH), jnp.float32) ** level_of(part_splits[4], (TOKENS, QH), ((0, 8), (1, 2)), -0.2, 0.2), 5.5, 6.5),
        "row_delta": noise(part_splits[5], (TOKENS, QH), 4.0, 24.0, ((0, 8), (1, 2)), jnp.float32),
        "doc_ids": jnp.searchsorted(jnp.cumsum(ragged(part_splits[6], DOCS, TOKENS, TOKENS // 2, 0)), jnp.arange(TOKENS), side="right").astype(jnp.int32),
        "pairs": draw_pairs(jax.random.fold_in(jax.random.fold_in(key_of[8], part), 71), part),
    }


def block_terms(query_blk, upstream, log_norm, row_terms, key_blk, value_blk, allowed, factor):
    query_wide = query_blk.astype(jnp.float32)
    upstream_wide = upstream.astype(jnp.float32)
    key_wide = key_blk.astype(jnp.float32)
    value_wide = value_blk.astype(jnp.float32)
    scores = jnp.einsum('tghd,kgd->tghk', query_wide, key_wide) * factor
    probs = jnp.exp(scores - log_norm[..., None])
    if allowed is not None:
        probs = jnp.where(allowed[:, None, None, :], probs, 0.0)
    grad_probs = jnp.einsum('tghd,kgd->tghk', upstream_wide, value_wide)
    grad_scores = probs * (grad_probs - row_terms[..., None])
    probs_low = lax.optimization_barrier(probs.astype(jnp.bfloat16)).astype(jnp.float32)
    scores_low = lax.optimization_barrier(grad_scores.astype(jnp.bfloat16)).astype(jnp.float32)
    grad_val = jnp.einsum('tghk,tghd->kgd', probs_low, upstream_wide)
    grad_key = jnp.einsum('tghk,tghd->kgd', scores_low, query_wide) * factor
    grad_query = jnp.einsum('tghk,kgd->tghd', scores_low, key_wide) * factor
    return grad_query, grad_key, grad_val


def reference(queries, keys, values, grad_out, row_lse, row_delta, doc_ids, pairs):
    grouped = QH // KVH
    factor = HD ** -0.5
    query_all = queries.reshape(NCHUNK, TOK_DEV, KVH, grouped, HD)
    upstream_all = grad_out.reshape(NCHUNK, TOK_DEV, KVH, grouped, HD)
    keys_all = keys.reshape(NCHUNK, TOK_DEV, KVH, HD)
    values_all = values.reshape(NCHUNK, TOK_DEV, KVH, HD)
    norm_all = row_lse.reshape(NCHUNK, TOK_DEV, KVH, grouped)
    terms_all = row_delta.reshape(NCHUNK, TOK_DEV, KVH, grouped)
    docs_all = doc_ids.reshape(NCHUNK, TOK_DEV)
    positions = jnp.arange(TOK_DEV, dtype=jnp.int32)
    causal = positions[:, None] >= positions[None, :]

    def advance(totals, span_idx):
        key_total, value_total = totals
        query_blk = query_all[span_idx]
        upstream = upstream_all[span_idx]
        log_norm = norm_all[span_idx]
        row_terms = terms_all[span_idx]
        docs = docs_all[span_idx]
        allowed = causal & (docs[:, None] == docs[None, :])
        query_sum, key_part, value_part = block_terms(query_blk, upstream, log_norm, row_terms, keys_all[span_idx], values_all[span_idx], allowed, factor)
        key_total = key_total.at[span_idx].add(key_part)
        value_total = value_total.at[span_idx].add(value_part)
        for which in range(2):
            target = pairs[span_idx, which]
            query_part, key_part, value_part = block_terms(query_blk, upstream, log_norm, row_terms, keys_all[target], values_all[target], None, factor)
            query_sum = query_sum + query_part
            key_total = key_total.at[target].add(key_part)
            value_total = value_total.at[target].add(value_part)
        return (key_total, value_total), query_sum

    zero_grads = jnp.zeros((NCHUNK, TOK_DEV, KVH, HD), jnp.float32)
    (key_total, value_total), query_grads = lax.scan(advance, (zero_grads, zero_grads), jnp.arange(NCHUNK, dtype=jnp.int32))
    return (query_grads.reshape(TOKENS, QH, HD), key_total.reshape(TOKENS, KVH, HD), value_total.reshape(TOKENS, KVH, HD))
```

```python
import functools

import jax
import jax.numpy as jnp
from jax import lax
from jax.experimental import pallas as pl
from jax.experimental.pallas import tpu as pltpu
from jax.sharding import PartitionSpec as P

QH = 64
KVH = 4
LOG2E = 1.4426950408889634
ROWS = 512
VMEM_LIMIT = 24 * 1024 * 1024


def rows_dot(left, right):
    return lax.dot_general(left, right, (((1,), (1,)), ((), ())), preferred_element_type=jnp.float32)


def tile_terms(key_blk, value_blk, query_blk, upstream, log_norm, row_terms, allowed, factor):
    scores = rows_dot(key_blk, query_blk)
    probs = jnp.exp2(scores * (factor * LOG2E) - log_norm * LOG2E)
    if allowed is not None:
        probs = jnp.where(allowed, probs, 0.0)
    grad_probs = rows_dot(value_blk, upstream)
    grad_scores = probs * (grad_probs - row_terms)
    return probs.astype(jnp.bfloat16), grad_scores.astype(jnp.bfloat16)


def chunks(query_ref, rows):
    tokens, grouped, head_dim = query_ref.shape
    step = rows // grouped
    return [(i, slice(i * step, (i + 1) * step), slice(i * rows, (i + 1) * rows)) for i in range(tokens // step)]


def local_kernel(factor, rows, kv_ref, query_ref, up_ref, norm_ref, term_ref, docs_ref, doc_col_ref,
                 dkv_ref, dq_ref):
    tokens, grouped, head_dim = query_ref.shape
    key_blk, value_blk = kv_ref[0, 0], kv_ref[1, 0]
    grad_key = jnp.zeros((tokens, head_dim), jnp.float32)
    grad_val = jnp.zeros((tokens, head_dim), jnp.float32)
    for i, toks, cols in chunks(query_ref, rows):
        query_blk = query_ref[toks].reshape(rows, head_dim)
        upstream = up_ref[toks].reshape(rows, head_dim)
        position = lax.broadcasted_iota(jnp.int32, (tokens, rows), 1) // grouped + toks.start
        allowed = (lax.broadcasted_iota(jnp.int32, (tokens, rows), 0) <= position) & (
            doc_col_ref[...] == docs_ref[:, cols]
        )
        probs, grads = tile_terms(
            key_blk, value_blk, query_blk, upstream, norm_ref[0, :, cols], term_ref[0, :, cols], allowed, factor
        )
        grad_val += jnp.dot(probs, upstream, preferred_element_type=jnp.float32)
        grad_key += jnp.dot(grads, query_blk, preferred_element_type=jnp.float32)
        grad_query = lax.dot_general(
            grads, key_blk, (((0,), (0,)), ((), ())), preferred_element_type=jnp.float32
        )
        dq_ref[toks] = (grad_query * factor).reshape(rows // grouped, grouped, head_dim)
    dkv_ref[0, 0] = grad_key * factor
    dkv_ref[1, 0] = grad_val


def listed_kernel(factor, rows, index_ref, one_ref, two_ref, query_ref, up_ref, norm_ref, term_ref, dkv_ref):
    tokens, grouped, head_dim = query_ref.shape
    key_blk = jnp.concatenate([one_ref[0, 0, 0], two_ref[0, 0, 0]], axis=0)
    value_blk = jnp.concatenate([one_ref[0, 1, 0], two_ref[0, 1, 0]], axis=0)
    grad_key = jnp.zeros((2 * tokens, head_dim), jnp.float32)
    grad_val = jnp.zeros((2 * tokens, head_dim), jnp.float32)
    for i, toks, cols in chunks(query_ref, rows):
        query_blk = query_ref[toks].reshape(rows, head_dim)
        upstream = up_ref[toks].reshape(rows, head_dim)
        probs, grads = tile_terms(
            key_blk, value_blk, query_blk, upstream, norm_ref[0, :, cols], term_ref[0, :, cols], None, factor
        )
        grad_val += jnp.dot(probs, upstream, preferred_element_type=jnp.float32)
        grad_key += jnp.dot(grads, query_blk, preferred_element_type=jnp.float32)
    grad_key = (grad_key * factor).astype(dkv_ref.dtype)
    grad_val = grad_val.astype(dkv_ref.dtype)
    for which in range(2):
        dkv_ref[which, 0, 0] = grad_key[which * tokens:(which + 1) * tokens]
        dkv_ref[which, 1, 0] = grad_val[which * tokens:(which + 1) * tokens]


def query_kernel(factor, rows, index_ref, one_ref, two_ref, query_ref, up_ref, norm_ref, term_ref, near_ref, dq_ref):
    tokens, grouped, head_dim = query_ref.shape
    key_blk = jnp.concatenate([one_ref[0, 0, 0], two_ref[0, 0, 0]], axis=0)
    value_blk = jnp.concatenate([one_ref[0, 1, 0], two_ref[0, 1, 0]], axis=0)
    for i, toks, cols in chunks(query_ref, rows):
        query_blk = query_ref[toks].reshape(rows, head_dim)
        upstream = up_ref[toks].reshape(rows, head_dim)
        probs, grads = tile_terms(
            key_blk, value_blk, query_blk, upstream, norm_ref[0, :, cols], term_ref[0, :, cols], None, factor
        )
        grad_query = lax.dot_general(
            grads, key_blk, (((0,), (0,)), ((), ())), preferred_element_type=jnp.float32
        )
        dq_ref[toks] = near_ref[toks] + (grad_query * factor).reshape(rows // grouped, grouped, head_dim)


def body(queries, keys, values, grad_out, row_lse, row_delta, doc_ids, pairs):
    tokens, heads, head_dim = queries.shape
    kv_heads = keys.shape[1]
    grouped = QH // KVH
    factor = head_dim ** (-0.5)
    ring = lax.axis_size("ctx")
    subs = lax.axis_size("sub")
    ctx = lax.axis_index("ctx")
    sub = lax.axis_index("sub")
    rows = min(ROWS, tokens * grouped)
    cols = tokens * grouped

    kv = jnp.stack([keys, values]).transpose(0, 2, 1, 3)
    norm = row_lse.reshape(tokens, kv_heads, grouped).transpose(1, 0, 2).reshape(kv_heads, 1, cols)
    term = row_delta.reshape(tokens, kv_heads, grouped).transpose(1, 0, 2).reshape(kv_heads, 1, cols)
    docs = jnp.repeat(doc_ids, grouped).reshape(1, cols)
    doc_col = doc_ids.reshape(tokens, 1)

    gathered = lax.all_gather(kv, ("ctx", "sub"), axis=0, tiled=False)
    index = lax.dynamic_index_in_dim(pairs, ctx * subs + sub, 0, keepdims=False)

    params = pltpu.CompilerParams(vmem_limit_bytes=VMEM_LIMIT, dimension_semantics=("arbitrary",))
    row_spec = lambda g, *_: (0, g, 0)
    lane_spec = lambda g, *_: (g, 0, 0)
    query_specs = [
        pl.BlockSpec((tokens, grouped, head_dim), row_spec),
        pl.BlockSpec((tokens, grouped, head_dim), row_spec),
        pl.BlockSpec((1, 1, cols), lane_spec),
        pl.BlockSpec((1, 1, cols), lane_spec),
    ]
    work = 2 * tokens * tokens * heads * head_dim
    moved = 2 * queries.size * 2

    near_kv, near_query = pl.pallas_call(
        functools.partial(local_kernel, factor, rows),
        grid=(kv_heads,),
        in_specs=[pl.BlockSpec((2, 1, tokens, head_dim), lambda g: (0, g, 0, 0))]
        + query_specs
        + [pl.BlockSpec((1, cols), lambda g: (0, 0)), pl.BlockSpec((tokens, 1), lambda g: (0, 0))],
        out_specs=[
            pl.BlockSpec((2, 1, tokens, head_dim), lambda g: (0, g, 0, 0)),
            pl.BlockSpec((tokens, grouped, head_dim), row_spec),
        ],
        out_shape=[
            jax.ShapeDtypeStruct((2, kv_heads, tokens, head_dim), jnp.float32),
            jax.ShapeDtypeStruct((tokens, heads, head_dim), jnp.float32),
        ],
        compiler_params=params,
        cost_estimate=pl.CostEstimate(flops=5 * work, bytes_accessed=2 * moved, transcendentals=0),
        name="local_block",
    )(kv, queries, grad_out, norm, term, docs, doc_col)

    far_specs = [
        pl.BlockSpec((1, 2, 1, tokens, head_dim), lambda g, idx: (idx[0], 0, g, 0, 0)),
        pl.BlockSpec((1, 2, 1, tokens, head_dim), lambda g, idx: (idx[1], 0, g, 0, 0)),
    ]
    far_kv = pl.pallas_call(
        functools.partial(listed_kernel, factor, rows),
        grid_spec=pltpu.PrefetchScalarGridSpec(
            num_scalar_prefetch=1,
            grid=(kv_heads,),
            in_specs=far_specs + query_specs,
            out_specs=pl.BlockSpec((2, 2, 1, tokens, head_dim), lambda g, idx: (0, 0, g, 0, 0)),
        ),
        out_shape=jax.ShapeDtypeStruct((2, 2, kv_heads, tokens, head_dim), jnp.bfloat16),
        compiler_params=params,
        cost_estimate=pl.CostEstimate(flops=8 * work, bytes_accessed=moved, transcendentals=0),
        name="listed_keys",
    )(index, gathered, gathered, queries, grad_out, norm, term)

    grad_queries = pl.pallas_call(
        functools.partial(query_kernel, factor, rows),
        grid_spec=pltpu.PrefetchScalarGridSpec(
            num_scalar_prefetch=1,
            grid=(kv_heads,),
            in_specs=far_specs + query_specs + [pl.BlockSpec((tokens, grouped, head_dim), row_spec)],
            out_specs=pl.BlockSpec((tokens, grouped, head_dim), row_spec),
        ),
        out_shape=jax.ShapeDtypeStruct((tokens, heads, head_dim), jnp.float32),
        compiler_params=params,
        cost_estimate=pl.CostEstimate(flops=6 * work, bytes_accessed=3 * moved, transcendentals=0),
        name="listed_queries",
    )(index, gathered, gathered, queries, grad_out, norm, term, near_query)

    swap = [(i, i ^ 1) for i in range(subs)]
    other_kv = lax.ppermute(far_kv, "sub", swap)
    other_index = lax.dynamic_index_in_dim(pairs, ctx * subs + (1 - sub), 0, keepdims=False)
    near = near_kv
    blocks = []
    for shift in range(ring):
        owner = lax.rem(ctx + shift, ring) * subs + sub
        block = jnp.zeros(kv.shape, jnp.float32)
        for which in range(2):
            block += jnp.where(index[which] == owner, far_kv[which].astype(jnp.float32), 0.0)
            block += jnp.where(other_index[which] == owner, other_kv[which].astype(jnp.float32), 0.0)
        blocks.append(block)
    near = near + blocks[0]
    for shift in range(1, ring):
        near = near + lax.ppermute(
            blocks[shift].astype(jnp.bfloat16), "ctx", [(i, (i + shift) % ring) for i in range(ring)]
        ).astype(jnp.float32)
    near = near.transpose(0, 2, 1, 3)
    return (grad_queries, near[0], near[1])


def solution(mesh):
    return jax.shard_map(
        body,
        mesh=mesh,
        in_specs=(
            P(("groups", "ctx", "sub"), "head", None),
            P(("groups", "ctx", "sub"), "head", None),
            P(("groups", "ctx", "sub"), "head", None),
            P(("groups", "ctx", "sub"), "head", None),
            P(("groups", "ctx", "sub"), "head"),
            P(("groups", "ctx", "sub"), "head"),
            P(("groups", "ctx", "sub")),
            P("groups", None),
        ),
        out_specs=(
            P(("groups", "ctx", "sub"), "head", None),
            P(("groups", "ctx", "sub"), "head", None),
            P(("groups", "ctx", "sub"), "head", None),
        ),
        check_vma=False,
    )
```

```python
import functools

import jax
import jax.numpy as jnp
from jax import lax
from jax.experimental import pallas as pl
from jax.experimental.pallas import tpu as pltpu
from jax.sharding import PartitionSpec as P

QH = 64
KVH = 4
LOG2E = 1.4426950408889634
ROWS = 512
VMEM_LIMIT = 24 * 1024 * 1024

VMEM_SPEC = pl.BlockSpec(memory_space=pltpu.VMEM)
SMEM_SPEC = pl.BlockSpec(memory_space=pltpu.SMEM)
ANY_SPEC = pl.BlockSpec(memory_space=pl.ANY)


def rows_dot(left, right):
    return lax.dot_general(left, right, (((1,), (1,)), ((), ())), preferred_element_type=jnp.float32)


def tile_terms(key_blk, value_blk, query_blk, upstream, log_norm, row_terms, allowed, factor):
    scores = rows_dot(key_blk, query_blk)
    probs = jnp.exp2(scores * (factor * LOG2E) - log_norm * LOG2E)
    if allowed is not None:
        probs = jnp.where(allowed, probs, 0.0)
    grad_probs = rows_dot(value_blk, upstream)
    grad_scores = probs * (grad_probs - row_terms)
    return probs.astype(jnp.bfloat16), grad_scores.astype(jnp.bfloat16)


def chunks(query_ref, rows):
    tokens, grouped, head_dim = query_ref.shape
    step = rows // grouped
    return [(i, slice(i * step, (i + 1) * step), slice(i * rows, (i + 1) * rows)) for i in range(tokens // step)]


def pack_kernel(key_ref, value_ref, kv_ref):
    for head in range(key_ref.shape[1]):
        kv_ref[0, head] = key_ref[:, head, :]
        kv_ref[1, head] = value_ref[:, head, :]


def choose_kernel(subs, place_ref, pairs_ref, *refs):
    *column, near_ref, out_ref = refs
    ring = len(column)
    ctx, sub = place_ref[0], place_ref[1]
    for which in range(2):
        span = pairs_ref[which, ctx * subs + (1 - sub)]
        shift = lax.rem(ctx - span // subs + ring, ring)
        for step in range(ring):
            @pl.when(shift == step)
            def _():
                out_ref[which] = column[step][...]


def far_blocks(subs, place_ref, pairs_ref, column, other_ref, far_ref):
    ring = len(column)
    ctx, sub = place_ref[0], place_ref[1]
    for which in range(2):
        span = pairs_ref[which, ctx * subs + sub]
        shift = lax.rem(ctx - span // subs + ring, ring)
        mine = lax.rem(span, subs) == sub

        @pl.when(jnp.logical_not(mine))
        def _():
            far_ref[which] = other_ref[which]

        for step in range(ring):
            @pl.when(mine & (shift == step))
            def _():
                far_ref[which] = column[step][...]


def local_kernel(factor, rows, kv_ref, query_ref, up_ref, norm_ref, term_ref, docs_ref, doc_col_ref,
                 dkv_ref, dq_ref):
    tokens, grouped, head_dim = query_ref.shape
    key_blk, value_blk = kv_ref[0, 0], kv_ref[1, 0]
    grad_key = jnp.zeros((tokens, head_dim), jnp.float32)
    grad_val = jnp.zeros((tokens, head_dim), jnp.float32)
    for i, toks, cols in chunks(query_ref, rows):
        query_blk = query_ref[toks].reshape(rows, head_dim)
        upstream = up_ref[toks].reshape(rows, head_dim)
        position = lax.broadcasted_iota(jnp.int32, (tokens, rows), 1) // grouped + toks.start
        allowed = (lax.broadcasted_iota(jnp.int32, (tokens, rows), 0) <= position) & (
            doc_col_ref[...] == docs_ref[:, cols]
        )
        probs, grads = tile_terms(
            key_blk, value_blk, query_blk, upstream, norm_ref[0, :, cols], term_ref[0, :, cols], allowed, factor
        )
        grad_val += jnp.dot(probs, upstream, preferred_element_type=jnp.float32)
        grad_key += jnp.dot(grads, query_blk, preferred_element_type=jnp.float32)
        grad_query = lax.dot_general(
            grads, key_blk, (((0,), (0,)), ((), ())), preferred_element_type=jnp.float32
        )
        dq_ref[toks] = (grad_query * factor).reshape(rows // grouped, grouped, head_dim)
    dkv_ref[0, 0] = grad_key * factor
    dkv_ref[1, 0] = grad_val


def listed_kernel(factor, rows, subs, place_ref, pairs_ref, *refs):
    (*column, other_ref, query_ref, up_ref, norm_ref, term_ref, dkv_ref, far_ref) = refs
    tokens, grouped, head_dim = query_ref.shape
    head = pl.program_id(0)

    @pl.when(head == 0)
    def _():
        far_blocks(subs, place_ref, pairs_ref, column, other_ref, far_ref)

    key_blk = jnp.concatenate([far_ref[0, 0, head], far_ref[1, 0, head]], axis=0)
    value_blk = jnp.concatenate([far_ref[0, 1, head], far_ref[1, 1, head]], axis=0)
    grad_key = jnp.zeros((2 * tokens, head_dim), jnp.float32)
    grad_val = jnp.zeros((2 * tokens, head_dim), jnp.float32)
    for i, toks, cols in chunks(query_ref, rows):
        query_blk = query_ref[toks].reshape(rows, head_dim)
        upstream = up_ref[toks].reshape(rows, head_dim)
        probs, grads = tile_terms(
            key_blk, value_blk, query_blk, upstream, norm_ref[0, :, cols], term_ref[0, :, cols], None, factor
        )
        grad_val += jnp.dot(probs, upstream, preferred_element_type=jnp.float32)
        grad_key += jnp.dot(grads, query_blk, preferred_element_type=jnp.float32)
    grad_key = (grad_key * factor).astype(dkv_ref.dtype)
    grad_val = grad_val.astype(dkv_ref.dtype)
    for which in range(2):
        dkv_ref[which, 0, 0] = grad_key[which * tokens:(which + 1) * tokens]
        dkv_ref[which, 1, 0] = grad_val[which * tokens:(which + 1) * tokens]


def query_kernel(factor, rows, subs, place_ref, pairs_ref, *refs):
    (*column, other_ref, query_ref, up_ref, norm_ref, term_ref, near_ref, dq_ref, far_ref) = refs
    tokens, grouped, head_dim = query_ref.shape
    head = pl.program_id(0)

    @pl.when(head == 0)
    def _():
        far_blocks(subs, place_ref, pairs_ref, column, other_ref, far_ref)

    key_blk = jnp.concatenate([far_ref[0, 0, head], far_ref[1, 0, head]], axis=0)
    value_blk = jnp.concatenate([far_ref[0, 1, head], far_ref[1, 1, head]], axis=0)
    for i, toks, cols in chunks(query_ref, rows):
        query_blk = query_ref[toks].reshape(rows, head_dim)
        upstream = up_ref[toks].reshape(rows, head_dim)
        probs, grads = tile_terms(
            key_blk, value_blk, query_blk, upstream, norm_ref[0, :, cols], term_ref[0, :, cols], None, factor
        )
        grad_query = lax.dot_general(
            grads, key_blk, (((0,), (0,)), ((), ())), preferred_element_type=jnp.float32
        )
        dq_ref[toks] = near_ref[toks] + (grad_query * factor).reshape(rows // grouped, grouped, head_dim)


def combine_kernel(subs, place_ref, pairs_ref, mine_ref, other_ref, *out_refs):
    ring = len(out_refs)
    ctx, sub = place_ref[0], place_ref[1]
    parts = []
    for ref, core in ((mine_ref, sub), (other_ref, 1 - sub)):
        for which in range(2):
            span = pairs_ref[which, ctx * subs + core]
            shift = lax.rem(span // subs - ctx + ring, ring)
            parts.append((ref, which, jnp.where(lax.rem(span, subs) == sub, shift, ring)))
    for step, out_ref in enumerate(out_refs):
        total = jnp.zeros(out_ref.shape, jnp.float32)
        for ref, which, shift in parts:
            total += jnp.where(shift == step, ref[which].astype(jnp.float32), 0.0)
        out_ref[...] = total.astype(out_ref.dtype)


def total_kernel(near_ref, own_ref, *refs):
    *column, dk_ref, dv_ref = refs
    for part, out_ref in enumerate((dk_ref, dv_ref)):
        for head in range(out_ref.shape[1]):
            total = near_ref[part, head] + own_ref[part, head]
            for ref in column:
                total += ref[part, head].astype(jnp.float32)
            out_ref[:, head, :] = total


def body(queries, keys, values, grad_out, row_lse, row_delta, doc_ids, pairs):
    tokens, heads, head_dim = queries.shape
    kv_heads = keys.shape[1]
    grouped = QH // KVH
    factor = head_dim ** (-0.5)
    ring = lax.axis_size("ctx")
    subs = lax.axis_size("sub")
    rows = min(ROWS, tokens * grouped)
    cols = tokens * grouped
    place = jnp.stack([lax.axis_index("ctx"), lax.axis_index("sub")])
    listed = pairs.T
    span_shape = (2, kv_heads, tokens, head_dim)

    def shifted(array, shift):
        return lax.ppermute(array, "ctx", [(i, (i + shift) % ring) for i in range(ring)])

    def swapped(array):
        return lax.ppermute(array, "sub", [(i, i ^ 1) for i in range(subs)])

    small = pltpu.CompilerParams(vmem_limit_bytes=VMEM_LIMIT)
    kv = pl.pallas_call(
        pack_kernel,
        in_specs=[VMEM_SPEC] * 2,
        out_specs=VMEM_SPEC,
        out_shape=jax.ShapeDtypeStruct(span_shape, jnp.bfloat16),
        compiler_params=small,
        name="pack",
    )(keys, values)
    column = [kv] + [shifted(kv, shift) for shift in range(1, ring)]

    norm = row_lse.reshape(tokens, kv_heads, grouped).transpose(1, 0, 2).reshape(kv_heads, 1, cols)
    term = row_delta.reshape(tokens, kv_heads, grouped).transpose(1, 0, 2).reshape(kv_heads, 1, cols)
    docs = jnp.repeat(doc_ids, grouped).reshape(1, cols)
    doc_col = doc_ids.reshape(tokens, 1)

    params = pltpu.CompilerParams(vmem_limit_bytes=VMEM_LIMIT, dimension_semantics=("arbitrary",))
    row_spec = pl.BlockSpec((tokens, grouped, head_dim), lambda g: (0, g, 0))
    lane_spec = pl.BlockSpec((1, 1, cols), lambda g: (g, 0, 0))
    query_specs = [row_spec, row_spec, lane_spec, lane_spec]
    work = 2 * tokens * tokens * heads * head_dim
    moved = 2 * queries.size * 2

    near_kv, near_query = pl.pallas_call(
        functools.partial(local_kernel, factor, rows),
        grid=(kv_heads,),
        in_specs=[pl.BlockSpec((2, 1, tokens, head_dim), lambda g: (0, g, 0, 0))]
        + query_specs
        + [pl.BlockSpec((1, cols), lambda g: (0, 0)), pl.BlockSpec((tokens, 1), lambda g: (0, 0))],
        out_specs=[pl.BlockSpec((2, 1, tokens, head_dim), lambda g: (0, g, 0, 0)), row_spec],
        out_shape=[
            jax.ShapeDtypeStruct(span_shape, jnp.float32),
            jax.ShapeDtypeStruct((tokens, heads, head_dim), jnp.float32),
        ],
        compiler_params=params,
        cost_estimate=pl.CostEstimate(flops=5 * work, bytes_accessed=2 * moved, transcendentals=0),
        name="local_block",
    )(kv, queries, grad_out, norm, term, docs, doc_col)

    chosen = pl.pallas_call(
        functools.partial(choose_kernel, subs),
        in_specs=[SMEM_SPEC] * 2 + [VMEM_SPEC] * ring + [ANY_SPEC],
        out_specs=VMEM_SPEC,
        out_shape=jax.ShapeDtypeStruct((2, *span_shape), jnp.bfloat16),
        compiler_params=small,
        name="choose",
    )(place, listed, *column, near_kv)
    other = swapped(chosen)

    far_specs = (
        [SMEM_SPEC] * 2
        + [pl.BlockSpec(span_shape, lambda g: (0, 0, 0, 0))] * ring
        + [pl.BlockSpec((2, *span_shape), lambda g: (0, 0, 0, 0, 0))]
        + query_specs
    )
    far_scratch = [pltpu.VMEM((2, *span_shape), jnp.bfloat16)]
    far_args = (place, listed, *column, other, queries, grad_out, norm, term)
    far_kv = pl.pallas_call(
        functools.partial(listed_kernel, factor, rows, subs),
        grid=(kv_heads,),
        in_specs=far_specs,
        out_specs=pl.BlockSpec((2, 2, 1, tokens, head_dim), lambda g: (0, 0, g, 0, 0)),
        out_shape=jax.ShapeDtypeStruct((2, *span_shape), jnp.bfloat16),
        scratch_shapes=far_scratch,
        compiler_params=params,
        cost_estimate=pl.CostEstimate(flops=8 * work, bytes_accessed=moved, transcendentals=0),
        name="listed_keys",
    )(*far_args)
    other_kv = swapped(far_kv)

    blocks = pl.pallas_call(
        functools.partial(combine_kernel, subs),
        in_specs=[SMEM_SPEC] * 2 + [VMEM_SPEC] * 2,
        out_specs=[VMEM_SPEC] * ring,
        out_shape=[jax.ShapeDtypeStruct(span_shape, jnp.float32)]
        + [jax.ShapeDtypeStruct(span_shape, jnp.bfloat16)] * (ring - 1),
        compiler_params=small,
        name="combine",
    )(place, listed, far_kv, other_kv)
    arrived = [shifted(blocks[shift], shift) for shift in range(1, ring)]

    grad_queries = pl.pallas_call(
        functools.partial(query_kernel, factor, rows, subs),
        grid=(kv_heads,),
        in_specs=far_specs + [row_spec],
        out_specs=row_spec,
        out_shape=jax.ShapeDtypeStruct((tokens, heads, head_dim), jnp.float32),
        scratch_shapes=far_scratch,
        compiler_params=params,
        cost_estimate=pl.CostEstimate(flops=6 * work, bytes_accessed=3 * moved, transcendentals=0),
        name="listed_queries",
    )(*far_args, near_query)

    grad_keys, grad_values = pl.pallas_call(
        total_kernel,
        in_specs=[VMEM_SPEC] * (ring + 1),
        out_specs=[VMEM_SPEC] * 2,
        out_shape=[jax.ShapeDtypeStruct((tokens, kv_heads, head_dim), jnp.float32)] * 2,
        compiler_params=small,
        name="total",
    )(near_kv, blocks[0], *arrived)
    return (grad_queries, grad_keys, grad_values)


def solution(mesh):
    return jax.shard_map(
        body,
        mesh=mesh,
        in_specs=(
            P(("groups", "ctx", "sub"), "head", None),
            P(("groups", "ctx", "sub"), "head", None),
            P(("groups", "ctx", "sub"), "head", None),
            P(("groups", "ctx", "sub"), "head", None),
            P(("groups", "ctx", "sub"), "head"),
            P(("groups", "ctx", "sub"), "head"),
            P(("groups", "ctx", "sub")),
            P("groups", None),
        ),
        out_specs=(
            P(("groups", "ctx", "sub"), "head", None),
            P(("groups", "ctx", "sub"), "head", None),
            P(("groups", "ctx", "sub"), "head", None),
        ),
        check_vma=False,
    )
```

```python
import functools

import jax
import jax.numpy as jnp
from jax import lax
from jax.experimental import pallas as pl
from jax.experimental.pallas import tpu as pltpu
from jax.sharding import PartitionSpec as P

QH = 64
KVH = 4
LOG2E = 1.4426950408889634
ROWS = 512
PARTS = 1
VMEM_LIMIT = 24 * 1024 * 1024

VMEM_SPEC = pl.BlockSpec(memory_space=pltpu.VMEM)
SMEM_SPEC = pl.BlockSpec(memory_space=pltpu.SMEM)
ANY_SPEC = pl.BlockSpec(memory_space=pl.ANY)


def rows_dot(left, right):
    return lax.dot_general(left, right, (((1,), (1,)), ((), ())), preferred_element_type=jnp.float32)


def tile_terms(key_blk, value_blk, query_blk, upstream, log_norm, row_terms, allowed, factor):
    scores = rows_dot(key_blk, query_blk)
    probs = jnp.exp2(scores * (factor * LOG2E) - log_norm)
    if allowed is not None:
        probs = jnp.where(allowed, probs, 0.0)
    grad_probs = rows_dot(value_blk, upstream)
    grad_scores = probs * (grad_probs - row_terms)
    return probs.astype(jnp.bfloat16), grad_scores.astype(jnp.bfloat16)


def chunks(query_ref, rows):
    tokens, grouped, head_dim = query_ref.shape
    step = rows // grouped
    return [(i, slice(i * step, (i + 1) * step), slice(i * rows, (i + 1) * rows)) for i in range(tokens // step)]


def pack_kernel(key_ref, value_ref, *kv_refs):
    each = kv_refs[0].shape[1]
    for head in range(key_ref.shape[1]):
        kv_refs[head // each][0, head % each] = key_ref[:, head, :]
        kv_refs[head // each][1, head % each] = value_ref[:, head, :]


def spread_kernel(grouped, norm_ref, term_ref, docs_ref, norm_row_ref, term_row_ref, docs_row_ref, doc_col_ref):
    heads, tokens = norm_ref.shape
    cols = tokens * grouped
    pieces = []
    for value in (norm_ref[...] * LOG2E, term_ref[...]):
        for _ in range(3):
            piece = value.astype(jnp.bfloat16)
            value = value - piece.astype(jnp.float32)
            pieces.append(piece)
    docs = docs_ref[...].astype(jnp.float32)
    pieces.append(jnp.broadcast_to(docs, (grouped, tokens)).astype(jnp.bfloat16))
    column = lax.broadcasted_iota(jnp.int32, (tokens, cols), 1)
    token = lax.broadcasted_iota(jnp.int32, (tokens, cols), 0)
    pick = jnp.where(token == column // grouped, 1.0, 0.0).astype(jnp.bfloat16)
    spread = jnp.dot(jnp.concatenate(pieces, axis=0), pick, preferred_element_type=jnp.float32)
    keep = lax.broadcasted_iota(jnp.int32, (grouped, cols), 0) == (
        lax.broadcasted_iota(jnp.int32, (grouped, cols), 1) % grouped
    )
    for i, out_ref in enumerate((norm_row_ref, term_row_ref)):
        base = 3 * i * heads
        value = spread[base:base + heads] + spread[base + heads:base + 2 * heads]
        value = value + spread[base + 2 * heads:base + 3 * heads]
        for head in range(out_ref.shape[0]):
            group = value[head * grouped:(head + 1) * grouped]
            out_ref[head] = jnp.sum(jnp.where(keep, group, 0.0), axis=0, keepdims=True)
    docs_row_ref[...] = spread[6 * heads:6 * heads + 1]
    doc_col_ref[...] = jnp.broadcast_to(docs, (tokens, tokens)).T


def step_of(span, place_ref, subs, ring, back):
    gap = place_ref[0] - span // subs
    return lax.rem((-gap if back else gap) + ring, ring)


def choose_kernel(subs, place_ref, *refs):
    *column, _, _, out_ref = refs
    ring = len(column)
    for which in range(2):
        shift = step_of(place_ref[4 + which], place_ref, subs, ring, False)
        for step in range(ring):
            @pl.when(shift == step)
            def _():
                out_ref[which] = column[step][...]


def far_blocks(subs, place_ref, column, other_ref, far_ref, first):
    ring = len(column)
    heads = slice(first, first + other_ref.shape[2])
    for which in range(2):
        span = place_ref[2 + which]
        shift = step_of(span, place_ref, subs, ring, False)
        mine = lax.rem(span, subs) == place_ref[1]

        @pl.when(jnp.logical_not(mine))
        def _():
            far_ref[which, :, heads] = other_ref[which]

        for step in range(ring):
            @pl.when(mine & (shift == step))
            def _():
                far_ref[which, :, heads] = column[step][...]


def local_kernel(factor, rows, *refs):
    *kv_refs, query_ref, up_ref, norm_ref, term_ref, docs_ref, doc_col_ref, dkv_ref, dq_ref = refs
    tokens, grouped, head_dim = query_ref.shape
    each = kv_refs[0].shape[1]
    head = pl.program_id(0)
    key_blk, value_blk = kv_refs[0][0, head % each], kv_refs[0][1, head % each]
    for part in range(1, len(kv_refs)):
        key_blk = jnp.where(head // each == part, kv_refs[part][0, head % each], key_blk)
        value_blk = jnp.where(head // each == part, kv_refs[part][1, head % each], value_blk)
    doc_col = jnp.concatenate([doc_col_ref[...]] * (rows // tokens), axis=1)
    grad_key = jnp.zeros((tokens, head_dim), jnp.float32)
    grad_val = jnp.zeros((tokens, head_dim), jnp.float32)
    for i, toks, cols in chunks(query_ref, rows):
        query_blk = query_ref[toks].reshape(rows, head_dim)
        upstream = up_ref[toks].reshape(rows, head_dim)
        position = lax.broadcasted_iota(jnp.int32, (tokens, rows), 1) // grouped + toks.start
        allowed = (lax.broadcasted_iota(jnp.int32, (tokens, rows), 0) <= position) & (doc_col == docs_ref[:, cols])
        probs, grads = tile_terms(
            key_blk, value_blk, query_blk, upstream, norm_ref[0, :, cols], term_ref[0, :, cols], allowed, factor
        )
        grad_val += jnp.dot(probs, upstream, preferred_element_type=jnp.float32)
        grad_key += jnp.dot(grads, query_blk, preferred_element_type=jnp.float32)
        grad_query = lax.dot_general(
            grads, key_blk, (((0,), (0,)), ((), ())), preferred_element_type=jnp.float32
        )
        dq_ref[toks] = (grad_query * factor).reshape(rows // grouped, grouped, head_dim)
    dkv_ref[0, 0] = grad_key * factor
    dkv_ref[1, 0] = grad_val


def listed_kernel(factor, rows, subs, place_ref, *refs):
    (*column, other_ref, query_ref, up_ref, norm_ref, term_ref, dkv_ref, far_ref) = refs
    tokens, grouped, head_dim = query_ref.shape
    head = pl.program_id(0)

    @pl.when(head == 0)
    def _():
        far_blocks(subs, place_ref, column, other_ref, far_ref, 0)

    key_blk = jnp.concatenate([far_ref[0, 0, head], far_ref[1, 0, head]], axis=0)
    value_blk = jnp.concatenate([far_ref[0, 1, head], far_ref[1, 1, head]], axis=0)
    grad_key = jnp.zeros((2 * tokens, head_dim), jnp.float32)
    grad_val = jnp.zeros((2 * tokens, head_dim), jnp.float32)
    for i, toks, cols in chunks(query_ref, rows):
        query_blk = query_ref[toks].reshape(rows, head_dim)
        upstream = up_ref[toks].reshape(rows, head_dim)
        probs, grads = tile_terms(
            key_blk, value_blk, query_blk, upstream, norm_ref[0, :, cols], term_ref[0, :, cols], None, factor
        )
        grad_val += jnp.dot(probs, upstream, preferred_element_type=jnp.float32)
        grad_key += jnp.dot(grads, query_blk, preferred_element_type=jnp.float32)
    grad_key = (grad_key * factor).astype(dkv_ref.dtype)
    grad_val = grad_val.astype(dkv_ref.dtype)
    for which in range(2):
        dkv_ref[which, 0, 0] = grad_key[which * tokens:(which + 1) * tokens]
        dkv_ref[which, 1, 0] = grad_val[which * tokens:(which + 1) * tokens]


def query_kernel(factor, rows, subs, parts, place_ref, *refs):
    (*held, query_ref, up_ref, norm_ref, term_ref, near_ref, _, dq_ref, far_ref) = refs
    tokens, grouped, head_dim = query_ref.shape
    head = pl.program_id(0)

    @pl.when(head == 0)
    def _():
        each = len(held) // parts
        for part in range(parts):
            *column, other_ref = held[part * each:(part + 1) * each]
            far_blocks(subs, place_ref, column, other_ref, far_ref, part * other_ref.shape[2])

    key_blk = jnp.concatenate([far_ref[0, 0, head], far_ref[1, 0, head]], axis=0)
    value_blk = jnp.concatenate([far_ref[0, 1, head], far_ref[1, 1, head]], axis=0)
    for i, toks, cols in chunks(query_ref, rows):
        query_blk = query_ref[toks].reshape(rows, head_dim)
        upstream = up_ref[toks].reshape(rows, head_dim)
        probs, grads = tile_terms(
            key_blk, value_blk, query_blk, upstream, norm_ref[0, :, cols], term_ref[0, :, cols], None, factor
        )
        grad_query = lax.dot_general(
            grads, key_blk, (((0,), (0,)), ((), ())), preferred_element_type=jnp.float32
        )
        dq_ref[toks] = near_ref[toks] + (grad_query * factor).reshape(rows // grouped, grouped, head_dim)


def combine_kernel(subs, place_ref, mine_ref, other_ref, *out_refs):
    ring = len(out_refs)
    sub = place_ref[1]
    parts = []
    for i, ref in enumerate((mine_ref, other_ref)):
        for which in range(2):
            span = place_ref[2 + 2 * i + which]
            shift = step_of(span, place_ref, subs, ring, True)
            parts.append((ref, which, jnp.where(lax.rem(span, subs) == sub, shift, ring)))
    for step, out_ref in enumerate(out_refs):
        total = jnp.zeros(out_ref.shape, jnp.float32)
        for ref, which, shift in parts:
            total += jnp.where(shift == step, ref[which].astype(jnp.float32), 0.0)
        out_ref[...] = total.astype(out_ref.dtype)


def total_kernel(parts, near_ref, *refs):
    *blocks, dk_ref, dv_ref = refs
    count = len(blocks) // parts
    heads = dk_ref.shape[1]
    each = heads // parts
    for kind, out_ref in enumerate((dk_ref, dv_ref)):
        for head in range(heads):
            total = near_ref[kind, head]
            for ref in blocks[head // each * count:(head // each + 1) * count]:
                total += ref[kind, head % each].astype(jnp.float32)
            out_ref[:, head, :] = total


def body(queries, keys, values, grad_out, row_lse, row_delta, doc_ids, pairs):
    tokens, heads, head_dim = queries.shape
    kv_heads = keys.shape[1]
    grouped = QH // KVH
    factor = head_dim ** (-0.5)
    ring = lax.axis_size("ctx")
    subs = lax.axis_size("sub")
    ctx = lax.axis_index("ctx")
    sub = lax.axis_index("sub")
    rows = min(ROWS, tokens * grouped)
    cols = tokens * grouped
    parts = PARTS if kv_heads % PARTS == 0 else 1
    each = kv_heads // parts
    span_shape = (2, each, tokens, head_dim)
    lists = lax.dynamic_slice_in_dim(pairs, ctx * subs, subs, 0)
    place = jnp.concatenate(
        [jnp.stack([ctx, sub]), jnp.where(sub == 0, lists, lists[::-1]).reshape(-1)]
    )

    def shifted(array, shift):
        return lax.ppermute(array, "ctx", [(i, (i + shift) % ring) for i in range(ring)])

    def swapped(array):
        return lax.ppermute(array, "sub", [(i, i ^ 1) for i in range(subs)])

    small = pltpu.CompilerParams(vmem_limit_bytes=VMEM_LIMIT)
    kv = pl.pallas_call(
        pack_kernel,
        in_specs=[VMEM_SPEC] * 2,
        out_specs=[VMEM_SPEC] * parts,
        out_shape=[jax.ShapeDtypeStruct(span_shape, jnp.bfloat16)] * parts,
        compiler_params=small,
        name="pack",
    )(keys, values)
    columns = [[block] + [shifted(block, shift) for shift in range(1, ring)] for block in kv]

    norm, term, docs, doc_col = pl.pallas_call(
        functools.partial(spread_kernel, grouped),
        in_specs=[VMEM_SPEC] * 3,
        out_specs=[VMEM_SPEC] * 4,
        out_shape=[
            jax.ShapeDtypeStruct((kv_heads, 1, cols), jnp.float32),
            jax.ShapeDtypeStruct((kv_heads, 1, cols), jnp.float32),
            jax.ShapeDtypeStruct((1, cols), jnp.float32),
            jax.ShapeDtypeStruct((tokens, tokens), jnp.float32),
        ],
        compiler_params=small,
        name="spread",
    )(row_lse.T, row_delta.T, doc_ids.reshape(1, tokens))

    params = pltpu.CompilerParams(vmem_limit_bytes=VMEM_LIMIT, dimension_semantics=("arbitrary",))
    work = 2 * tokens * tokens * heads * head_dim
    moved = 2 * queries.size * 2

    def query_specs(first):
        row_spec = pl.BlockSpec((tokens, grouped, head_dim), lambda g: (0, first + g, 0))
        lane_spec = pl.BlockSpec((1, 1, cols), lambda g: (first + g, 0, 0))
        return [row_spec, row_spec, lane_spec, lane_spec]

    def whole(shape):
        return pl.BlockSpec(shape, lambda g: (0,) * len(shape))

    row_spec = query_specs(0)[0]
    near_kv, near_query = pl.pallas_call(
        functools.partial(local_kernel, factor, rows),
        grid=(kv_heads,),
        in_specs=[whole(span_shape)] * parts + query_specs(0) + [whole((1, cols)), whole((tokens, tokens))],
        out_specs=[pl.BlockSpec((2, 1, tokens, head_dim), lambda g: (0, g, 0, 0)), row_spec],
        out_shape=[
            jax.ShapeDtypeStruct((2, kv_heads, tokens, head_dim), jnp.float32),
            jax.ShapeDtypeStruct((tokens, heads, head_dim), jnp.float32),
        ],
        compiler_params=params,
        cost_estimate=pl.CostEstimate(flops=5 * work, bytes_accessed=2 * moved, transcendentals=0),
        name="local_block",
    )(*kv, queries, grad_out, norm, term, docs, doc_col)

    held, sums = [], []
    after = near_kv
    for part, column in enumerate(columns):
        chosen = pl.pallas_call(
            functools.partial(choose_kernel, subs),
            in_specs=[SMEM_SPEC] + [VMEM_SPEC] * ring + [ANY_SPEC] * 2,
            out_specs=VMEM_SPEC,
            out_shape=jax.ShapeDtypeStruct((2, *span_shape), jnp.bfloat16),
            compiler_params=small,
            name="choose",
        )(place, *column, near_kv, after)
        other = swapped(chosen)
        held += [*column, other]
        far_kv = pl.pallas_call(
            functools.partial(listed_kernel, factor, rows, subs),
            grid=(each,),
            in_specs=[SMEM_SPEC]
            + [whole(span_shape)] * ring
            + [whole((2, *span_shape))]
            + query_specs(part * each),
            out_specs=pl.BlockSpec((2, 2, 1, tokens, head_dim), lambda g: (0, 0, g, 0, 0)),
            out_shape=jax.ShapeDtypeStruct((2, *span_shape), jnp.bfloat16),
            scratch_shapes=[pltpu.VMEM((2, *span_shape), jnp.bfloat16)],
            compiler_params=params,
            cost_estimate=pl.CostEstimate(flops=8 * work // parts, bytes_accessed=moved // parts, transcendentals=0),
            name="listed_keys",
        )(place, *column, other, queries, grad_out, norm, term)
        other_kv = swapped(far_kv)
        blocks = pl.pallas_call(
            functools.partial(combine_kernel, subs),
            in_specs=[SMEM_SPEC] + [VMEM_SPEC] * 2,
            out_specs=[VMEM_SPEC] * ring,
            out_shape=[jax.ShapeDtypeStruct(span_shape, jnp.float32)]
            + [jax.ShapeDtypeStruct(span_shape, jnp.bfloat16)] * (ring - 1),
            compiler_params=small,
            name="combine",
        )(place, far_kv, other_kv)
        sums += [blocks[0]] + [shifted(blocks[shift], shift) for shift in range(1, ring)]
        after = blocks[0]

    grad_queries = pl.pallas_call(
        functools.partial(query_kernel, factor, rows, subs, parts),
        grid=(kv_heads,),
        in_specs=[SMEM_SPEC]
        + ([whole(span_shape)] * ring + [whole((2, *span_shape))]) * parts
        + query_specs(0)
        + [row_spec, ANY_SPEC],
        out_specs=row_spec,
        out_shape=jax.ShapeDtypeStruct((tokens, heads, head_dim), jnp.float32),
        scratch_shapes=[pltpu.VMEM((2, 2, kv_heads, tokens, head_dim), jnp.bfloat16)],
        compiler_params=params,
        cost_estimate=pl.CostEstimate(flops=6 * work, bytes_accessed=3 * moved, transcendentals=0),
        name="listed_queries",
    )(place, *held, queries, grad_out, norm, term, near_query, after)

    grad_keys, grad_values = pl.pallas_call(
        functools.partial(total_kernel, parts),
        in_specs=[VMEM_SPEC] * (parts * ring + 1),
        out_specs=[VMEM_SPEC] * 2,
        out_shape=[jax.ShapeDtypeStruct((tokens, kv_heads, head_dim), jnp.float32)] * 2,
        compiler_params=small,
        name="total",
    )(near_kv, *sums)
    return (grad_queries, grad_keys, grad_values)


def solution(mesh):
    return jax.shard_map(
        body,
        mesh=mesh,
        in_specs=(
            P(("groups", "ctx", "sub"), "head", None),
            P(("groups", "ctx", "sub"), "head", None),
            P(("groups", "ctx", "sub"), "head", None),
            P(("groups", "ctx", "sub"), "head", None),
            P(("groups", "ctx", "sub"), "head"),
            P(("groups", "ctx", "sub"), "head"),
            P(("groups", "ctx", "sub")),
            P("groups", None),
        ),
        out_specs=(
            P(("groups", "ctx", "sub"), "head", None),
            P(("groups", "ctx", "sub"), "head", None),
            P(("groups", "ctx", "sub"), "head", None),
        ),
        check_vma=False,
    )
```

```python
import functools

import jax
import jax.numpy as jnp
from jax import lax
from jax.experimental import pallas as pl
from jax.experimental.pallas import tpu as pltpu
from jax.sharding import PartitionSpec as P

QH = 64
KVH = 4
LOG2E = 1.4426950408889634
ROWS = 512
PARTS = 1
VMEM_LIMIT = 24 * 1024 * 1024

VMEM_SPEC = pl.BlockSpec(memory_space=pltpu.VMEM)
ANY_SPEC = pl.BlockSpec(memory_space=pl.ANY)
HBM_SPEC = pl.BlockSpec(memory_space=pltpu.HBM)


def rows_dot(left, right):
    return lax.dot_general(left, right, (((1,), (1,)), ((), ())), preferred_element_type=jnp.float32)


def tile_terms(key_blk, value_blk, query_blk, upstream, log_norm, row_terms, allowed, factor):
    scores = rows_dot(key_blk, query_blk)
    probs = jnp.exp2(scores * (factor * LOG2E) - log_norm)
    if allowed is not None:
        probs = jnp.where(allowed, probs, 0.0)
    grad_probs = rows_dot(value_blk, upstream)
    grad_scores = probs * (grad_probs - row_terms)
    return probs.astype(jnp.bfloat16), grad_scores.astype(jnp.bfloat16)


def chunks(tokens, grouped, rows):
    step = rows // grouped
    return [(i, slice(i * step, (i + 1) * step), slice(i * rows, (i + 1) * rows)) for i in range(tokens // step)]


def start_all(sources, targets, sems):
    copies = [pltpu.make_async_copy(source, target, sems.at[i]) for i, (source, target) in enumerate(zip(sources, targets))]
    for copy in copies:
        copy.start()
    return copies


class Rows:
    def __init__(self, query_ref, up_ref, held_ref, sems, first, rows):
        _, self.count, tokens, self.grouped, self.head_dim = held_ref.shape
        self.held, self.rows = held_ref, rows
        self.steps = chunks(tokens, self.grouped, rows)
        self.copies = {}
        for head in range(self.count):
            heads = slice((first + head) * self.grouped, (first + head + 1) * self.grouped)
            for i, toks, _ in self.steps:
                for kind, ref in enumerate((query_ref, up_ref)):
                    copy = pltpu.make_async_copy(
                        ref.at[toks, heads], held_ref.at[kind, head, toks], sems.at[head, i, kind]
                    )
                    copy.start()
                    self.copies[head, i, kind] = copy

    def blocks(self, head):
        for i, toks, cols in self.steps:
            pair = []
            for kind in range(2):
                self.copies[head, i, kind].wait()
                pair.append(self.held[kind, head, toks].reshape(self.rows, self.head_dim))
            yield toks, cols, *pair


def pack_kernel(key_ref, value_ref, *refs):
    *kv_refs, held_ref, sems = refs
    each = kv_refs[0].shape[1]
    copies = start_all((key_ref, value_ref), (held_ref.at[0], held_ref.at[1]), sems)
    for kind, copy in enumerate(copies):
        copy.wait()
        for head in range(held_ref.shape[2]):
            kv_refs[head // each][kind, head % each] = held_ref[kind, :, head, :]


def spread_kernel(
    grouped, ring, subs, norm_ref, term_ref, docs_ref, pairs_ref,
    norm_row_ref, term_row_ref, docs_row_ref, doc_col_ref, places_ref,
    held_ref, held_docs, held_pairs, sems,
):
    _, heads, tokens = held_ref.shape
    copies = start_all(
        (pairs_ref, docs_ref, norm_ref, term_ref), (held_pairs, held_docs, held_ref.at[0], held_ref.at[1]), sems
    )
    cols = tokens * grouped
    column = lax.broadcasted_iota(jnp.int32, (tokens, cols), 1)
    token = lax.broadcasted_iota(jnp.int32, (tokens, cols), 0)
    pick = jnp.where(token == column // grouped, 1.0, 0.0).astype(jnp.bfloat16)
    keep = lax.broadcasted_iota(jnp.int32, (grouped, cols), 0) == (
        lax.broadcasted_iota(jnp.int32, (grouped, cols), 1) % grouped
    )
    for copy in copies:
        copy.wait()

    ctx, sub = lax.axis_index("ctx"), lax.axis_index("sub")
    pairs = held_pairs[...]
    lane = lax.broadcasted_iota(jnp.int32, pairs.shape, 1)

    def listed_by(core):
        mask = lane == ctx * subs + core
        span = jnp.sum(jnp.where(mask, pairs, 0).astype(jnp.float32), axis=1, keepdims=True)
        span = jnp.broadcast_to(span, (2, places_ref.shape[1])).astype(jnp.int32)
        return span // subs, span % subs

    def around(gap):
        return jnp.where(gap < 0, gap + ring, gap)

    (mine, mine_sub), (other, other_sub) = listed_by(sub), listed_by(1 - sub)
    places_ref[0:2] = around(ctx - other)
    places_ref[2:4] = jnp.where(mine_sub == sub, around(ctx - mine), ring)
    places_ref[4:6] = jnp.where(mine_sub == sub, around(mine - ctx), ring)
    places_ref[6:8] = jnp.where(other_sub == sub, around(other - ctx), ring)

    pieces = []
    for value in (held_ref[0] * LOG2E, held_ref[1]):
        for _ in range(3):
            piece = value.astype(jnp.bfloat16)
            value = value - piece.astype(jnp.float32)
            pieces.append(piece)
    docs = held_docs[...].astype(jnp.float32)
    pieces.append(jnp.broadcast_to(docs, (grouped, tokens)).astype(jnp.bfloat16))
    spread = jnp.dot(jnp.concatenate(pieces, axis=0), pick, preferred_element_type=jnp.float32)
    for i, out_ref in enumerate((norm_row_ref, term_row_ref)):
        base = 3 * i * heads
        value = spread[base:base + heads] + spread[base + heads:base + 2 * heads]
        value = value + spread[base + 2 * heads:base + 3 * heads]
        for head in range(out_ref.shape[0]):
            group = value[head * grouped:(head + 1) * grouped]
            out_ref[head] = jnp.sum(jnp.where(keep, group, 0.0), axis=0, keepdims=True)
    docs_row_ref[...] = spread[6 * heads:6 * heads + 1]
    doc_col_ref[...] = jnp.broadcast_to(docs, (tokens, tokens)).T


def pick_block(sources, row):
    chosen = sources[0].astype(jnp.float32)
    for step in range(1, len(sources)):
        chosen = jnp.where(row == step, sources[step].astype(jnp.float32), chosen)
    return chosen.astype(jnp.bfloat16)


def choose_kernel(places_ref, *refs):
    *column, _, _, out_ref = refs
    for which in range(2):
        row = places_ref[which:which + 1]
        for kind in range(2):
            for head in range(out_ref.shape[2]):
                out_ref[which, kind, head] = pick_block([ref[kind, head] for ref in column], row)


def far_blocks(places_ref, column, other_ref, head):
    return [
        jnp.concatenate(
            [
                pick_block(
                    [ref[kind, head] for ref in column] + [other_ref[which, kind, head]],
                    places_ref[2 + which:3 + which],
                )
                for which in range(2)
            ],
            axis=0,
        )
        for kind in range(2)
    ]


def local_kernel(factor, rows, *refs):
    *kv_refs, query_ref, up_ref, norm_ref, term_ref, docs_ref, doc_col_ref, dkv_ref, dq_ref, held_ref, sems = refs
    source = Rows(query_ref, up_ref, held_ref, sems, 0, rows)
    tokens, grouped, head_dim = held_ref.shape[2:]
    each = kv_refs[0].shape[1]
    doc_col = jnp.concatenate([doc_col_ref[...]] * (rows // tokens), axis=1)
    for head in range(source.count):
        key_blk, value_blk = kv_refs[head // each][0, head % each], kv_refs[head // each][1, head % each]
        grad_key = jnp.zeros((tokens, head_dim), jnp.float32)
        grad_val = jnp.zeros((tokens, head_dim), jnp.float32)
        for toks, cols, query_blk, upstream in source.blocks(head):
            position = lax.broadcasted_iota(jnp.int32, (tokens, rows), 1) // grouped + toks.start
            allowed = (lax.broadcasted_iota(jnp.int32, (tokens, rows), 0) <= position) & (
                doc_col == docs_ref[:, cols]
            )
            probs, grads = tile_terms(
                key_blk, value_blk, query_blk, upstream, norm_ref[head, :, cols], term_ref[head, :, cols],
                allowed, factor,
            )
            grad_val += jnp.dot(probs, upstream, preferred_element_type=jnp.float32)
            grad_key += jnp.dot(grads, query_blk, preferred_element_type=jnp.float32)
            grad_query = lax.dot_general(
                grads, key_blk, (((0,), (0,)), ((), ())), preferred_element_type=jnp.float32
            )
            dq_ref[toks, head * grouped:(head + 1) * grouped] = (grad_query * factor).reshape(
                rows // grouped, grouped, head_dim
            )
        dkv_ref[0, head] = grad_key * factor
        dkv_ref[1, head] = grad_val


def listed_kernel(factor, rows, first, places_ref, *refs):
    *column, other_ref, query_ref, up_ref, norm_ref, term_ref, dkv_ref, held_ref, sems = refs
    source = Rows(query_ref, up_ref, held_ref, sems, first, rows)
    tokens, grouped, head_dim = held_ref.shape[2:]
    for head in range(source.count):
        key_blk, value_blk = far_blocks(places_ref, column, other_ref, head)
        grad_key = jnp.zeros((2 * tokens, head_dim), jnp.float32)
        grad_val = jnp.zeros((2 * tokens, head_dim), jnp.float32)
        for toks, cols, query_blk, upstream in source.blocks(head):
            probs, grads = tile_terms(
                key_blk, value_blk, query_blk, upstream,
                norm_ref[first + head, :, cols], term_ref[first + head, :, cols], None, factor,
            )
            grad_val += jnp.dot(probs, upstream, preferred_element_type=jnp.float32)
            grad_key += jnp.dot(grads, query_blk, preferred_element_type=jnp.float32)
        grad_key = (grad_key * factor).astype(dkv_ref.dtype)
        grad_val = grad_val.astype(dkv_ref.dtype)
        for which in range(2):
            dkv_ref[which, 0, head] = grad_key[which * tokens:(which + 1) * tokens]
            dkv_ref[which, 1, head] = grad_val[which * tokens:(which + 1) * tokens]


def query_kernel(factor, rows, parts, places_ref, *refs):
    *inputs, query_ref, up_ref, norm_ref, term_ref, near_ref, _, dq_ref, held_ref, sems = refs
    source = Rows(query_ref, up_ref, held_ref, sems, 0, rows)
    tokens, grouped, head_dim = held_ref.shape[2:]
    size = len(inputs) // parts
    each = source.count // parts
    for head in range(source.count):
        *column, other_ref = inputs[head // each * size:(head // each + 1) * size]
        key_blk, value_blk = far_blocks(places_ref, column, other_ref, head % each)
        for toks, cols, query_blk, upstream in source.blocks(head):
            _, grads = tile_terms(
                key_blk, value_blk, query_blk, upstream, norm_ref[head, :, cols], term_ref[head, :, cols],
                None, factor,
            )
            grad_query = lax.dot_general(
                grads, key_blk, (((0,), (0,)), ((), ())), preferred_element_type=jnp.float32
            )
            heads = slice(head * grouped, (head + 1) * grouped)
            dq_ref[toks, heads] = near_ref[toks, heads] + (grad_query * factor).reshape(
                rows // grouped, grouped, head_dim
            )


def combine_kernel(places_ref, mine_ref, other_ref, *out_refs):
    for step, out_ref in enumerate(out_refs):
        for kind in range(2):
            for head in range(out_ref.shape[1]):
                total = None
                for i, ref in enumerate((mine_ref, other_ref)):
                    for which in range(2):
                        row = places_ref[4 + 2 * i + which:5 + 2 * i + which]
                        term = jnp.where(row == step, ref[which, kind, head].astype(jnp.float32), 0.0)
                        total = term if total is None else total + term
                out_ref[kind, head] = total.astype(out_ref.dtype)


def total_kernel(parts, near_ref, *refs):
    *blocks, dk_ref, dv_ref = refs
    count = len(blocks) // parts
    heads = dk_ref.shape[1]
    each = heads // parts
    for kind, out_ref in enumerate((dk_ref, dv_ref)):
        for head in range(heads):
            total = near_ref[kind, head]
            for ref in blocks[head // each * count:(head // each + 1) * count]:
                total += ref[kind, head % each].astype(jnp.float32)
            out_ref[:, head, :] = total


def body(queries, keys, values, grad_out, row_lse, row_delta, doc_ids, pairs):
    tokens, heads, head_dim = queries.shape
    kv_heads = keys.shape[1]
    grouped = QH // KVH
    factor = head_dim ** (-0.5)
    ring = lax.axis_size("ctx")
    subs = lax.axis_size("sub")
    rows = min(ROWS, tokens * grouped)
    cols = tokens * grouped
    parts = PARTS if kv_heads % PARTS == 0 else 1
    each = kv_heads // parts
    span_shape = (2, each, tokens, head_dim)

    def shifted(array, shift):
        return lax.ppermute(array, "ctx", [(i, (i + shift) % ring) for i in range(ring)])

    def swapped(array):
        return lax.ppermute(array, "sub", [(i, i ^ 1) for i in range(subs)])

    def in_hbm(*arrays):
        return [pltpu.with_memory_space_constraint(array, pltpu.HBM) for array in arrays]

    params = pltpu.CompilerParams(vmem_limit_bytes=VMEM_LIMIT)
    kv = pl.pallas_call(
        pack_kernel,
        in_specs=[HBM_SPEC] * 2,
        out_specs=[VMEM_SPEC] * parts,
        out_shape=[jax.ShapeDtypeStruct(span_shape, jnp.bfloat16)] * parts,
        scratch_shapes=[pltpu.VMEM((2, *keys.shape), jnp.bfloat16), pltpu.SemaphoreType.DMA((2,))],
        compiler_params=params,
        name="pack",
    )(*in_hbm(keys, values))
    columns = [[block] + [shifted(block, shift) for shift in range(1, ring)] for block in kv]

    norm, term, docs, doc_col, places = pl.pallas_call(
        functools.partial(spread_kernel, grouped, ring, subs),
        in_specs=[HBM_SPEC] * 4,
        out_specs=[VMEM_SPEC] * 5,
        out_shape=[
            jax.ShapeDtypeStruct((kv_heads, 1, cols), jnp.float32),
            jax.ShapeDtypeStruct((kv_heads, 1, cols), jnp.float32),
            jax.ShapeDtypeStruct((1, cols), jnp.float32),
            jax.ShapeDtypeStruct((tokens, tokens), jnp.float32),
            jax.ShapeDtypeStruct((8, head_dim), jnp.int32),
        ],
        scratch_shapes=[
            pltpu.VMEM((2, heads, tokens), jnp.float32),
            pltpu.VMEM((1, tokens), jnp.int32),
            pltpu.VMEM(pairs.shape[::-1], jnp.int32),
            pltpu.SemaphoreType.DMA((4,)),
        ],
        compiler_params=params,
        name="spread",
    )(*in_hbm(row_lse.T, row_delta.T, doc_ids.reshape(1, tokens), pairs.T))

    work = 2 * tokens * tokens * heads * head_dim
    moved = 2 * queries.size * 2

    def row_scratch(count):
        return [
            pltpu.VMEM((2, count, tokens, grouped, head_dim), jnp.bfloat16),
            pltpu.SemaphoreType.DMA((count, cols // rows, 2)),
        ]

    row_specs = [HBM_SPEC] * 2 + [VMEM_SPEC] * 2
    near_kv, near_query = pl.pallas_call(
        functools.partial(local_kernel, factor, rows),
        in_specs=[VMEM_SPEC] * parts + row_specs + [VMEM_SPEC] * 2,
        out_specs=[VMEM_SPEC] * 2,
        out_shape=[
            jax.ShapeDtypeStruct((2, kv_heads, tokens, head_dim), jnp.float32),
            jax.ShapeDtypeStruct((tokens, heads, head_dim), jnp.float32),
        ],
        scratch_shapes=row_scratch(kv_heads),
        compiler_params=params,
        cost_estimate=pl.CostEstimate(flops=5 * work, bytes_accessed=2 * moved, transcendentals=0),
        name="local_block",
    )(*kv, *in_hbm(queries, grad_out), norm, term, docs, doc_col)

    inputs, sums = [], []
    after = near_kv
    for part, column in enumerate(columns):
        chosen = pl.pallas_call(
            choose_kernel,
            in_specs=[VMEM_SPEC] * (ring + 1) + [ANY_SPEC] * 2,
            out_specs=VMEM_SPEC,
            out_shape=jax.ShapeDtypeStruct((2, *span_shape), jnp.bfloat16),
            compiler_params=params,
            name="choose",
        )(places, *column, near_kv, after)
        other = swapped(chosen)
        inputs += [*column, other]
        far_kv = pl.pallas_call(
            functools.partial(listed_kernel, factor, rows, part * each),
            in_specs=[VMEM_SPEC] * (ring + 2) + row_specs,
            out_specs=VMEM_SPEC,
            out_shape=jax.ShapeDtypeStruct((2, *span_shape), jnp.bfloat16),
            scratch_shapes=row_scratch(each),
            compiler_params=params,
            cost_estimate=pl.CostEstimate(flops=8 * work // parts, bytes_accessed=moved // parts, transcendentals=0),
            name="listed_keys",
        )(places, *column, other, *in_hbm(queries, grad_out), norm, term)
        other_kv = swapped(far_kv)
        blocks = pl.pallas_call(
            combine_kernel,
            in_specs=[VMEM_SPEC] * 3,
            out_specs=[VMEM_SPEC] * ring,
            out_shape=[jax.ShapeDtypeStruct(span_shape, jnp.float32)]
            + [jax.ShapeDtypeStruct(span_shape, jnp.bfloat16)] * (ring - 1),
            compiler_params=params,
            name="combine",
        )(places, far_kv, other_kv)
        sums += [blocks[0]] + [shifted(blocks[shift], shift) for shift in range(1, ring)]
        after = blocks[0]

    grad_queries = pl.pallas_call(
        functools.partial(query_kernel, factor, rows, parts),
        in_specs=[VMEM_SPEC] * (1 + len(inputs)) + row_specs + [VMEM_SPEC, ANY_SPEC],
        out_specs=VMEM_SPEC,
        out_shape=jax.ShapeDtypeStruct((tokens, heads, head_dim), jnp.float32),
        scratch_shapes=row_scratch(kv_heads),
        compiler_params=params,
        cost_estimate=pl.CostEstimate(flops=6 * work, bytes_accessed=3 * moved, transcendentals=0),
        name="listed_queries",
    )(places, *inputs, *in_hbm(queries, grad_out), norm, term, near_query, after)

    grad_keys, grad_values = pl.pallas_call(
        functools.partial(total_kernel, parts),
        in_specs=[VMEM_SPEC] * (parts * ring + 1),
        out_specs=[VMEM_SPEC] * 2,
        out_shape=[jax.ShapeDtypeStruct((tokens, kv_heads, head_dim), jnp.float32)] * 2,
        compiler_params=params,
        name="total",
    )(near_kv, *sums)
    return (grad_queries, grad_keys, grad_values)


def solution(mesh):
    return jax.shard_map(
        body,
        mesh=mesh,
        in_specs=(
            P(("groups", "ctx", "sub"), "head", None),
            P(("groups", "ctx", "sub"), "head", None),
            P(("groups", "ctx", "sub"), "head", None),
            P(("groups", "ctx", "sub"), "head", None),
            P(("groups", "ctx", "sub"), "head"),
            P(("groups", "ctx", "sub"), "head"),
            P(("groups", "ctx", "sub")),
            P("groups", None),
        ),
        out_specs=(
            P(("groups", "ctx", "sub"), "head", None),
            P(("groups", "ctx", "sub"), "head", None),
            P(("groups", "ctx", "sub"), "head", None),
        ),
        check_vma=False,
    )
```

```python
import functools

import jax
import jax.numpy as jnp
from jax import lax
from jax.experimental import pallas as pl
from jax.experimental.pallas import tpu as pltpu
from jax.sharding import PartitionSpec as P

QH = 64
KVH = 4
LOG2E = 1.4426950408889634
ROWS = 512
PARTS = 1
VMEM_LIMIT = 24 * 1024 * 1024

VMEM_SPEC = pl.BlockSpec(memory_space=pltpu.VMEM)
ANY_SPEC = pl.BlockSpec(memory_space=pl.ANY)
HBM_SPEC = pl.BlockSpec(memory_space=pltpu.HBM)


def rows_dot(left, right):
    return lax.dot_general(left, right, (((1,), (1,)), ((), ())), preferred_element_type=jnp.float32)


def tile_terms(key_blk, value_blk, query_blk, upstream, log_norm, row_terms, allowed, factor):
    scores = rows_dot(key_blk, query_blk)
    probs = jnp.exp2(scores * (factor * LOG2E) - log_norm)
    if allowed is not None:
        probs = jnp.where(allowed, probs, 0.0)
    grad_probs = rows_dot(value_blk, upstream)
    grad_scores = probs * (grad_probs - row_terms)
    return probs.astype(jnp.bfloat16), grad_scores.astype(jnp.bfloat16)


def chunks(tokens, grouped, rows):
    step = rows // grouped
    return [(i, slice(i * step, (i + 1) * step), slice(i * rows, (i + 1) * rows)) for i in range(tokens // step)]


def start_all(sources, targets, sems):
    copies = [pltpu.make_async_copy(source, target, sems.at[i]) for i, (source, target) in enumerate(zip(sources, targets))]
    for copy in copies:
        copy.start()
    return copies


def bring_rows(query_ref, up_ref, held_ref, sems, rows):
    _, count, tokens, grouped, _ = held_ref.shape
    copies = {}
    for head in range(count):
        heads = slice(head * grouped, (head + 1) * grouped)
        for i, toks, _ in chunks(tokens, grouped, rows):
            copies[head, i] = [
                pltpu.make_async_copy(ref.at[toks, heads], held_ref.at[kind, head, toks], sems.at[head, i, kind])
                for kind, ref in enumerate((query_ref, up_ref))
            ]
            for copy in copies[head, i]:
                copy.start()
    return copies


def row_blocks(held_ref, head, rows, copies=None):
    _, _, tokens, grouped, head_dim = held_ref.shape
    for i, toks, cols in chunks(tokens, grouped, rows):
        for copy in copies[head, i] if copies else ():
            copy.wait()
        yield toks, cols, *(held_ref[kind, head, toks].reshape(rows, head_dim) for kind in range(2))


def pack_kernel(key_ref, value_ref, *refs):
    *kv_refs, held_ref, sems = refs
    each = kv_refs[0].shape[1]
    copies = start_all((key_ref, value_ref), (held_ref.at[0], held_ref.at[1]), sems)
    for kind, copy in enumerate(copies):
        copy.wait()
        for head in range(held_ref.shape[2]):
            kv_refs[head // each][kind, head % each] = held_ref[kind, :, head, :]


def spread_kernel(
    grouped, ring, subs, norm_ref, term_ref, docs_ref, pairs_ref,
    norm_row_ref, term_row_ref, docs_row_ref, doc_col_ref, places_ref,
    held_ref, held_docs, held_pairs, sems,
):
    _, heads, tokens = held_ref.shape
    copies = start_all(
        (pairs_ref, docs_ref, norm_ref, term_ref), (held_pairs, held_docs, held_ref.at[0], held_ref.at[1]), sems
    )
    cols = tokens * grouped
    column = lax.broadcasted_iota(jnp.int32, (tokens, cols), 1)
    token = lax.broadcasted_iota(jnp.int32, (tokens, cols), 0)
    pick = jnp.where(token == column // grouped, 1.0, 0.0).astype(jnp.bfloat16)
    keep = lax.broadcasted_iota(jnp.int32, (grouped, cols), 0) == (
        lax.broadcasted_iota(jnp.int32, (grouped, cols), 1) % grouped
    )
    for copy in copies:
        copy.wait()

    ctx, sub = lax.axis_index("ctx"), lax.axis_index("sub")
    pairs = held_pairs[...]
    lane = lax.broadcasted_iota(jnp.int32, pairs.shape, 1)

    def listed_by(core):
        mask = lane == ctx * subs + core
        span = jnp.sum(jnp.where(mask, pairs, 0).astype(jnp.float32), axis=1, keepdims=True)
        span = jnp.broadcast_to(span, (2, places_ref.shape[1])).astype(jnp.int32)
        return span // subs, span % subs

    def around(gap):
        return jnp.where(gap < 0, gap + ring, gap)

    (mine, mine_sub), (other, other_sub) = listed_by(sub), listed_by(1 - sub)
    places_ref[0:2] = around(ctx - other)
    places_ref[2:4] = jnp.where(mine_sub == sub, around(ctx - mine), ring)
    places_ref[4:6] = jnp.where(mine_sub == sub, around(mine - ctx), ring)
    places_ref[6:8] = jnp.where(other_sub == sub, around(other - ctx), ring)

    pieces = []
    for value in (held_ref[0] * LOG2E, held_ref[1]):
        for _ in range(3):
            piece = value.astype(jnp.bfloat16)
            value = value - piece.astype(jnp.float32)
            pieces.append(piece)
    docs = held_docs[...].astype(jnp.float32)
    pieces.append(jnp.broadcast_to(docs, (grouped, tokens)).astype(jnp.bfloat16))
    spread = jnp.dot(jnp.concatenate(pieces, axis=0), pick, preferred_element_type=jnp.float32)
    for i, out_ref in enumerate((norm_row_ref, term_row_ref)):
        base = 3 * i * heads
        value = spread[base:base + heads] + spread[base + heads:base + 2 * heads]
        value = value + spread[base + 2 * heads:base + 3 * heads]
        for head in range(out_ref.shape[0]):
            group = value[head * grouped:(head + 1) * grouped]
            out_ref[head] = jnp.sum(jnp.where(keep, group, 0.0), axis=0, keepdims=True)
    docs_row_ref[...] = spread[6 * heads:6 * heads + 1]
    doc_col_ref[...] = jnp.broadcast_to(docs, (tokens, tokens)).T


def pick_block(sources, row):
    chosen = sources[0].astype(jnp.float32)
    for step in range(1, len(sources)):
        chosen = jnp.where(row == step, sources[step].astype(jnp.float32), chosen)
    return chosen.astype(jnp.bfloat16)


def choose_kernel(places_ref, *refs):
    *column, _, _, out_ref = refs
    for which in range(2):
        row = places_ref[which:which + 1]
        for kind in range(2):
            for head in range(out_ref.shape[2]):
                out_ref[which, kind, head] = pick_block([ref[kind, head] for ref in column], row)


def far_blocks(places_ref, column, other_ref, head):
    return [
        jnp.concatenate(
            [
                pick_block(
                    [ref[kind, head] for ref in column] + [other_ref[which, kind, head]],
                    places_ref[2 + which:3 + which],
                )
                for which in range(2)
            ],
            axis=0,
        )
        for kind in range(2)
    ]


def local_kernel(factor, rows, *refs):
    *kv_refs, query_ref, up_ref, norm_ref, term_ref, docs_ref, doc_col_ref, dkv_ref, dq_ref, held_ref, sems = refs
    copies = bring_rows(query_ref, up_ref, held_ref, sems, rows)
    tokens, grouped, head_dim = held_ref.shape[2:]
    each = kv_refs[0].shape[1]
    doc_col = jnp.concatenate([doc_col_ref[...]] * (rows // tokens), axis=1)
    for head in range(held_ref.shape[1]):
        key_blk, value_blk = kv_refs[head // each][0, head % each], kv_refs[head // each][1, head % each]
        grad_key = jnp.zeros((tokens, head_dim), jnp.float32)
        grad_val = jnp.zeros((tokens, head_dim), jnp.float32)
        for toks, cols, query_blk, upstream in row_blocks(held_ref, head, rows, copies):
            position = lax.broadcasted_iota(jnp.int32, (tokens, rows), 1) // grouped + toks.start
            allowed = (lax.broadcasted_iota(jnp.int32, (tokens, rows), 0) <= position) & (
                doc_col == docs_ref[:, cols]
            )
            probs, grads = tile_terms(
                key_blk, value_blk, query_blk, upstream, norm_ref[head, :, cols], term_ref[head, :, cols],
                allowed, factor,
            )
            grad_val += jnp.dot(probs, upstream, preferred_element_type=jnp.float32)
            grad_key += jnp.dot(grads, query_blk, preferred_element_type=jnp.float32)
            grad_query = lax.dot_general(
                grads, key_blk, (((0,), (0,)), ((), ())), preferred_element_type=jnp.float32
            )
            dq_ref[toks, head * grouped:(head + 1) * grouped] = (grad_query * factor).reshape(
                rows // grouped, grouped, head_dim
            )
        dkv_ref[0, head] = grad_key * factor
        dkv_ref[1, head] = grad_val


def listed_kernel(factor, rows, first, places_ref, *refs):
    *column, other_ref, held_ref, norm_ref, term_ref, dkv_ref = refs
    tokens, grouped, head_dim = held_ref.shape[2:]
    for head in range(other_ref.shape[2]):
        key_blk, value_blk = far_blocks(places_ref, column, other_ref, head)
        grad_key = jnp.zeros((2 * tokens, head_dim), jnp.float32)
        grad_val = jnp.zeros((2 * tokens, head_dim), jnp.float32)
        for toks, cols, query_blk, upstream in row_blocks(held_ref, first + head, rows):
            probs, grads = tile_terms(
                key_blk, value_blk, query_blk, upstream,
                norm_ref[first + head, :, cols], term_ref[first + head, :, cols], None, factor,
            )
            grad_val += jnp.dot(probs, upstream, preferred_element_type=jnp.float32)
            grad_key += jnp.dot(grads, query_blk, preferred_element_type=jnp.float32)
        grad_key = (grad_key * factor).astype(dkv_ref.dtype)
        grad_val = grad_val.astype(dkv_ref.dtype)
        for which in range(2):
            dkv_ref[which, 0, head] = grad_key[which * tokens:(which + 1) * tokens]
            dkv_ref[which, 1, head] = grad_val[which * tokens:(which + 1) * tokens]


def query_kernel(factor, rows, parts, places_ref, *refs):
    *inputs, held_ref, norm_ref, term_ref, near_ref, _, dq_ref = refs
    tokens, grouped, head_dim = held_ref.shape[2:]
    size = len(inputs) // parts
    each = held_ref.shape[1] // parts
    for head in range(held_ref.shape[1]):
        *column, other_ref = inputs[head // each * size:(head // each + 1) * size]
        key_blk, value_blk = far_blocks(places_ref, column, other_ref, head % each)
        for toks, cols, query_blk, upstream in row_blocks(held_ref, head, rows):
            _, grads = tile_terms(
                key_blk, value_blk, query_blk, upstream, norm_ref[head, :, cols], term_ref[head, :, cols],
                None, factor,
            )
            grad_query = lax.dot_general(
                grads, key_blk, (((0,), (0,)), ((), ())), preferred_element_type=jnp.float32
            )
            heads = slice(head * grouped, (head + 1) * grouped)
            dq_ref[toks, heads] = near_ref[toks, heads] + (grad_query * factor).reshape(
                rows // grouped, grouped, head_dim
            )


def combine_kernel(places_ref, mine_ref, other_ref, *out_refs):
    for step, out_ref in enumerate(out_refs):
        for kind in range(2):
            for head in range(out_ref.shape[1]):
                total = None
                for i, ref in enumerate((mine_ref, other_ref)):
                    for which in range(2):
                        row = places_ref[4 + 2 * i + which:5 + 2 * i + which]
                        term = jnp.where(row == step, ref[which, kind, head].astype(jnp.float32), 0.0)
                        total = term if total is None else total + term
                out_ref[kind, head] = total.astype(out_ref.dtype)


def total_kernel(parts, near_ref, *refs):
    *blocks, dk_ref, dv_ref = refs
    count = len(blocks) // parts
    heads = dk_ref.shape[1]
    each = heads // parts
    for kind, out_ref in enumerate((dk_ref, dv_ref)):
        for head in range(heads):
            total = near_ref[kind, head]
            for ref in blocks[head // each * count:(head // each + 1) * count]:
                total += ref[kind, head % each].astype(jnp.float32)
            out_ref[:, head, :] = total


def body(queries, keys, values, grad_out, row_lse, row_delta, doc_ids, pairs):
    tokens, heads, head_dim = queries.shape
    kv_heads = keys.shape[1]
    grouped = QH // KVH
    factor = head_dim ** (-0.5)
    ring = lax.axis_size("ctx")
    subs = lax.axis_size("sub")
    rows = min(ROWS, tokens * grouped)
    cols = tokens * grouped
    parts = PARTS if kv_heads % PARTS == 0 else 1
    each = kv_heads // parts
    span_shape = (2, each, tokens, head_dim)

    def shifted(array, shift):
        return lax.ppermute(array, "ctx", [(i, (i + shift) % ring) for i in range(ring)])

    def swapped(array):
        return lax.ppermute(array, "sub", [(i, i ^ 1) for i in range(subs)])

    def in_hbm(*arrays):
        return [pltpu.with_memory_space_constraint(array, pltpu.HBM) for array in arrays]

    params = pltpu.CompilerParams(vmem_limit_bytes=VMEM_LIMIT)
    kv = pl.pallas_call(
        pack_kernel,
        in_specs=[HBM_SPEC] * 2,
        out_specs=[VMEM_SPEC] * parts,
        out_shape=[jax.ShapeDtypeStruct(span_shape, jnp.bfloat16)] * parts,
        scratch_shapes=[pltpu.VMEM((2, *keys.shape), jnp.bfloat16), pltpu.SemaphoreType.DMA((2,))],
        compiler_params=params,
        name="pack",
    )(*in_hbm(keys, values))
    columns = [[block] + [shifted(block, shift) for shift in range(1, ring)] for block in kv]

    norm, term, docs, doc_col, places = pl.pallas_call(
        functools.partial(spread_kernel, grouped, ring, subs),
        in_specs=[HBM_SPEC] * 4,
        out_specs=[VMEM_SPEC] * 5,
        out_shape=[
            jax.ShapeDtypeStruct((kv_heads, 1, cols), jnp.float32),
            jax.ShapeDtypeStruct((kv_heads, 1, cols), jnp.float32),
            jax.ShapeDtypeStruct((1, cols), jnp.float32),
            jax.ShapeDtypeStruct((tokens, tokens), jnp.float32),
            jax.ShapeDtypeStruct((8, head_dim), jnp.int32),
        ],
        scratch_shapes=[
            pltpu.VMEM((2, heads, tokens), jnp.float32),
            pltpu.VMEM((1, tokens), jnp.int32),
            pltpu.VMEM(pairs.shape[::-1], jnp.int32),
            pltpu.SemaphoreType.DMA((4,)),
        ],
        compiler_params=params,
        name="spread",
    )(*in_hbm(row_lse.T, row_delta.T, doc_ids.reshape(1, tokens), pairs.T))

    work = 2 * tokens * tokens * heads * head_dim
    moved = 2 * queries.size * 2

    row_specs = [VMEM_SPEC] * 3
    near_kv, near_query, held = pl.pallas_call(
        functools.partial(local_kernel, factor, rows),
        in_specs=[VMEM_SPEC] * parts + [HBM_SPEC] * 2 + [VMEM_SPEC] * 4,
        out_specs=[VMEM_SPEC] * 3,
        out_shape=[
            jax.ShapeDtypeStruct((2, kv_heads, tokens, head_dim), jnp.float32),
            jax.ShapeDtypeStruct((tokens, heads, head_dim), jnp.float32),
            jax.ShapeDtypeStruct((2, kv_heads, tokens, grouped, head_dim), jnp.bfloat16),
        ],
        scratch_shapes=[pltpu.SemaphoreType.DMA((kv_heads, cols // rows, 2))],
        compiler_params=params,
        cost_estimate=pl.CostEstimate(flops=5 * work, bytes_accessed=2 * moved, transcendentals=0),
        name="local_block",
    )(*kv, *in_hbm(queries, grad_out), norm, term, docs, doc_col)

    inputs, sums = [], []
    after = near_kv
    for part, column in enumerate(columns):
        chosen = pl.pallas_call(
            choose_kernel,
            in_specs=[VMEM_SPEC] * (ring + 1) + [ANY_SPEC] * 2,
            out_specs=VMEM_SPEC,
            out_shape=jax.ShapeDtypeStruct((2, *span_shape), jnp.bfloat16),
            compiler_params=params,
            name="choose",
        )(places, *column, near_kv, after)
        other = swapped(chosen)
        inputs += [*column, other]
        far_kv = pl.pallas_call(
            functools.partial(listed_kernel, factor, rows, part * each),
            in_specs=[VMEM_SPEC] * (ring + 2) + row_specs,
            out_specs=VMEM_SPEC,
            out_shape=jax.ShapeDtypeStruct((2, *span_shape), jnp.bfloat16),
            compiler_params=params,
            cost_estimate=pl.CostEstimate(flops=8 * work // parts, bytes_accessed=moved // parts, transcendentals=0),
            name="listed_keys",
        )(places, *column, other, held, norm, term)
        other_kv = swapped(far_kv)
        blocks = pl.pallas_call(
            combine_kernel,
            in_specs=[VMEM_SPEC] * 3,
            out_specs=[VMEM_SPEC] * ring,
            out_shape=[jax.ShapeDtypeStruct(span_shape, jnp.float32)]
            + [jax.ShapeDtypeStruct(span_shape, jnp.bfloat16)] * (ring - 1),
            compiler_params=params,
            name="combine",
        )(places, far_kv, other_kv)
        sums += [blocks[0]] + [shifted(blocks[shift], shift) for shift in range(1, ring)]
        after = blocks[0]

    grad_queries = pl.pallas_call(
        functools.partial(query_kernel, factor, rows, parts),
        in_specs=[VMEM_SPEC] * (1 + len(inputs)) + row_specs + [VMEM_SPEC, ANY_SPEC],
        out_specs=VMEM_SPEC,
        out_shape=jax.ShapeDtypeStruct((tokens, heads, head_dim), jnp.float32),
        compiler_params=params,
        cost_estimate=pl.CostEstimate(flops=6 * work, bytes_accessed=3 * moved, transcendentals=0),
        name="listed_queries",
    )(places, *inputs, held, norm, term, near_query, after)

    grad_keys, grad_values = pl.pallas_call(
        functools.partial(total_kernel, parts),
        in_specs=[VMEM_SPEC] * (parts * ring + 1),
        out_specs=[VMEM_SPEC] * 2,
        out_shape=[jax.ShapeDtypeStruct((tokens, kv_heads, head_dim), jnp.float32)] * 2,
        compiler_params=params,
        name="total",
    )(near_kv, *sums)
    return (grad_queries, grad_keys, grad_values)


def solution(mesh):
    return jax.shard_map(
        body,
        mesh=mesh,
        in_specs=(
            P(("groups", "ctx", "sub"), "head", None),
            P(("groups", "ctx", "sub"), "head", None),
            P(("groups", "ctx", "sub"), "head", None),
            P(("groups", "ctx", "sub"), "head", None),
            P(("groups", "ctx", "sub"), "head"),
            P(("groups", "ctx", "sub"), "head"),
            P(("groups", "ctx", "sub")),
            P("groups", None),
        ),
        out_specs=(
            P(("groups", "ctx", "sub"), "head", None),
            P(("groups", "ctx", "sub"), "head", None),
            P(("groups", "ctx", "sub"), "head", None),
        ),
        check_vma=False,
    )
```

```python
import functools

import jax
import jax.numpy as jnp
from jax import lax
from jax.experimental import pallas as pl
from jax.experimental.pallas import tpu as pltpu
from jax.sharding import PartitionSpec as P

QH = 64
KVH = 4
LOG2E = 1.4426950408889634
ROWS = 512
VMEM_LIMIT = 24 * 1024 * 1024

VMEM_SPEC = pl.BlockSpec(memory_space=pltpu.VMEM)
ANY_SPEC = pl.BlockSpec(memory_space=pl.ANY)
HBM_SPEC = pl.BlockSpec(memory_space=pltpu.HBM)


def rows_dot(left, right):
    return lax.dot_general(left, right, (((1,), (1,)), ((), ())), preferred_element_type=jnp.float32)


def tile_terms(key_blk, value_blk, query_blk, upstream, log_norm, row_terms, allowed, factor):
    scores = rows_dot(key_blk, query_blk)
    probs = jnp.exp2(scores * (factor * LOG2E) - log_norm)
    if allowed is not None:
        probs = jnp.where(allowed, probs, 0.0)
    grad_probs = rows_dot(value_blk, upstream)
    grad_scores = probs * (grad_probs - row_terms)
    return probs.astype(jnp.bfloat16), grad_scores.astype(jnp.bfloat16)


def chunks(tokens, grouped, rows):
    step = rows // grouped
    return [(i, slice(i * step, (i + 1) * step), slice(i * rows, (i + 1) * rows)) for i in range(tokens // step)]


def start_all(sources, targets, sems):
    copies = [pltpu.make_async_copy(source, target, sems.at[i]) for i, (source, target) in enumerate(zip(sources, targets))]
    for copy in copies:
        copy.start()
    return copies


def bring_rows(query_ref, up_ref, held_ref, sems, rows):
    _, count, tokens, grouped, _ = held_ref.shape
    copies = {}
    for head in range(count):
        heads = slice(head * grouped, (head + 1) * grouped)
        for i, toks, _ in chunks(tokens, grouped, rows):
            copies[head, i] = [
                pltpu.make_async_copy(ref.at[toks, heads], held_ref.at[kind, head, toks], sems.at[head, i, kind])
                for kind, ref in enumerate((query_ref, up_ref))
            ]
            for copy in copies[head, i]:
                copy.start()
    return copies


def row_blocks(held_ref, head, rows, copies=None):
    _, _, tokens, grouped, head_dim = held_ref.shape
    for i, toks, cols in chunks(tokens, grouped, rows):
        for copy in copies[head, i] if copies else ():
            copy.wait()
        yield toks, cols, *(held_ref[kind, head, toks].reshape(rows, head_dim) for kind in range(2))


def pack_kernel(key_ref, value_ref, kv_ref, held_ref, sems):
    copies = start_all((key_ref, value_ref), (held_ref.at[0], held_ref.at[1]), sems)
    for kind, copy in enumerate(copies):
        copy.wait()
        for head in range(held_ref.shape[2]):
            kv_ref[kind, head] = held_ref[kind, :, head, :]


def spread_kernel(
    grouped, ring, subs, norm_ref, term_ref, docs_ref, pairs_ref,
    norm_row_ref, term_row_ref, docs_row_ref, doc_col_ref, places_ref,
    held_ref, held_docs, held_pairs, sems,
):
    _, heads, tokens = held_ref.shape
    copies = start_all(
        (pairs_ref, docs_ref, norm_ref, term_ref), (held_pairs, held_docs, held_ref.at[0], held_ref.at[1]), sems
    )
    cols = tokens * grouped
    column = lax.broadcasted_iota(jnp.int32, (tokens, cols), 1)
    token = lax.broadcasted_iota(jnp.int32, (tokens, cols), 0)
    pick = jnp.where(token == column // grouped, 1.0, 0.0).astype(jnp.bfloat16)
    keep = lax.broadcasted_iota(jnp.int32, (grouped, cols), 0) == (
        lax.broadcasted_iota(jnp.int32, (grouped, cols), 1) % grouped
    )
    for copy in copies:
        copy.wait()

    ctx, sub = lax.axis_index("ctx"), lax.axis_index("sub")
    pairs = held_pairs[...]
    lane = lax.broadcasted_iota(jnp.int32, pairs.shape, 1)

    def listed_by(core):
        mask = lane == ctx * subs + core
        span = jnp.sum(jnp.where(mask, pairs, 0).astype(jnp.float32), axis=1, keepdims=True)
        span = jnp.broadcast_to(span, (2, places_ref.shape[1])).astype(jnp.int32)
        return span // subs, span % subs

    def around(gap):
        return jnp.where(gap < 0, gap + ring, gap)

    (mine, mine_sub), (other, other_sub) = listed_by(sub), listed_by(1 - sub)
    places_ref[0:2] = around(ctx - other)
    places_ref[2:4] = around(ctx - mine) + jnp.where(mine_sub == sub, 0, ring)
    places_ref[4:6] = jnp.where(mine_sub == sub, around(mine - ctx), ring)
    places_ref[6:8] = jnp.where(other_sub == sub, around(other - ctx), ring)

    pieces = []
    for value in (held_ref[0] * LOG2E, held_ref[1]):
        for _ in range(3):
            piece = value.astype(jnp.bfloat16)
            value = value - piece.astype(jnp.float32)
            pieces.append(piece)
    docs = held_docs[...].astype(jnp.float32)
    pieces.append(jnp.broadcast_to(docs, (grouped, tokens)).astype(jnp.bfloat16))
    spread = jnp.dot(jnp.concatenate(pieces, axis=0), pick, preferred_element_type=jnp.float32)
    for i, out_ref in enumerate((norm_row_ref, term_row_ref)):
        base = 3 * i * heads
        value = spread[base:base + heads] + spread[base + heads:base + 2 * heads]
        value = value + spread[base + 2 * heads:base + 3 * heads]
        for head in range(out_ref.shape[0]):
            group = value[head * grouped:(head + 1) * grouped]
            out_ref[head] = jnp.sum(jnp.where(keep, group, 0.0), axis=0, keepdims=True)
    docs_row_ref[...] = spread[6 * heads:6 * heads + 1]
    doc_col_ref[...] = jnp.broadcast_to(docs, (tokens, tokens)).T


def pick_block(first, others, row):
    chosen = first.astype(jnp.float32)
    for code, block in others:
        chosen = jnp.where(row == code, block.astype(jnp.float32), chosen)
    return chosen.astype(jnp.bfloat16)


def choose_kernel(shifts, places_ref, *refs):
    *column, _, out_ref = refs
    for which in range(2):
        row = places_ref[which:which + 1]
        for kind in range(2):
            for head in range(out_ref.shape[2]):
                blocks = [(shift, ref[kind, head]) for shift, ref in zip(shifts, column)]
                out_ref[which, kind, head] = pick_block(blocks[0][1], blocks[1:], row)


def far_blocks(groups, ring, places_ref, column, others, head):
    held = []
    for kind in range(2):
        pair = []
        for which in range(2):
            given = [
                (ring + shift, other_ref[which, kind, head])
                for shifts, other_ref in zip(groups[1:], others[1:]) for shift in shifts
            ]
            own = [(shift, ref[kind, head]) for shift, ref in zip(sum(groups, []), column)]
            pair.append(pick_block(others[0][which, kind, head], given + own, places_ref[2 + which:3 + which]))
        held.append(jnp.concatenate(pair, axis=0))
    return held


def local_kernel(
    factor, rows, kv_ref, query_ref, up_ref, norm_ref, term_ref, docs_ref, doc_col_ref, dkv_ref, dq_ref, held_ref, sems
):
    copies = bring_rows(query_ref, up_ref, held_ref, sems, rows)
    tokens, grouped, head_dim = held_ref.shape[2:]
    doc_col = jnp.concatenate([doc_col_ref[...]] * (rows // tokens), axis=1)
    for head in range(held_ref.shape[1]):
        key_blk, value_blk = kv_ref[0, head], kv_ref[1, head]
        grad_key = jnp.zeros((tokens, head_dim), jnp.float32)
        grad_val = jnp.zeros((tokens, head_dim), jnp.float32)
        for toks, cols, query_blk, upstream in row_blocks(held_ref, head, rows, copies):
            position = lax.broadcasted_iota(jnp.int32, (tokens, rows), 1) // grouped + toks.start
            allowed = (lax.broadcasted_iota(jnp.int32, (tokens, rows), 0) <= position) & (
                doc_col == docs_ref[:, cols]
            )
            probs, grads = tile_terms(
                key_blk, value_blk, query_blk, upstream, norm_ref[head, :, cols], term_ref[head, :, cols],
                allowed, factor,
            )
            grad_val += jnp.dot(probs, upstream, preferred_element_type=jnp.float32)
            grad_key += jnp.dot(grads, query_blk, preferred_element_type=jnp.float32)
            grad_query = lax.dot_general(
                grads, key_blk, (((0,), (0,)), ((), ())), preferred_element_type=jnp.float32
            )
            dq_ref[toks, head * grouped:(head + 1) * grouped] = (grad_query * factor).reshape(
                rows // grouped, grouped, head_dim
            )
        dkv_ref[0, head] = grad_key * factor
        dkv_ref[1, head] = grad_val


def listed_kernel(factor, rows, shifts, ring, places_ref, *refs):
    *column, other_ref, held_ref, norm_ref, term_ref, _, dkv_ref = refs
    tokens, grouped, head_dim = held_ref.shape[2:]
    for head in range(other_ref.shape[2]):
        key_blk, value_blk = far_blocks([shifts], ring, places_ref, column, [other_ref], head)
        grad_key = jnp.zeros((2 * tokens, head_dim), jnp.float32)
        grad_val = jnp.zeros((2 * tokens, head_dim), jnp.float32)
        for toks, cols, query_blk, upstream in row_blocks(held_ref, head, rows):
            probs, grads = tile_terms(
                key_blk, value_blk, query_blk, upstream,
                norm_ref[head, :, cols], term_ref[head, :, cols], None, factor,
            )
            grad_val += jnp.dot(probs, upstream, preferred_element_type=jnp.float32)
            grad_key += jnp.dot(grads, query_blk, preferred_element_type=jnp.float32)
        grad_key = (grad_key * factor).astype(dkv_ref.dtype)
        grad_val = grad_val.astype(dkv_ref.dtype)
        for which in range(2):
            dkv_ref[which, 0, head] = grad_key[which * tokens:(which + 1) * tokens]
            dkv_ref[which, 1, head] = grad_val[which * tokens:(which + 1) * tokens]


def query_kernel(factor, rows, groups, ring, places_ref, *refs):
    *inputs, held_ref, norm_ref, term_ref, near_ref, _, dq_ref = refs
    tokens, grouped, head_dim = held_ref.shape[2:]
    column, others = inputs[:ring], inputs[ring:]
    for head in range(held_ref.shape[1]):
        key_blk, value_blk = far_blocks(groups, ring, places_ref, column, others, head)
        for toks, cols, query_blk, upstream in row_blocks(held_ref, head, rows):
            _, grads = tile_terms(
                key_blk, value_blk, query_blk, upstream, norm_ref[head, :, cols], term_ref[head, :, cols],
                None, factor,
            )
            grad_query = lax.dot_general(
                grads, key_blk, (((0,), (0,)), ((), ())), preferred_element_type=jnp.float32
            )
            heads = slice(head * grouped, (head + 1) * grouped)
            dq_ref[toks, heads] = near_ref[toks, heads] + (grad_query * factor).reshape(
                rows // grouped, grouped, head_dim
            )


def combine_kernel(shifts, places_ref, mine_ref, other_ref, *refs):
    for shift, out_ref in zip(shifts, refs[1:]):
        for kind in range(2):
            for head in range(out_ref.shape[1]):
                total = None
                for i, ref in enumerate((mine_ref, other_ref)):
                    for which in range(2):
                        row = places_ref[4 + 2 * i + which:5 + 2 * i + which]
                        term = jnp.where(row == shift, ref[which, kind, head].astype(jnp.float32), 0.0)
                        total = term if total is None else total + term
                out_ref[kind, head] = total.astype(out_ref.dtype)


def total_kernel(near_ref, *refs):
    *blocks, dk_ref, dv_ref = refs
    for kind, out_ref in enumerate((dk_ref, dv_ref)):
        for head in range(out_ref.shape[1]):
            total = near_ref[kind, head]
            for ref in blocks:
                total += ref[kind, head].astype(jnp.float32)
            out_ref[:, head, :] = total


def body(queries, keys, values, grad_out, row_lse, row_delta, doc_ids, pairs):
    tokens, heads, head_dim = queries.shape
    kv_heads = keys.shape[1]
    grouped = QH // KVH
    factor = head_dim ** (-0.5)
    ring = lax.axis_size("ctx")
    subs = lax.axis_size("sub")
    rows = min(ROWS, tokens * grouped)
    cols = tokens * grouped
    span_shape = (2, kv_heads, tokens, head_dim)
    near = [shift for shift in range(1, ring) if min(shift, ring - shift) <= ring // 4]
    groups = [[shift for shift in range(ring) if shift not in near], near]

    def shifted(array, shift):
        return lax.ppermute(array, "ctx", [(i, (i + shift) % ring) for i in range(ring)])

    def swapped(array):
        return lax.ppermute(array, "sub", [(i, i ^ 1) for i in range(subs)])

    def in_hbm(*arrays):
        return [pltpu.with_memory_space_constraint(array, pltpu.HBM) for array in arrays]

    params = pltpu.CompilerParams(vmem_limit_bytes=VMEM_LIMIT)
    kv = pl.pallas_call(
        pack_kernel,
        in_specs=[HBM_SPEC] * 2,
        out_specs=VMEM_SPEC,
        out_shape=jax.ShapeDtypeStruct(span_shape, jnp.bfloat16),
        scratch_shapes=[pltpu.VMEM((2, *keys.shape), jnp.bfloat16), pltpu.SemaphoreType.DMA((2,))],
        compiler_params=params,
        name="pack",
    )(*in_hbm(keys, values))
    columns = [[shifted(kv, shift) if shift else kv for shift in shifts] for shifts in groups]

    norm, term, docs, doc_col, places = pl.pallas_call(
        functools.partial(spread_kernel, grouped, ring, subs),
        in_specs=[HBM_SPEC] * 4,
        out_specs=[VMEM_SPEC] * 5,
        out_shape=[
            jax.ShapeDtypeStruct((kv_heads, 1, cols), jnp.float32),
            jax.ShapeDtypeStruct((kv_heads, 1, cols), jnp.float32),
            jax.ShapeDtypeStruct((1, cols), jnp.float32),
            jax.ShapeDtypeStruct((tokens, tokens), jnp.float32),
            jax.ShapeDtypeStruct((8, head_dim), jnp.int32),
        ],
        scratch_shapes=[
            pltpu.VMEM((2, heads, tokens), jnp.float32),
            pltpu.VMEM((1, tokens), jnp.int32),
            pltpu.VMEM(pairs.shape[::-1], jnp.int32),
            pltpu.SemaphoreType.DMA((4,)),
        ],
        compiler_params=params,
        name="spread",
    )(*in_hbm(row_lse.T, row_delta.T, doc_ids.reshape(1, tokens), pairs.T))

    work = 2 * tokens * tokens * heads * head_dim
    moved = 2 * queries.size * 2

    row_specs = [VMEM_SPEC] * 3
    near_kv, near_query, held = pl.pallas_call(
        functools.partial(local_kernel, factor, rows),
        in_specs=[VMEM_SPEC] + [HBM_SPEC] * 2 + [VMEM_SPEC] * 4,
        out_specs=[VMEM_SPEC] * 3,
        out_shape=[
            jax.ShapeDtypeStruct((2, kv_heads, tokens, head_dim), jnp.float32),
            jax.ShapeDtypeStruct((tokens, heads, head_dim), jnp.float32),
            jax.ShapeDtypeStruct((2, kv_heads, tokens, grouped, head_dim), jnp.bfloat16),
        ],
        scratch_shapes=[pltpu.SemaphoreType.DMA((kv_heads, cols // rows, 2))],
        compiler_params=params,
        cost_estimate=pl.CostEstimate(flops=5 * work, bytes_accessed=2 * moved, transcendentals=0),
        name="local_block",
    )(kv, *in_hbm(queries, grad_out), norm, term, docs, doc_col)

    def choose(group, after):
        return pl.pallas_call(
            functools.partial(choose_kernel, groups[group]),
            in_specs=[VMEM_SPEC] * (len(groups[group]) + 1) + [ANY_SPEC],
            out_specs=VMEM_SPEC,
            out_shape=jax.ShapeDtypeStruct((2, *span_shape), jnp.bfloat16),
            compiler_params=params,
            name="choose",
        )(places, *columns[group], after)

    def listed(group, other, after):
        return pl.pallas_call(
            functools.partial(listed_kernel, factor, rows, groups[group], ring),
            in_specs=[VMEM_SPEC] * (len(groups[group]) + 2) + row_specs + [ANY_SPEC],
            out_specs=VMEM_SPEC,
            out_shape=jax.ShapeDtypeStruct((2, *span_shape), jnp.bfloat16),
            compiler_params=params,
            cost_estimate=pl.CostEstimate(flops=8 * work, bytes_accessed=moved, transcendentals=0),
            name="listed_keys",
        )(places, *columns[group], other, held, norm, term, after)

    def combine(group, far_kv, other_kv, after):
        return pl.pallas_call(
            functools.partial(combine_kernel, groups[group]),
            in_specs=[VMEM_SPEC] * 3 + [ANY_SPEC],
            out_specs=[VMEM_SPEC] * len(groups[group]),
            out_shape=[
                jax.ShapeDtypeStruct(span_shape, jnp.bfloat16 if shift else jnp.float32) for shift in groups[group]
            ],
            compiler_params=params,
            name="combine",
        )(places, far_kv, other_kv, after)

    chosen = choose(0, near_kv)
    others = [swapped(chosen)]
    far_kv = listed(0, others[0], near_kv)
    other_kv = swapped(far_kv)
    chosen = choose(1, far_kv)
    others.append(swapped(chosen))
    blocks = combine(0, far_kv, other_kv, chosen)
    sums = [shifted(block, shift) if shift else block for shift, block in zip(groups[0], blocks)]
    far_kv = listed(1, others[1], blocks[0])
    blocks = combine(1, far_kv, swapped(far_kv), far_kv)
    sums += [shifted(block, shift) for shift, block in zip(groups[1], blocks)]

    grad_queries = pl.pallas_call(
        functools.partial(query_kernel, factor, rows, groups, ring),
        in_specs=[VMEM_SPEC] * (1 + ring + len(groups)) + row_specs + [VMEM_SPEC, ANY_SPEC],
        out_specs=VMEM_SPEC,
        out_shape=jax.ShapeDtypeStruct((tokens, heads, head_dim), jnp.float32),
        compiler_params=params,
        cost_estimate=pl.CostEstimate(flops=6 * work, bytes_accessed=3 * moved, transcendentals=0),
        name="listed_queries",
    )(places, *columns[0], *columns[1], *others, held, norm, term, near_query, blocks[0])

    grad_keys, grad_values = pl.pallas_call(
        total_kernel,
        in_specs=[VMEM_SPEC] * (ring + 1),
        out_specs=[VMEM_SPEC] * 2,
        out_shape=[jax.ShapeDtypeStruct((tokens, kv_heads, head_dim), jnp.float32)] * 2,
        compiler_params=params,
        name="total",
    )(near_kv, *sums)
    return (grad_queries, grad_keys, grad_values)


def solution(mesh):
    return jax.shard_map(
        body,
        mesh=mesh,
        in_specs=(
            P(("groups", "ctx", "sub"), "head", None),
            P(("groups", "ctx", "sub"), "head", None),
            P(("groups", "ctx", "sub"), "head", None),
            P(("groups", "ctx", "sub"), "head", None),
            P(("groups", "ctx", "sub"), "head"),
            P(("groups", "ctx", "sub"), "head"),
            P(("groups", "ctx", "sub")),
            P("groups", None),
        ),
        out_specs=(
            P(("groups", "ctx", "sub"), "head", None),
            P(("groups", "ctx", "sub"), "head", None),
            P(("groups", "ctx", "sub"), "head", None),
        ),
        check_vma=False,
    )
```

```python
import functools

import jax
import jax.numpy as jnp
from jax import lax
from jax.experimental import pallas as pl
from jax.experimental.pallas import tpu as pltpu
from jax.sharding import PartitionSpec as P

QH = 64
KVH = 4
LOG2E = 1.4426950408889634
ROWS = 512
VMEM_LIMIT = 24 * 1024 * 1024

VMEM_SPEC = pl.BlockSpec(memory_space=pltpu.VMEM)
ANY_SPEC = pl.BlockSpec(memory_space=pl.ANY)
HBM_SPEC = pl.BlockSpec(memory_space=pltpu.HBM)


def rows_dot(left, right):
    return lax.dot_general(left, right, (((1,), (1,)), ((), ())), preferred_element_type=jnp.float32)


def tile_terms(key_blk, value_blk, query_blk, upstream, log_norm, row_terms, allowed, factor):
    scores = rows_dot(key_blk, query_blk)
    probs = jnp.exp2(scores * (factor * LOG2E) - log_norm)
    if allowed is not None:
        probs = jnp.where(allowed, probs, 0.0)
    grad_probs = rows_dot(value_blk, upstream)
    grad_scores = probs * (grad_probs - row_terms)
    return probs.astype(jnp.bfloat16), grad_scores.astype(jnp.bfloat16)


def chunks(tokens, grouped, rows):
    step = rows // grouped
    return [(i, slice(i * step, (i + 1) * step), slice(i * rows, (i + 1) * rows)) for i in range(tokens // step)]


def start_all(sources, targets, sems):
    copies = [pltpu.make_async_copy(source, target, sems.at[i]) for i, (source, target) in enumerate(zip(sources, targets))]
    for copy in copies:
        copy.start()
    return copies


def bring_rows(query_ref, up_ref, held_ref, sems, rows):
    _, count, tokens, grouped, _ = held_ref.shape
    copies = {}
    for head in range(count):
        heads = slice(head * grouped, (head + 1) * grouped)
        for i, toks, _ in chunks(tokens, grouped, rows):
            copies[head, i] = [
                pltpu.make_async_copy(ref.at[toks, heads], held_ref.at[kind, head, toks], sems.at[head, i, kind])
                for kind, ref in enumerate((query_ref, up_ref))
            ]
            for copy in copies[head, i]:
                copy.start()
    return copies


def row_blocks(held_ref, head, rows):
    _, _, tokens, grouped, head_dim = held_ref.shape
    for _, toks, cols in chunks(tokens, grouped, rows):
        yield toks, cols, *(held_ref[kind, head, toks].reshape(rows, head_dim) for kind in range(2))


def pack_kernel(key_ref, value_ref, kv_ref, held_ref, sems):
    copies = start_all((key_ref, value_ref), (held_ref.at[0], held_ref.at[1]), sems)
    for kind, copy in enumerate(copies):
        copy.wait()
        for head in range(held_ref.shape[2]):
            kv_ref[kind, head] = held_ref[kind, :, head, :]


def spread_kernel(
    grouped, ring, subs, rows, norm_ref, term_ref, docs_ref, pairs_ref, query_ref, up_ref,
    norm_row_ref, term_row_ref, docs_row_ref, doc_col_ref, places_ref, row_ref,
    held_ref, held_docs, held_pairs, sems, row_sems,
):
    _, heads, tokens = held_ref.shape
    copies = start_all(
        (pairs_ref, docs_ref, norm_ref, term_ref), (held_pairs, held_docs, held_ref.at[0], held_ref.at[1]), sems
    )
    brought = bring_rows(query_ref, up_ref, row_ref, row_sems, rows)
    cols = tokens * grouped
    column = lax.broadcasted_iota(jnp.int32, (tokens, cols), 1)
    token = lax.broadcasted_iota(jnp.int32, (tokens, cols), 0)
    pick = jnp.where(token == column // grouped, 1.0, 0.0).astype(jnp.bfloat16)
    keep = lax.broadcasted_iota(jnp.int32, (grouped, cols), 0) == (
        lax.broadcasted_iota(jnp.int32, (grouped, cols), 1) % grouped
    )
    for copy in copies:
        copy.wait()

    ctx, sub = lax.axis_index("ctx"), lax.axis_index("sub")
    pairs = held_pairs[...]
    lane = lax.broadcasted_iota(jnp.int32, pairs.shape, 1)

    def listed_by(core):
        mask = lane == ctx * subs + core
        span = jnp.sum(jnp.where(mask, pairs, 0).astype(jnp.float32), axis=1, keepdims=True)
        span = jnp.broadcast_to(span, (2, places_ref.shape[1])).astype(jnp.int32)
        return span // subs, span % subs

    (mine, mine_sub), (other, other_sub) = listed_by(sub), listed_by(1 - sub)
    places_ref[0:2] = other ^ ctx
    places_ref[2:4] = jnp.where(mine_sub == sub, mine ^ ctx, ring)
    places_ref[4:6] = places_ref[2:4]
    places_ref[6:8] = jnp.where(other_sub == sub, other ^ ctx, ring)

    pieces = []
    for value in (held_ref[0] * LOG2E, held_ref[1]):
        for _ in range(3):
            piece = value.astype(jnp.bfloat16)
            value = value - piece.astype(jnp.float32)
            pieces.append(piece)
    docs = held_docs[...].astype(jnp.float32)
    pieces.append(jnp.broadcast_to(docs, (grouped, tokens)).astype(jnp.bfloat16))
    spread = jnp.dot(jnp.concatenate(pieces, axis=0), pick, preferred_element_type=jnp.float32)
    for i, out_ref in enumerate((norm_row_ref, term_row_ref)):
        base = 3 * i * heads
        value = spread[base:base + heads] + spread[base + heads:base + 2 * heads]
        value = value + spread[base + 2 * heads:base + 3 * heads]
        for head in range(out_ref.shape[0]):
            group = value[head * grouped:(head + 1) * grouped]
            out_ref[head] = jnp.sum(jnp.where(keep, group, 0.0), axis=0, keepdims=True)
    docs_row_ref[...] = spread[6 * heads:6 * heads + 1]
    doc_col_ref[...] = jnp.broadcast_to(docs, (tokens, tokens)).T
    for pair in brought.values():
        for copy in pair:
            copy.wait()


def pick_block(sources, row):
    chosen = sources[0].astype(jnp.float32)
    for step in range(1, len(sources)):
        chosen = jnp.where(row == step, sources[step].astype(jnp.float32), chosen)
    return chosen.astype(jnp.bfloat16)


def choose_kernel(places_ref, *refs):
    *column, _, out_ref = refs
    for which in range(2):
        row = places_ref[which:which + 1]
        for kind in range(2):
            for head in range(out_ref.shape[2]):
                out_ref[which, kind, head] = pick_block([ref[kind, head] for ref in column], row)


def far_blocks(places_ref, column, other_ref, head):
    return [
        jnp.concatenate(
            [
                pick_block(
                    [ref[kind, head] for ref in column] + [other_ref[which, kind, head]],
                    places_ref[2 + which:3 + which],
                )
                for which in range(2)
            ],
            axis=0,
        )
        for kind in range(2)
    ]


def local_kernel(
    factor, rows, first, kv_ref, row_ref, norm_ref, term_ref, docs_ref, doc_col_ref, _, dkv_ref, dq_ref
):
    tokens, grouped, head_dim = row_ref.shape[2:]
    doc_col = jnp.concatenate([doc_col_ref[...]] * (rows // tokens), axis=1)
    for place in range(dkv_ref.shape[1]):
        head = first + place
        key_blk, value_blk = kv_ref[0, head], kv_ref[1, head]
        grad_key = jnp.zeros((tokens, head_dim), jnp.float32)
        grad_val = jnp.zeros((tokens, head_dim), jnp.float32)
        for toks, cols, query_blk, upstream in row_blocks(row_ref, head, rows):
            position = lax.broadcasted_iota(jnp.int32, (tokens, rows), 1) // grouped + toks.start
            allowed = (lax.broadcasted_iota(jnp.int32, (tokens, rows), 0) <= position) & (
                doc_col == docs_ref[:, cols]
            )
            probs, grads = tile_terms(
                key_blk, value_blk, query_blk, upstream, norm_ref[head, :, cols], term_ref[head, :, cols],
                allowed, factor,
            )
            grad_val += jnp.dot(probs, upstream, preferred_element_type=jnp.float32)
            grad_key += jnp.dot(grads, query_blk, preferred_element_type=jnp.float32)
            grad_query = lax.dot_general(
                grads, key_blk, (((0,), (0,)), ((), ())), preferred_element_type=jnp.float32
            )
            dq_ref[toks, place * grouped:(place + 1) * grouped] = (grad_query * factor).reshape(
                rows // grouped, grouped, head_dim
            )
        dkv_ref[0, place] = grad_key * factor
        dkv_ref[1, place] = grad_val


def listed_kernel(factor, rows, places_ref, *refs):
    *column, other_ref, held_ref, norm_ref, term_ref, dkv_ref = refs
    tokens, grouped, head_dim = held_ref.shape[2:]
    for head in range(other_ref.shape[2]):
        key_blk, value_blk = far_blocks(places_ref, column, other_ref, head)
        grad_key = jnp.zeros((2 * tokens, head_dim), jnp.float32)
        grad_val = jnp.zeros((2 * tokens, head_dim), jnp.float32)
        for toks, cols, query_blk, upstream in row_blocks(held_ref, head, rows):
            probs, grads = tile_terms(
                key_blk, value_blk, query_blk, upstream,
                norm_ref[head, :, cols], term_ref[head, :, cols], None, factor,
            )
            grad_val += jnp.dot(probs, upstream, preferred_element_type=jnp.float32)
            grad_key += jnp.dot(grads, query_blk, preferred_element_type=jnp.float32)
        grad_key = (grad_key * factor).astype(dkv_ref.dtype)
        grad_val = grad_val.astype(dkv_ref.dtype)
        for which in range(2):
            dkv_ref[which, 0, head] = grad_key[which * tokens:(which + 1) * tokens]
            dkv_ref[which, 1, head] = grad_val[which * tokens:(which + 1) * tokens]


def query_kernel(factor, rows, places_ref, *refs):
    *column, other_ref, held_ref, norm_ref, term_ref, near_one, near_two, _, dq_ref = refs
    tokens, grouped, head_dim = held_ref.shape[2:]
    half = near_one.shape[1] // grouped
    for head in range(held_ref.shape[1]):
        near_ref, place = (near_one, head) if head < half else (near_two, head - half)
        key_blk, value_blk = far_blocks(places_ref, column, other_ref, head)
        for toks, cols, query_blk, upstream in row_blocks(held_ref, head, rows):
            _, grads = tile_terms(
                key_blk, value_blk, query_blk, upstream, norm_ref[head, :, cols], term_ref[head, :, cols],
                None, factor,
            )
            grad_query = lax.dot_general(
                grads, key_blk, (((0,), (0,)), ((), ())), preferred_element_type=jnp.float32
            )
            near = near_ref[toks, place * grouped:(place + 1) * grouped]
            dq_ref[toks, head * grouped:(head + 1) * grouped] = near + (grad_query * factor).reshape(
                rows // grouped, grouped, head_dim
            )


def combine_kernel(places_ref, mine_ref, other_ref, *out_refs):
    for step, out_ref in enumerate(out_refs):
        for kind in range(2):
            for head in range(out_ref.shape[1]):
                total = None
                for i, ref in enumerate((mine_ref, other_ref)):
                    for which in range(2):
                        row = places_ref[4 + 2 * i + which:5 + 2 * i + which]
                        term = jnp.where(row == step, ref[which, kind, head].astype(jnp.float32), 0.0)
                        total = term if total is None else total + term
                out_ref[kind, head] = total.astype(out_ref.dtype)


def merge_kernel(own_ref, *refs):
    *arrived, _, out_ref = refs
    total = own_ref[...]
    for ref in arrived:
        total += ref[...].astype(jnp.float32)
    out_ref[...] = total.astype(out_ref.dtype)


def total_kernel(near_one, near_two, *refs):
    *blocks, dk_ref, dv_ref = refs
    half = near_one.shape[1]
    for kind, out_ref in enumerate((dk_ref, dv_ref)):
        for head in range(out_ref.shape[1]):
            total = near_one[kind, head] if head < half else near_two[kind, head - half]
            for ref in blocks:
                total += ref[kind, head].astype(jnp.float32)
            out_ref[:, head, :] = total


def body(queries, keys, values, grad_out, row_lse, row_delta, doc_ids, pairs):
    tokens, heads, head_dim = queries.shape
    kv_heads = keys.shape[1]
    grouped = QH // KVH
    factor = head_dim ** (-0.5)
    ring = lax.axis_size("ctx")
    subs = lax.axis_size("sub")
    rows = min(ROWS, tokens * grouped)
    cols = tokens * grouped
    span_shape = (2, kv_heads, tokens, head_dim)

    def crossed(array, bit):
        return lax.ppermute(array, "ctx", [(i, i ^ bit) for i in range(ring)])

    def swapped(array):
        return lax.ppermute(array, "sub", [(i, i ^ 1) for i in range(subs)])

    def in_hbm(*arrays):
        return [pltpu.with_memory_space_constraint(array, pltpu.HBM) for array in arrays]

    params = pltpu.CompilerParams(vmem_limit_bytes=VMEM_LIMIT)
    kv = pl.pallas_call(
        pack_kernel,
        in_specs=[HBM_SPEC] * 2,
        out_specs=VMEM_SPEC,
        out_shape=jax.ShapeDtypeStruct(span_shape, jnp.bfloat16),
        scratch_shapes=[pltpu.VMEM((2, *keys.shape), jnp.bfloat16), pltpu.SemaphoreType.DMA((2,))],
        compiler_params=params,
        name="pack",
    )(*in_hbm(keys, values))
    column = {0: kv}
    for place in sorted(range(1, ring), key=lambda place: -(place & -place)):
        low = place & -place
        column[place] = crossed(column[place ^ low], low)
    column = [column[place] for place in range(ring)]

    norm, term, docs, doc_col, places, held = pl.pallas_call(
        functools.partial(spread_kernel, grouped, ring, subs, rows),
        in_specs=[HBM_SPEC] * 6,
        out_specs=[VMEM_SPEC] * 6,
        out_shape=[
            jax.ShapeDtypeStruct((kv_heads, 1, cols), jnp.float32),
            jax.ShapeDtypeStruct((kv_heads, 1, cols), jnp.float32),
            jax.ShapeDtypeStruct((1, cols), jnp.float32),
            jax.ShapeDtypeStruct((tokens, tokens), jnp.float32),
            jax.ShapeDtypeStruct((8, head_dim), jnp.int32),
            jax.ShapeDtypeStruct((2, kv_heads, tokens, grouped, head_dim), jnp.bfloat16),
        ],
        scratch_shapes=[
            pltpu.VMEM((2, heads, tokens), jnp.float32),
            pltpu.VMEM((1, tokens), jnp.int32),
            pltpu.VMEM(pairs.shape[::-1], jnp.int32),
            pltpu.SemaphoreType.DMA((4,)),
            pltpu.SemaphoreType.DMA((kv_heads, cols // rows, 2)),
        ],
        compiler_params=params,
        name="spread",
    )(*in_hbm(row_lse.T, row_delta.T, doc_ids.reshape(1, tokens), pairs.T, queries, grad_out))

    work = 2 * tokens * tokens * heads * head_dim
    moved = 2 * queries.size * 2

    row_specs = [VMEM_SPEC] * 3
    half = (kv_heads + 1) // 2

    def local(first, count, after):
        return pl.pallas_call(
            functools.partial(local_kernel, factor, rows, first),
            in_specs=[VMEM_SPEC] + row_specs + [VMEM_SPEC] * 2 + [ANY_SPEC],
            out_specs=[VMEM_SPEC] * 2,
            out_shape=[
                jax.ShapeDtypeStruct((2, count, tokens, head_dim), jnp.float32),
                jax.ShapeDtypeStruct((tokens, count * grouped, head_dim), jnp.float32),
            ],
            compiler_params=params,
            cost_estimate=pl.CostEstimate(
                flops=5 * work * count // kv_heads, bytes_accessed=2 * moved * count // kv_heads, transcendentals=0
            ),
            name="local_block",
        )(kv, held, norm, term, docs, doc_col, after)

    near_kv, near_query = local(0, half, places)

    chosen = pl.pallas_call(
        choose_kernel,
        in_specs=[VMEM_SPEC] * (ring + 1) + [ANY_SPEC],
        out_specs=VMEM_SPEC,
        out_shape=jax.ShapeDtypeStruct((2, *span_shape), jnp.bfloat16),
        compiler_params=params,
        name="choose",
    )(places, *column, near_kv)
    other = swapped(chosen)
    far_kv = pl.pallas_call(
        functools.partial(listed_kernel, factor, rows),
        in_specs=[VMEM_SPEC] * (ring + 2) + row_specs,
        out_specs=VMEM_SPEC,
        out_shape=jax.ShapeDtypeStruct((2, *span_shape), jnp.bfloat16),
        compiler_params=params,
        cost_estimate=pl.CostEstimate(flops=8 * work, bytes_accessed=moved, transcendentals=0),
        name="listed_keys",
    )(places, *column, other, held, norm, term)
    other_kv = swapped(far_kv)
    sums = pl.pallas_call(
        combine_kernel,
        in_specs=[VMEM_SPEC] * 3,
        out_specs=[VMEM_SPEC] * ring,
        out_shape=[
            jax.ShapeDtypeStruct(span_shape, jnp.bfloat16 if place % 2 else jnp.float32) for place in range(ring)
        ],
        compiler_params=params,
        name="combine",
    )(places, far_kv, other_kv)

    after, last = sums[0], (near_kv, near_query)
    if half < kv_heads:
        last = local(half, kv_heads - half, after)
        after = last[0]
    arrived = {place: [] for place in range(ring)}
    for place in sorted(range(1, ring), key=lambda place: (place & -place, -place)):
        low = place & -place
        block = sums[place]
        if arrived[place]:
            block = pl.pallas_call(
                merge_kernel,
                in_specs=[VMEM_SPEC] * (1 + len(arrived[place])) + [ANY_SPEC],
                out_specs=VMEM_SPEC,
                out_shape=jax.ShapeDtypeStruct(span_shape, jnp.bfloat16),
                compiler_params=params,
                name="merge",
            )(block, *arrived[place], after)
            after = block
        arrived[place ^ low].append(crossed(block, low))

    grad_queries = pl.pallas_call(
        functools.partial(query_kernel, factor, rows),
        in_specs=[VMEM_SPEC] * (2 + ring) + row_specs + [VMEM_SPEC] * 2 + [ANY_SPEC],
        out_specs=VMEM_SPEC,
        out_shape=jax.ShapeDtypeStruct((tokens, heads, head_dim), jnp.float32),
        compiler_params=params,
        cost_estimate=pl.CostEstimate(flops=6 * work, bytes_accessed=3 * moved, transcendentals=0),
        name="listed_queries",
    )(places, *column, other, held, norm, term, near_query, last[1], after)

    grad_keys, grad_values = pl.pallas_call(
        total_kernel,
        in_specs=[VMEM_SPEC] * (3 + len(arrived[0])),
        out_specs=[VMEM_SPEC] * 2,
        out_shape=[jax.ShapeDtypeStruct((tokens, kv_heads, head_dim), jnp.float32)] * 2,
        compiler_params=params,
        name="total",
    )(near_kv, last[0], sums[0], *arrived[0])
    return (grad_queries, grad_keys, grad_values)


def solution(mesh):
    return jax.shard_map(
        body,
        mesh=mesh,
        in_specs=(
            P(("groups", "ctx", "sub"), "head", None),
            P(("groups", "ctx", "sub"), "head", None),
            P(("groups", "ctx", "sub"), "head", None),
            P(("groups", "ctx", "sub"), "head", None),
            P(("groups", "ctx", "sub"), "head"),
            P(("groups", "ctx", "sub"), "head"),
            P(("groups", "ctx", "sub")),
            P("groups", None),
        ),
        out_specs=(
            P(("groups", "ctx", "sub"), "head", None),
            P(("groups", "ctx", "sub"), "head", None),
            P(("groups", "ctx", "sub"), "head", None),
        ),
        check_vma=False,
    )
```

```python
import functools

import jax
import jax.numpy as jnp
from jax import lax
from jax.experimental import pallas as pl
from jax.experimental.pallas import tpu as pltpu
from jax.sharding import PartitionSpec as P

QH = 64
KVH = 4
LOG2E = 1.4426950408889634
ROWS = 512
VMEM_LIMIT = 24 * 1024 * 1024

VMEM_SPEC = pl.BlockSpec(memory_space=pltpu.VMEM)
ANY_SPEC = pl.BlockSpec(memory_space=pl.ANY)
HBM_SPEC = pl.BlockSpec(memory_space=pltpu.HBM)


def rows_dot(left, right):
    return lax.dot_general(left, right, (((1,), (1,)), ((), ())), preferred_element_type=jnp.float32)


def tile_terms(key_blk, value_blk, query_blk, upstream, log_norm, row_terms, allowed, factor):
    scores = rows_dot(key_blk, query_blk)
    probs = jnp.exp2(scores * (factor * LOG2E) - log_norm)
    if allowed is not None:
        probs = jnp.where(allowed, probs, 0.0)
    grad_probs = rows_dot(value_blk, upstream)
    grad_scores = probs * (grad_probs - row_terms)
    return probs.astype(jnp.bfloat16), grad_scores.astype(jnp.bfloat16)


def chunks(tokens, grouped, rows):
    step = rows // grouped
    return [(i, slice(i * step, (i + 1) * step), slice(i * rows, (i + 1) * rows)) for i in range(tokens // step)]


def start_all(sources, targets, sems):
    copies = [pltpu.make_async_copy(source, target, sems.at[i]) for i, (source, target) in enumerate(zip(sources, targets))]
    for copy in copies:
        copy.start()
    return copies


def bring_rows(query_ref, up_ref, held_ref, sems, rows):
    _, count, tokens, grouped, _ = held_ref.shape
    copies = {}
    for head in range(count):
        heads = slice(head * grouped, (head + 1) * grouped)
        for i, toks, _ in chunks(tokens, grouped, rows):
            copies[head, i] = [
                pltpu.make_async_copy(ref.at[toks, heads], held_ref.at[kind, head, toks], sems.at[head, i, kind])
                for kind, ref in enumerate((query_ref, up_ref))
            ]
            for copy in copies[head, i]:
                copy.start()
    return copies


def row_blocks(held_ref, head, rows):
    _, _, tokens, grouped, head_dim = held_ref.shape
    for _, toks, cols in chunks(tokens, grouped, rows):
        yield toks, cols, *(held_ref[kind, head, toks].reshape(rows, head_dim) for kind in range(2))


def pack_kernel(key_ref, value_ref, kv_ref, held_ref, sems):
    copies = start_all((key_ref, value_ref), (held_ref.at[0], held_ref.at[1]), sems)
    for kind, copy in enumerate(copies):
        copy.wait()
        for head in range(held_ref.shape[2]):
            kv_ref[kind, head] = held_ref[kind, :, head, :]


def spread_kernel(
    grouped, ring, subs, rows, norm_ref, term_ref, docs_ref, pairs_ref, query_ref, up_ref,
    norm_row_ref, term_row_ref, docs_row_ref, doc_col_ref, places_ref, row_ref,
    held_ref, held_docs, held_pairs, sems, row_sems,
):
    _, heads, tokens = held_ref.shape
    copies = start_all(
        (pairs_ref, docs_ref, norm_ref, term_ref), (held_pairs, held_docs, held_ref.at[0], held_ref.at[1]), sems
    )
    brought = bring_rows(query_ref, up_ref, row_ref, row_sems, rows)
    cols = tokens * grouped
    column = lax.broadcasted_iota(jnp.int32, (tokens, cols), 1)
    token = lax.broadcasted_iota(jnp.int32, (tokens, cols), 0)
    pick = jnp.where(token == column // grouped, 1.0, 0.0).astype(jnp.bfloat16)
    keep = lax.broadcasted_iota(jnp.int32, (grouped, cols), 0) == (
        lax.broadcasted_iota(jnp.int32, (grouped, cols), 1) % grouped
    )
    for copy in copies:
        copy.wait()

    ctx, sub = lax.axis_index("ctx"), lax.axis_index("sub")
    pairs = held_pairs[...]
    lane = lax.broadcasted_iota(jnp.int32, pairs.shape, 1)

    def listed_by(core):
        mask = lane == ctx * subs + core
        span = jnp.sum(jnp.where(mask, pairs, 0).astype(jnp.float32), axis=1, keepdims=True)
        span = jnp.broadcast_to(span, (2, places_ref.shape[1])).astype(jnp.int32)
        return span // subs, span % subs

    (mine, mine_sub), (other, other_sub) = listed_by(sub), listed_by(1 - sub)
    places_ref[0:2] = other ^ ctx
    places_ref[2:4] = jnp.where(mine_sub == sub, mine ^ ctx, ring)
    places_ref[4:6] = places_ref[2:4]
    places_ref[6:8] = jnp.where(other_sub == sub, other ^ ctx, ring)

    pieces = []
    for value in (held_ref[0] * LOG2E, held_ref[1]):
        for _ in range(3):
            piece = value.astype(jnp.bfloat16)
            value = value - piece.astype(jnp.float32)
            pieces.append(piece)
    docs = held_docs[...].astype(jnp.float32)
    pieces.append(jnp.broadcast_to(docs, (grouped, tokens)).astype(jnp.bfloat16))
    spread = jnp.dot(jnp.concatenate(pieces, axis=0), pick, preferred_element_type=jnp.float32)
    for i, out_ref in enumerate((norm_row_ref, term_row_ref)):
        base = 3 * i * heads
        value = spread[base:base + heads] + spread[base + heads:base + 2 * heads]
        value = value + spread[base + 2 * heads:base + 3 * heads]
        for head in range(out_ref.shape[0]):
            group = value[head * grouped:(head + 1) * grouped]
            out_ref[head] = jnp.sum(jnp.where(keep, group, 0.0), axis=0, keepdims=True)
    docs_row_ref[...] = spread[6 * heads:6 * heads + 1]
    doc_col_ref[...] = jnp.broadcast_to(docs, (tokens, tokens)).T
    for pair in brought.values():
        for copy in pair:
            copy.wait()


def pick_block(sources, row):
    chosen = sources[0].astype(jnp.float32)
    for step in range(1, len(sources)):
        chosen = jnp.where(row == step, sources[step].astype(jnp.float32), chosen)
    return chosen.astype(jnp.bfloat16)


def choose_kernel(places_ref, *refs):
    *column, _, out_ref = refs
    for which in range(2):
        row = places_ref[which:which + 1]
        for kind in range(2):
            for head in range(out_ref.shape[2]):
                out_ref[which, kind, head] = pick_block([ref[kind, head] for ref in column], row)


def far_blocks(places_ref, column, other_ref, head):
    return [
        jnp.concatenate(
            [
                pick_block(
                    [ref[kind, head] for ref in column] + [other_ref[which, kind, head]],
                    places_ref[2 + which:3 + which],
                )
                for which in range(2)
            ],
            axis=0,
        )
        for kind in range(2)
    ]


def local_kernel(
    factor, rows, first, kv_ref, row_ref, norm_ref, term_ref, docs_ref, doc_col_ref, _, dkv_ref, dq_ref
):
    tokens, grouped, head_dim = row_ref.shape[2:]
    doc_col = jnp.concatenate([doc_col_ref[...]] * (rows // tokens), axis=1)
    for place in range(dkv_ref.shape[1]):
        head = first + place
        key_blk, value_blk = kv_ref[0, head], kv_ref[1, head]
        grad_key = jnp.zeros((tokens, head_dim), jnp.float32)
        grad_val = jnp.zeros((tokens, head_dim), jnp.float32)
        for toks, cols, query_blk, upstream in row_blocks(row_ref, head, rows):
            position = lax.broadcasted_iota(jnp.int32, (tokens, rows), 1) // grouped + toks.start
            allowed = (lax.broadcasted_iota(jnp.int32, (tokens, rows), 0) <= position) & (
                doc_col == docs_ref[:, cols]
            )
            probs, grads = tile_terms(
                key_blk, value_blk, query_blk, upstream, norm_ref[head, :, cols], term_ref[head, :, cols],
                allowed, factor,
            )
            grad_val += jnp.dot(probs, upstream, preferred_element_type=jnp.float32)
            grad_key += jnp.dot(grads, query_blk, preferred_element_type=jnp.float32)
            grad_query = lax.dot_general(
                grads, key_blk, (((0,), (0,)), ((), ())), preferred_element_type=jnp.float32
            )
            dq_ref[toks, place * grouped:(place + 1) * grouped] = (grad_query * factor).reshape(
                rows // grouped, grouped, head_dim
            )
        dkv_ref[0, place] = grad_key * factor
        dkv_ref[1, place] = grad_val


def listed_kernel(factor, rows, places_ref, *refs):
    *column, other_ref, held_ref, norm_ref, term_ref, dkv_ref = refs
    tokens, grouped, head_dim = held_ref.shape[2:]
    for head in range(other_ref.shape[2]):
        key_blk, value_blk = far_blocks(places_ref, column, other_ref, head)
        grad_key = jnp.zeros((2 * tokens, head_dim), jnp.float32)
        grad_val = jnp.zeros((2 * tokens, head_dim), jnp.float32)
        for toks, cols, query_blk, upstream in row_blocks(held_ref, head, rows):
            probs, grads = tile_terms(
                key_blk, value_blk, query_blk, upstream,
                norm_ref[head, :, cols], term_ref[head, :, cols], None, factor,
            )
            grad_val += jnp.dot(probs, upstream, preferred_element_type=jnp.float32)
            grad_key += jnp.dot(grads, query_blk, preferred_element_type=jnp.float32)
        grad_key = (grad_key * factor).astype(dkv_ref.dtype)
        grad_val = grad_val.astype(dkv_ref.dtype)
        for which in range(2):
            dkv_ref[which, 0, head] = grad_key[which * tokens:(which + 1) * tokens]
            dkv_ref[which, 1, head] = grad_val[which * tokens:(which + 1) * tokens]


def query_kernel(factor, rows, ready, places_ref, *refs):
    *column, other_ref, held_ref, norm_ref, term_ref, near_one, near_two, _, dq_ref = refs
    tokens, grouped, head_dim = held_ref.shape[2:]
    half = near_one.shape[1] // grouped
    if ready:
        dq_ref[:, :ready * grouped] = near_one[...]
    for head in range(ready, dq_ref.shape[1] // grouped):
        near_ref, place = (near_one, head) if head < half else (near_two, head - half)
        key_blk, value_blk = far_blocks(places_ref, column, other_ref, head)
        for toks, cols, query_blk, upstream in row_blocks(held_ref, head, rows):
            _, grads = tile_terms(
                key_blk, value_blk, query_blk, upstream, norm_ref[head, :, cols], term_ref[head, :, cols],
                None, factor,
            )
            grad_query = lax.dot_general(
                grads, key_blk, (((0,), (0,)), ((), ())), preferred_element_type=jnp.float32
            )
            near = near_ref[toks, place * grouped:(place + 1) * grouped]
            dq_ref[toks, head * grouped:(head + 1) * grouped] = near + (grad_query * factor).reshape(
                rows // grouped, grouped, head_dim
            )


def combine_kernel(places_ref, mine_ref, other_ref, *out_refs):
    for step, out_ref in enumerate(out_refs):
        for kind in range(2):
            for head in range(out_ref.shape[1]):
                total = None
                for i, ref in enumerate((mine_ref, other_ref)):
                    for which in range(2):
                        row = places_ref[4 + 2 * i + which:5 + 2 * i + which]
                        term = jnp.where(row == step, ref[which, kind, head].astype(jnp.float32), 0.0)
                        total = term if total is None else total + term
                out_ref[kind, head] = total.astype(out_ref.dtype)


def merge_kernel(own_ref, *refs):
    *arrived, later_ref, _, out_ref, later_out = refs
    total = own_ref[...]
    for ref in arrived:
        total += ref[...].astype(jnp.float32)
    out_ref[...] = total.astype(out_ref.dtype)
    later_out[...] = later_ref[...]


def total_kernel(near_one, near_two, *refs):
    *blocks, dk_ref, dv_ref = refs
    half = near_one.shape[1]
    for kind, out_ref in enumerate((dk_ref, dv_ref)):
        for head in range(out_ref.shape[1]):
            total = near_one[kind, head] if head < half else near_two[kind, head - half]
            for ref in blocks:
                total += ref[kind, head].astype(jnp.float32)
            out_ref[:, head, :] = total


def body(queries, keys, values, grad_out, row_lse, row_delta, doc_ids, pairs):
    tokens, heads, head_dim = queries.shape
    kv_heads = keys.shape[1]
    grouped = QH // KVH
    factor = head_dim ** (-0.5)
    ring = lax.axis_size("ctx")
    subs = lax.axis_size("sub")
    rows = min(ROWS, tokens * grouped)
    cols = tokens * grouped
    span_shape = (2, kv_heads, tokens, head_dim)

    def crossed(array, bit):
        return lax.ppermute(array, "ctx", [(i, i ^ bit) for i in range(ring)])

    def swapped(array):
        return lax.ppermute(array, "sub", [(i, i ^ 1) for i in range(subs)])

    def in_hbm(*arrays):
        return [pltpu.with_memory_space_constraint(array, pltpu.HBM) for array in arrays]

    params = pltpu.CompilerParams(vmem_limit_bytes=VMEM_LIMIT)
    kv = pl.pallas_call(
        pack_kernel,
        in_specs=[HBM_SPEC] * 2,
        out_specs=VMEM_SPEC,
        out_shape=jax.ShapeDtypeStruct(span_shape, jnp.bfloat16),
        scratch_shapes=[pltpu.VMEM((2, *keys.shape), jnp.bfloat16), pltpu.SemaphoreType.DMA((2,))],
        compiler_params=params,
        name="pack",
    )(*in_hbm(keys, values))
    column = {0: kv}
    for place in sorted(range(1, ring), key=lambda place: -(place & -place)):
        low = place & -place
        column[place] = crossed(column[place ^ low], low)
    column = [column[place] for place in range(ring)]

    norm, term, docs, doc_col, places, held = pl.pallas_call(
        functools.partial(spread_kernel, grouped, ring, subs, rows),
        in_specs=[HBM_SPEC] * 6,
        out_specs=[VMEM_SPEC] * 6,
        out_shape=[
            jax.ShapeDtypeStruct((kv_heads, 1, cols), jnp.float32),
            jax.ShapeDtypeStruct((kv_heads, 1, cols), jnp.float32),
            jax.ShapeDtypeStruct((1, cols), jnp.float32),
            jax.ShapeDtypeStruct((tokens, tokens), jnp.float32),
            jax.ShapeDtypeStruct((8, head_dim), jnp.int32),
            jax.ShapeDtypeStruct((2, kv_heads, tokens, grouped, head_dim), jnp.bfloat16),
        ],
        scratch_shapes=[
            pltpu.VMEM((2, heads, tokens), jnp.float32),
            pltpu.VMEM((1, tokens), jnp.int32),
            pltpu.VMEM(pairs.shape[::-1], jnp.int32),
            pltpu.SemaphoreType.DMA((4,)),
            pltpu.SemaphoreType.DMA((kv_heads, cols // rows, 2)),
        ],
        compiler_params=params,
        name="spread",
    )(*in_hbm(row_lse.T, row_delta.T, doc_ids.reshape(1, tokens), pairs.T, queries, grad_out))

    work = 2 * tokens * tokens * heads * head_dim
    moved = 2 * queries.size * 2

    row_specs = [VMEM_SPEC] * 3
    half = (kv_heads + 1) // 2

    def local(first, count, after):
        return pl.pallas_call(
            functools.partial(local_kernel, factor, rows, first),
            in_specs=[VMEM_SPEC] + row_specs + [VMEM_SPEC] * 2 + [ANY_SPEC],
            out_specs=[VMEM_SPEC] * 2,
            out_shape=[
                jax.ShapeDtypeStruct((2, count, tokens, head_dim), jnp.float32),
                jax.ShapeDtypeStruct((tokens, count * grouped, head_dim), jnp.float32),
            ],
            compiler_params=params,
            cost_estimate=pl.CostEstimate(
                flops=5 * work * count // kv_heads, bytes_accessed=2 * moved * count // kv_heads, transcendentals=0
            ),
            name="local_block",
        )(kv, held, norm, term, docs, doc_col, after)

    near_kv, near_query = local(0, half, places)

    chosen = pl.pallas_call(
        choose_kernel,
        in_specs=[VMEM_SPEC] * (ring + 1) + [ANY_SPEC],
        out_specs=VMEM_SPEC,
        out_shape=jax.ShapeDtypeStruct((2, *span_shape), jnp.bfloat16),
        compiler_params=params,
        name="choose",
    )(places, *column, near_kv)
    other = swapped(chosen)
    far_kv = pl.pallas_call(
        functools.partial(listed_kernel, factor, rows),
        in_specs=[VMEM_SPEC] * (ring + 2) + row_specs,
        out_specs=VMEM_SPEC,
        out_shape=jax.ShapeDtypeStruct((2, *span_shape), jnp.bfloat16),
        compiler_params=params,
        cost_estimate=pl.CostEstimate(flops=8 * work, bytes_accessed=moved, transcendentals=0),
        name="listed_keys",
    )(places, *column, other, held, norm, term)
    other_kv = swapped(far_kv)
    sums = pl.pallas_call(
        combine_kernel,
        in_specs=[VMEM_SPEC] * 3,
        out_specs=[VMEM_SPEC] * ring,
        out_shape=[
            jax.ShapeDtypeStruct(span_shape, jnp.bfloat16 if place % 2 else jnp.float32) for place in range(ring)
        ],
        compiler_params=params,
        name="combine",
    )(places, far_kv, other_kv)

    def queries_of(count, ready, near_one, near_two, after):
        share = count - ready
        return pl.pallas_call(
            functools.partial(query_kernel, factor, rows, ready),
            in_specs=[VMEM_SPEC] * (2 + ring) + row_specs + [VMEM_SPEC] * 2 + [ANY_SPEC],
            out_specs=VMEM_SPEC,
            out_shape=jax.ShapeDtypeStruct((tokens, count * grouped, head_dim), jnp.float32),
            compiler_params=params,
            cost_estimate=pl.CostEstimate(
                flops=6 * work * share // kv_heads, bytes_accessed=3 * moved * share // kv_heads, transcendentals=0
            ),
            name="listed_queries",
        )(places, *column, other, held, norm, term, near_one, near_two, after)

    after, last, ready = sums[0], (near_kv, near_query), 0
    if half < kv_heads:
        last = local(half, kv_heads - half, after)
        near_query = queries_of(half, 0, near_query, last[1], last[0])
        after, ready = near_query, half
    arrived = {place: [] for place in range(ring)}
    later = sums[1]
    for place in sorted(range(2, ring), key=lambda place: (place & -place, -place)):
        low = place & -place
        block = sums[place]
        if arrived[place]:
            block, later = pl.pallas_call(
                merge_kernel,
                in_specs=[VMEM_SPEC] * (2 + len(arrived[place])) + [ANY_SPEC],
                out_specs=[VMEM_SPEC] * 2,
                out_shape=[jax.ShapeDtypeStruct(span_shape, jnp.bfloat16)] * 2,
                compiler_params=params,
                name="merge",
            )(block, *arrived[place], later, after)
            after = block
        arrived[place ^ low].append(crossed(block, low))
    arrived[0].append(crossed(later, 1))

    grad_queries = queries_of(kv_heads, ready, near_query, last[1], after)

    grad_keys, grad_values = pl.pallas_call(
        total_kernel,
        in_specs=[VMEM_SPEC] * (3 + len(arrived[0])),
        out_specs=[VMEM_SPEC] * 2,
        out_shape=[jax.ShapeDtypeStruct((tokens, kv_heads, head_dim), jnp.float32)] * 2,
        compiler_params=params,
        name="total",
    )(near_kv, last[0], sums[0], *arrived[0])
    return (grad_queries, grad_keys, grad_values)


def solution(mesh):
    return jax.shard_map(
        body,
        mesh=mesh,
        in_specs=(
            P(("groups", "ctx", "sub"), "head", None),
            P(("groups", "ctx", "sub"), "head", None),
            P(("groups", "ctx", "sub"), "head", None),
            P(("groups", "ctx", "sub"), "head", None),
            P(("groups", "ctx", "sub"), "head"),
            P(("groups", "ctx", "sub"), "head"),
            P(("groups", "ctx", "sub")),
            P("groups", None),
        ),
        out_specs=(
            P(("groups", "ctx", "sub"), "head", None),
            P(("groups", "ctx", "sub"), "head", None),
            P(("groups", "ctx", "sub"), "head", None),
        ),
        check_vma=False,
    )
```

```python
import functools

import jax
import jax.numpy as jnp
from jax import lax
from jax.experimental import pallas as pl
from jax.experimental.pallas import tpu as pltpu
from jax.sharding import PartitionSpec as P

QH = 64
KVH = 4
LOG2E = 1.4426950408889634
ROWS = 512
VMEM_LIMIT = 24 * 1024 * 1024

VMEM_SPEC = pl.BlockSpec(memory_space=pltpu.VMEM)
ANY_SPEC = pl.BlockSpec(memory_space=pl.ANY)
HBM_SPEC = pl.BlockSpec(memory_space=pltpu.HBM)


def rows_dot(left, right):
    return lax.dot_general(left, right, (((1,), (1,)), ((), ())), preferred_element_type=jnp.float32)


def tile_terms(key_blk, value_blk, query_blk, upstream, log_norm, row_terms, allowed, factor):
    scores = rows_dot(key_blk, query_blk)
    probs = jnp.exp2(scores * (factor * LOG2E) - log_norm)
    if allowed is not None:
        probs = jnp.where(allowed, probs, 0.0)
    grad_probs = rows_dot(value_blk, upstream)
    grad_scores = probs * (grad_probs - row_terms)
    return probs.astype(jnp.bfloat16), grad_scores.astype(jnp.bfloat16)


def chunks(tokens, grouped, rows):
    step = rows // grouped
    return [(i, slice(i * step, (i + 1) * step), slice(i * rows, (i + 1) * rows)) for i in range(tokens // step)]


def start_all(sources, targets, sems):
    copies = [pltpu.make_async_copy(source, target, sems.at[i]) for i, (source, target) in enumerate(zip(sources, targets))]
    for copy in copies:
        copy.start()
    return copies


def bring_rows(query_ref, up_ref, held_ref, sems, rows):
    _, count, tokens, grouped, _ = held_ref.shape
    copies = {}
    for head in range(count):
        heads = slice(head * grouped, (head + 1) * grouped)
        for i, toks, _ in chunks(tokens, grouped, rows):
            copies[head, i] = [
                pltpu.make_async_copy(ref.at[toks, heads], held_ref.at[kind, head, toks], sems.at[head, i, kind])
                for kind, ref in enumerate((query_ref, up_ref))
            ]
            for copy in copies[head, i]:
                copy.start()
    return copies


def row_blocks(held_ref, head, rows, copies=None):
    _, _, tokens, grouped, head_dim = held_ref.shape
    for i, toks, cols in chunks(tokens, grouped, rows):
        for copy in copies[head, i] if copies else ():
            copy.wait()
        yield toks, cols, *(held_ref[kind, head, toks].reshape(rows, head_dim) for kind in range(2))


def pack_kernel(key_ref, value_ref, *refs):
    *kv_refs, held_ref, sems = refs
    each = kv_refs[0].shape[1]
    copies = start_all((key_ref, value_ref), (held_ref.at[0], held_ref.at[1]), sems)
    for kind, copy in enumerate(copies):
        copy.wait()
        for head in range(held_ref.shape[2]):
            kv_refs[head // each][kind, head % each] = held_ref[kind, :, head, :]


def spread_kernel(
    grouped, ring, subs, norm_ref, term_ref, docs_ref, pairs_ref,
    norm_row_ref, term_row_ref, docs_row_ref, doc_col_ref, places_ref,
    held_ref, held_docs, held_pairs, sems,
):
    _, heads, tokens = held_ref.shape
    copies = start_all(
        (pairs_ref, docs_ref, norm_ref, term_ref), (held_pairs, held_docs, held_ref.at[0], held_ref.at[1]), sems
    )
    cols = tokens * grouped
    column = lax.broadcasted_iota(jnp.int32, (tokens, cols), 1)
    token = lax.broadcasted_iota(jnp.int32, (tokens, cols), 0)
    pick = jnp.where(token == column // grouped, 1.0, 0.0).astype(jnp.bfloat16)
    keep = lax.broadcasted_iota(jnp.int32, (grouped, cols), 0) == (
        lax.broadcasted_iota(jnp.int32, (grouped, cols), 1) % grouped
    )
    for copy in copies:
        copy.wait()

    ctx, sub = lax.axis_index("ctx"), lax.axis_index("sub")
    pairs = held_pairs[...]
    lane = lax.broadcasted_iota(jnp.int32, pairs.shape, 1)

    def listed_by(core):
        mask = lane == ctx * subs + core
        span = jnp.sum(jnp.where(mask, pairs, 0).astype(jnp.float32), axis=1, keepdims=True)
        span = jnp.broadcast_to(span, (2, places_ref.shape[1])).astype(jnp.int32)
        return span // subs, span % subs

    (mine, mine_sub), (other, other_sub) = listed_by(sub), listed_by(1 - sub)
    places_ref[0:2] = other ^ ctx
    places_ref[2:4] = jnp.where(mine_sub == sub, mine ^ ctx, ring)
    places_ref[4:6] = places_ref[2:4]
    places_ref[6:8] = jnp.where(other_sub == sub, other ^ ctx, ring)

    pieces = []
    for value in (held_ref[0] * LOG2E, held_ref[1]):
        for _ in range(3):
            piece = value.astype(jnp.bfloat16)
            value = value - piece.astype(jnp.float32)
            pieces.append(piece)
    docs = held_docs[...].astype(jnp.float32)
    pieces.append(jnp.broadcast_to(docs, (grouped, tokens)).astype(jnp.bfloat16))
    spread = jnp.dot(jnp.concatenate(pieces, axis=0), pick, preferred_element_type=jnp.float32)
    for i, out_ref in enumerate((norm_row_ref, term_row_ref)):
        base = 3 * i * heads
        value = spread[base:base + heads] + spread[base + heads:base + 2 * heads]
        value = value + spread[base + 2 * heads:base + 3 * heads]
        for head in range(out_ref.shape[0]):
            group = value[head * grouped:(head + 1) * grouped]
            out_ref[head] = jnp.sum(jnp.where(keep, group, 0.0), axis=0, keepdims=True)
    docs_row_ref[...] = spread[6 * heads:6 * heads + 1]
    doc_col_ref[...] = jnp.broadcast_to(docs, (tokens, tokens)).T


def pick_block(sources, row):
    chosen = sources[0].astype(jnp.float32)
    for step in range(1, len(sources)):
        chosen = jnp.where(row == step, sources[step].astype(jnp.float32), chosen)
    return chosen.astype(jnp.bfloat16)


def choose_kernel(places_ref, *refs):
    *column, _, _, out_ref = refs
    for which in range(2):
        row = places_ref[which:which + 1]
        for kind in range(2):
            for head in range(out_ref.shape[2]):
                out_ref[which, kind, head] = pick_block([ref[kind, head] for ref in column[::-1]], row)


def far_blocks(places_ref, column, other_ref, head):
    return [
        jnp.concatenate(
            [
                pick_block(
                    [ref[kind, head] for ref in column[::-1]] + [other_ref[which, kind, head]],
                    places_ref[2 + which:3 + which],
                )
                for which in range(2)
            ],
            axis=0,
        )
        for kind in range(2)
    ]


def local_kernel(factor, rows, *refs):
    *kv_refs, query_ref, up_ref, norm_ref, term_ref, docs_ref, doc_col_ref, dkv_ref, dq_ref, held_ref, sems = refs
    copies = bring_rows(query_ref, up_ref, held_ref, sems, rows)
    tokens, grouped, head_dim = held_ref.shape[2:]
    each = kv_refs[0].shape[1]
    doc_col = jnp.concatenate([doc_col_ref[...]] * (rows // tokens), axis=1)
    for head in range(held_ref.shape[1]):
        key_blk, value_blk = kv_refs[head // each][0, head % each], kv_refs[head // each][1, head % each]
        grad_key = jnp.zeros((tokens, head_dim), jnp.float32)
        grad_val = jnp.zeros((tokens, head_dim), jnp.float32)
        for toks, cols, query_blk, upstream in row_blocks(held_ref, head, rows, copies):
            position = lax.broadcasted_iota(jnp.int32, (tokens, rows), 1) // grouped + toks.start
            allowed = (lax.broadcasted_iota(jnp.int32, (tokens, rows), 0) <= position) & (
                doc_col == docs_ref[:, cols]
            )
            probs, grads = tile_terms(
                key_blk, value_blk, query_blk, upstream, norm_ref[head, :, cols], term_ref[head, :, cols],
                allowed, factor,
            )
            grad_val += jnp.dot(probs, upstream, preferred_element_type=jnp.float32)
            grad_key += jnp.dot(grads, query_blk, preferred_element_type=jnp.float32)
            grad_query = lax.dot_general(
                grads, key_blk, (((0,), (0,)), ((), ())), preferred_element_type=jnp.float32
            )
            dq_ref[toks, head * grouped:(head + 1) * grouped] = (grad_query * factor).reshape(
                rows // grouped, grouped, head_dim
            )
        dkv_ref[0, head] = grad_key * factor
        dkv_ref[1, head] = grad_val


def listed_kernel(factor, rows, first, places_ref, *refs):
    *column, other_ref, held_ref, norm_ref, term_ref, dkv_ref = refs
    tokens, grouped, head_dim = held_ref.shape[2:]
    for head in range(other_ref.shape[2]):
        key_blk, value_blk = far_blocks(places_ref, column, other_ref, head)
        grad_key = jnp.zeros((2 * tokens, head_dim), jnp.float32)
        grad_val = jnp.zeros((2 * tokens, head_dim), jnp.float32)
        for toks, cols, query_blk, upstream in row_blocks(held_ref, first + head, rows):
            probs, grads = tile_terms(
                key_blk, value_blk, query_blk, upstream,
                norm_ref[first + head, :, cols], term_ref[first + head, :, cols], None, factor,
            )
            grad_val += jnp.dot(probs, upstream, preferred_element_type=jnp.float32)
            grad_key += jnp.dot(grads, query_blk, preferred_element_type=jnp.float32)
        grad_key = (grad_key * factor).astype(dkv_ref.dtype)
        grad_val = grad_val.astype(dkv_ref.dtype)
        for which in range(2):
            dkv_ref[which, 0, head] = grad_key[which * tokens:(which + 1) * tokens]
            dkv_ref[which, 1, head] = grad_val[which * tokens:(which + 1) * tokens]


def query_kernel(factor, rows, parts, places_ref, *refs):
    *inputs, held_ref, norm_ref, term_ref, near_ref, _, dq_ref = refs
    tokens, grouped, head_dim = held_ref.shape[2:]
    size = len(inputs) // parts
    each = held_ref.shape[1] // parts
    for head in range(held_ref.shape[1]):
        *column, other_ref = inputs[head // each * size:(head // each + 1) * size]
        key_blk, value_blk = far_blocks(places_ref, column, other_ref, head % each)
        for toks, cols, query_blk, upstream in row_blocks(held_ref, head, rows):
            _, grads = tile_terms(
                key_blk, value_blk, query_blk, upstream, norm_ref[head, :, cols], term_ref[head, :, cols],
                None, factor,
            )
            grad_query = lax.dot_general(
                grads, key_blk, (((0,), (0,)), ((), ())), preferred_element_type=jnp.float32
            )
            heads = slice(head * grouped, (head + 1) * grouped)
            dq_ref[toks, heads] = near_ref[toks, heads] + (grad_query * factor).reshape(
                rows // grouped, grouped, head_dim
            )


def combine_kernel(places_ref, mine_ref, other_ref, *out_refs):
    for step, out_ref in enumerate(out_refs):
        for kind in range(2):
            for head in range(out_ref.shape[1]):
                total = None
                for i, ref in enumerate((mine_ref, other_ref)):
                    for which in range(2):
                        row = places_ref[4 + 2 * i + which:5 + 2 * i + which]
                        term = jnp.where(row == step, ref[which, kind, head].astype(jnp.float32), 0.0)
                        total = term if total is None else total + term
                out_ref[kind, head] = total.astype(out_ref.dtype)


def total_kernel(parts, near_ref, *refs):
    *blocks, dk_ref, dv_ref = refs
    count = len(blocks) // parts
    heads = dk_ref.shape[1]
    each = heads // parts
    for kind, out_ref in enumerate((dk_ref, dv_ref)):
        for head in range(heads):
            total = near_ref[kind, head]
            for ref in blocks[head // each * count:(head // each + 1) * count]:
                total += ref[kind, head % each].astype(jnp.float32)
            out_ref[:, head, :] = total


def body(queries, keys, values, grad_out, row_lse, row_delta, doc_ids, pairs):
    tokens, heads, head_dim = queries.shape
    kv_heads = keys.shape[1]
    grouped = QH // KVH
    factor = head_dim ** (-0.5)
    ring = lax.axis_size("ctx")
    subs = lax.axis_size("sub")
    rows = min(ROWS, tokens * grouped)
    cols = tokens * grouped
    parts = 1
    each = kv_heads // parts
    span_shape = (2, each, tokens, head_dim)

    def crossed(blocks):
        return [lax.ppermute(blocks[e], "ctx", [(i, i ^ e) for i in range(ring)]) for e in range(ring - 1, 0, -1)]

    def swapped(array):
        return lax.ppermute(array, "sub", [(i, i ^ 1) for i in range(subs)])

    def in_hbm(*arrays):
        return [pltpu.with_memory_space_constraint(array, pltpu.HBM) for array in arrays]

    params = pltpu.CompilerParams(vmem_limit_bytes=VMEM_LIMIT)
    kv = pl.pallas_call(
        pack_kernel,
        in_specs=[HBM_SPEC] * 2,
        out_specs=[VMEM_SPEC] * parts,
        out_shape=[jax.ShapeDtypeStruct(span_shape, jnp.bfloat16)] * parts,
        scratch_shapes=[pltpu.VMEM((2, *keys.shape), jnp.bfloat16), pltpu.SemaphoreType.DMA((2,))],
        compiler_params=params,
        name="pack",
    )(*in_hbm(keys, values))
    columns = [[*crossed([block] * ring), block] for block in kv]

    norm, term, docs, doc_col, places = pl.pallas_call(
        functools.partial(spread_kernel, grouped, ring, subs),
        in_specs=[HBM_SPEC] * 4,
        out_specs=[VMEM_SPEC] * 5,
        out_shape=[
            jax.ShapeDtypeStruct((kv_heads, 1, cols), jnp.float32),
            jax.ShapeDtypeStruct((kv_heads, 1, cols), jnp.float32),
            jax.ShapeDtypeStruct((1, cols), jnp.float32),
            jax.ShapeDtypeStruct((tokens, tokens), jnp.float32),
            jax.ShapeDtypeStruct((8, head_dim), jnp.int32),
        ],
        scratch_shapes=[
            pltpu.VMEM((2, heads, tokens), jnp.float32),
            pltpu.VMEM((1, tokens), jnp.int32),
            pltpu.VMEM(pairs.shape[::-1], jnp.int32),
            pltpu.SemaphoreType.DMA((4,)),
        ],
        compiler_params=params,
        name="spread",
    )(*in_hbm(row_lse.T, row_delta.T, doc_ids.reshape(1, tokens), pairs.T))

    work = 2 * tokens * tokens * heads * head_dim
    moved = 2 * queries.size * 2

    row_specs = [VMEM_SPEC] * 3
    near_kv, near_query, held = pl.pallas_call(
        functools.partial(local_kernel, factor, rows),
        in_specs=[VMEM_SPEC] * parts + [HBM_SPEC] * 2 + [VMEM_SPEC] * 4,
        out_specs=[VMEM_SPEC] * 3,
        out_shape=[
            jax.ShapeDtypeStruct((2, kv_heads, tokens, head_dim), jnp.float32),
            jax.ShapeDtypeStruct((tokens, heads, head_dim), jnp.float32),
            jax.ShapeDtypeStruct((2, kv_heads, tokens, grouped, head_dim), jnp.bfloat16),
        ],
        scratch_shapes=[pltpu.SemaphoreType.DMA((kv_heads, cols // rows, 2))],
        compiler_params=params,
        cost_estimate=pl.CostEstimate(flops=5 * work, bytes_accessed=2 * moved, transcendentals=0),
        name="local_block",
    )(*kv, *in_hbm(queries, grad_out), norm, term, docs, doc_col)

    inputs, sums = [], []
    after = near_kv
    for part, column in enumerate(columns):
        chosen = pl.pallas_call(
            choose_kernel,
            in_specs=[VMEM_SPEC] * (ring + 1) + [ANY_SPEC] * 2,
            out_specs=VMEM_SPEC,
            out_shape=jax.ShapeDtypeStruct((2, *span_shape), jnp.bfloat16),
            compiler_params=params,
            name="choose",
        )(places, *column, near_kv, after)
        other = swapped(chosen)
        inputs += [*column, other]
        far_kv = pl.pallas_call(
            functools.partial(listed_kernel, factor, rows, part * each),
            in_specs=[VMEM_SPEC] * (ring + 2) + row_specs,
            out_specs=VMEM_SPEC,
            out_shape=jax.ShapeDtypeStruct((2, *span_shape), jnp.bfloat16),
            compiler_params=params,
            cost_estimate=pl.CostEstimate(flops=8 * work // parts, bytes_accessed=moved // parts, transcendentals=0),
            name="listed_keys",
        )(places, *column, other, held, norm, term)
        other_kv = swapped(far_kv)
        blocks = pl.pallas_call(
            combine_kernel,
            in_specs=[VMEM_SPEC] * 3,
            out_specs=[VMEM_SPEC] * ring,
            out_shape=[jax.ShapeDtypeStruct(span_shape, jnp.float32)]
            + [jax.ShapeDtypeStruct(span_shape, jnp.bfloat16)] * (ring - 1),
            compiler_params=params,
            name="combine",
        )(places, far_kv, other_kv)
        sums += [blocks[0], *crossed(blocks)]
        after = blocks[0]

    grad_queries = pl.pallas_call(
        functools.partial(query_kernel, factor, rows, parts),
        in_specs=[VMEM_SPEC] * (1 + len(inputs)) + row_specs + [VMEM_SPEC, ANY_SPEC],
        out_specs=VMEM_SPEC,
        out_shape=jax.ShapeDtypeStruct((tokens, heads, head_dim), jnp.float32),
        compiler_params=params,
        cost_estimate=pl.CostEstimate(flops=6 * work, bytes_accessed=3 * moved, transcendentals=0),
        name="listed_queries",
    )(places, *inputs, held, norm, term, near_query, after)

    grad_keys, grad_values = pl.pallas_call(
        functools.partial(total_kernel, parts),
        in_specs=[VMEM_SPEC] * (parts * ring + 1),
        out_specs=[VMEM_SPEC] * 2,
        out_shape=[jax.ShapeDtypeStruct((tokens, kv_heads, head_dim), jnp.float32)] * 2,
        compiler_params=params,
        name="total",
    )(near_kv, *sums)
    return (grad_queries, grad_keys, grad_values)


def solution(mesh):
    return jax.shard_map(
        body,
        mesh=mesh,
        in_specs=(
            P(("groups", "ctx", "sub"), "head", None),
            P(("groups", "ctx", "sub"), "head", None),
            P(("groups", "ctx", "sub"), "head", None),
            P(("groups", "ctx", "sub"), "head", None),
            P(("groups", "ctx", "sub"), "head"),
            P(("groups", "ctx", "sub"), "head"),
            P(("groups", "ctx", "sub")),
            P("groups", None),
        ),
        out_specs=(
            P(("groups", "ctx", "sub"), "head", None),
            P(("groups", "ctx", "sub"), "head", None),
            P(("groups", "ctx", "sub"), "head", None),
        ),
        check_vma=False,
    )
```

```python
import functools

import jax
import jax.numpy as jnp
from jax import lax
from jax.experimental import pallas as pl
from jax.experimental.pallas import tpu as pltpu
from jax.sharding import PartitionSpec as P

QH = 64
KVH = 4
LOG2E = 1.4426950408889634
ROWS = 512
VMEM_LIMIT = 24 * 1024 * 1024

VMEM_SPEC = pl.BlockSpec(memory_space=pltpu.VMEM)
ANY_SPEC = pl.BlockSpec(memory_space=pl.ANY)
HBM_SPEC = pl.BlockSpec(memory_space=pltpu.HBM)


def rows_dot(left, right):
    return lax.dot_general(left, right, (((1,), (1,)), ((), ())), preferred_element_type=jnp.float32)


def tile_terms(key_blk, value_blk, query_blk, upstream, log_norm, row_terms, allowed, factor):
    scores = rows_dot(key_blk, query_blk)
    probs = jnp.exp2(scores * (factor * LOG2E) - log_norm)
    if allowed is not None:
        probs = jnp.where(allowed, probs, 0.0)
    grad_probs = rows_dot(value_blk, upstream)
    grad_scores = probs * (grad_probs - row_terms)
    return probs.astype(jnp.bfloat16), grad_scores.astype(jnp.bfloat16)


def chunks(tokens, grouped, rows):
    step = rows // grouped
    return [(i, slice(i * step, (i + 1) * step), slice(i * rows, (i + 1) * rows)) for i in range(tokens // step)]


def send_order(ring):
    return sorted(range(ring), key=lambda e: (-e.bit_length(), e))


def by_place(column):
    order = send_order(len(column))
    return [column[order.index(e)] for e in range(len(column))]


def start_all(sources, targets, sems):
    copies = [pltpu.make_async_copy(source, target, sems.at[i]) for i, (source, target) in enumerate(zip(sources, targets))]
    for copy in copies:
        copy.start()
    return copies


def bring_rows(query_ref, up_ref, held_ref, sems, rows):
    _, count, tokens, grouped, _ = held_ref.shape
    copies = {}
    for head in range(count):
        heads = slice(head * grouped, (head + 1) * grouped)
        for i, toks, _ in chunks(tokens, grouped, rows):
            copies[head, i] = [
                pltpu.make_async_copy(ref.at[toks, heads], held_ref.at[kind, head, toks], sems.at[head, i, kind])
                for kind, ref in enumerate((query_ref, up_ref))
            ]
            for copy in copies[head, i]:
                copy.start()
    return copies


def row_blocks(held_ref, head, rows, copies=None):
    _, _, tokens, grouped, head_dim = held_ref.shape
    for i, toks, cols in chunks(tokens, grouped, rows):
        for copy in copies[head, i] if copies else ():
            copy.wait()
        yield toks, cols, *(held_ref[kind, head, toks].reshape(rows, head_dim) for kind in range(2))


def pack_kernel(key_ref, value_ref, *refs):
    *kv_refs, held_ref, sems = refs
    each = kv_refs[0].shape[1]
    copies = start_all((key_ref, value_ref), (held_ref.at[0], held_ref.at[1]), sems)
    for kind, copy in enumerate(copies):
        copy.wait()
        for head in range(held_ref.shape[2]):
            kv_refs[head // each][kind, head % each] = held_ref[kind, :, head, :]


def spread_kernel(
    grouped, ring, subs, norm_ref, term_ref, docs_ref, pairs_ref,
    norm_row_ref, term_row_ref, docs_row_ref, doc_col_ref, places_ref,
    held_ref, held_docs, held_pairs, sems,
):
    _, heads, tokens = held_ref.shape
    copies = start_all(
        (pairs_ref, docs_ref, norm_ref, term_ref), (held_pairs, held_docs, held_ref.at[0], held_ref.at[1]), sems
    )
    cols = tokens * grouped
    column = lax.broadcasted_iota(jnp.int32, (tokens, cols), 1)
    token = lax.broadcasted_iota(jnp.int32, (tokens, cols), 0)
    pick = jnp.where(token == column // grouped, 1.0, 0.0).astype(jnp.bfloat16)
    keep = lax.broadcasted_iota(jnp.int32, (grouped, cols), 0) == (
        lax.broadcasted_iota(jnp.int32, (grouped, cols), 1) % grouped
    )
    for copy in copies:
        copy.wait()

    ctx, sub = lax.axis_index("ctx"), lax.axis_index("sub")
    pairs = held_pairs[...]
    lane = lax.broadcasted_iota(jnp.int32, pairs.shape, 1)

    def listed_by(core):
        mask = lane == ctx * subs + core
        span = jnp.sum(jnp.where(mask, pairs, 0).astype(jnp.float32), axis=1, keepdims=True)
        span = jnp.broadcast_to(span, (2, places_ref.shape[1])).astype(jnp.int32)
        return span // subs, span % subs

    (mine, mine_sub), (other, other_sub) = listed_by(sub), listed_by(1 - sub)
    places_ref[0:2] = other ^ ctx
    places_ref[2:4] = jnp.where(mine_sub == sub, mine ^ ctx, ring)
    places_ref[4:6] = places_ref[2:4]
    places_ref[6:8] = jnp.where(other_sub == sub, other ^ ctx, ring)

    pieces = []
    for value in (held_ref[0] * LOG2E, held_ref[1]):
        for _ in range(3):
            piece = value.astype(jnp.bfloat16)
            value = value - piece.astype(jnp.float32)
            pieces.append(piece)
    docs = held_docs[...].astype(jnp.float32)
    pieces.append(jnp.broadcast_to(docs, (grouped, tokens)).astype(jnp.bfloat16))
    spread = jnp.dot(jnp.concatenate(pieces, axis=0), pick, preferred_element_type=jnp.float32)
    for i, out_ref in enumerate((norm_row_ref, term_row_ref)):
        base = 3 * i * heads
        value = spread[base:base + heads] + spread[base + heads:base + 2 * heads]
        value = value + spread[base + 2 * heads:base + 3 * heads]
        for head in range(out_ref.shape[0]):
            group = value[head * grouped:(head + 1) * grouped]
            out_ref[head] = jnp.sum(jnp.where(keep, group, 0.0), axis=0, keepdims=True)
    docs_row_ref[...] = spread[6 * heads:6 * heads + 1]
    doc_col_ref[...] = jnp.broadcast_to(docs, (tokens, tokens)).T


def pick_block(sources, row):
    chosen = sources[0].astype(jnp.float32)
    for step in range(1, len(sources)):
        chosen = jnp.where(row == step, sources[step].astype(jnp.float32), chosen)
    return chosen.astype(jnp.bfloat16)


def choose_kernel(places_ref, *refs):
    *column, _, _, out_ref = refs
    for which in range(2):
        row = places_ref[which:which + 1]
        for kind in range(2):
            for head in range(out_ref.shape[2]):
                out_ref[which, kind, head] = pick_block([ref[kind, head] for ref in by_place(column)], row)


def far_blocks(places_ref, column, other_ref, head):
    return [
        jnp.concatenate(
            [
                pick_block(
                    [ref[kind, head] for ref in by_place(column)] + [other_ref[which, kind, head]],
                    places_ref[2 + which:3 + which],
                )
                for which in range(2)
            ],
            axis=0,
        )
        for kind in range(2)
    ]


def local_kernel(factor, rows, *refs):
    *kv_refs, query_ref, up_ref, norm_ref, term_ref, docs_ref, doc_col_ref, dkv_ref, dq_ref, held_ref, sems = refs
    copies = bring_rows(query_ref, up_ref, held_ref, sems, rows)
    tokens, grouped, head_dim = held_ref.shape[2:]
    each = kv_refs[0].shape[1]
    doc_col = jnp.concatenate([doc_col_ref[...]] * (rows // tokens), axis=1)
    for head in range(held_ref.shape[1]):
        key_blk, value_blk = kv_refs[head // each][0, head % each], kv_refs[head // each][1, head % each]
        grad_key = jnp.zeros((tokens, head_dim), jnp.float32)
        grad_val = jnp.zeros((tokens, head_dim), jnp.float32)
        for toks, cols, query_blk, upstream in row_blocks(held_ref, head, rows, copies):
            position = lax.broadcasted_iota(jnp.int32, (tokens, rows), 1) // grouped + toks.start
            allowed = (lax.broadcasted_iota(jnp.int32, (tokens, rows), 0) <= position) & (
                doc_col == docs_ref[:, cols]
            )
            probs, grads = tile_terms(
                key_blk, value_blk, query_blk, upstream, norm_ref[head, :, cols], term_ref[head, :, cols],
                allowed, factor,
            )
            grad_val += jnp.dot(probs, upstream, preferred_element_type=jnp.float32)
            grad_key += jnp.dot(grads, query_blk, preferred_element_type=jnp.float32)
            grad_query = lax.dot_general(
                grads, key_blk, (((0,), (0,)), ((), ())), preferred_element_type=jnp.float32
            )
            dq_ref[toks, head * grouped:(head + 1) * grouped] = (grad_query * factor).reshape(
                rows // grouped, grouped, head_dim
            )
        dkv_ref[0, head] = grad_key * factor
        dkv_ref[1, head] = grad_val


def listed_kernel(factor, rows, first, places_ref, *refs):
    *column, other_ref, held_ref, norm_ref, term_ref, dkv_ref = refs
    tokens, grouped, head_dim = held_ref.shape[2:]
    for head in range(other_ref.shape[2]):
        key_blk, value_blk = far_blocks(places_ref, column, other_ref, head)
        grad_key = jnp.zeros((2 * tokens, head_dim), jnp.float32)
        grad_val = jnp.zeros((2 * tokens, head_dim), jnp.float32)
        for toks, cols, query_blk, upstream in row_blocks(held_ref, first + head, rows):
            probs, grads = tile_terms(
                key_blk, value_blk, query_blk, upstream,
                norm_ref[first + head, :, cols], term_ref[first + head, :, cols], None, factor,
            )
            grad_val += jnp.dot(probs, upstream, preferred_element_type=jnp.float32)
            grad_key += jnp.dot(grads, query_blk, preferred_element_type=jnp.float32)
        grad_key = (grad_key * factor).astype(dkv_ref.dtype)
        grad_val = grad_val.astype(dkv_ref.dtype)
        for which in range(2):
            dkv_ref[which, 0, head] = grad_key[which * tokens:(which + 1) * tokens]
            dkv_ref[which, 1, head] = grad_val[which * tokens:(which + 1) * tokens]


def query_kernel(factor, rows, parts, places_ref, *refs):
    *inputs, held_ref, norm_ref, term_ref, near_ref, _, dq_ref = refs
    tokens, grouped, head_dim = held_ref.shape[2:]
    size = len(inputs) // parts
    each = held_ref.shape[1] // parts
    for head in range(held_ref.shape[1]):
        *column, other_ref = inputs[head // each * size:(head // each + 1) * size]
        key_blk, value_blk = far_blocks(places_ref, column, other_ref, head % each)
        for toks, cols, query_blk, upstream in row_blocks(held_ref, head, rows):
            _, grads = tile_terms(
                key_blk, value_blk, query_blk, upstream, norm_ref[head, :, cols], term_ref[head, :, cols],
                None, factor,
            )
            grad_query = lax.dot_general(
                grads, key_blk, (((0,), (0,)), ((), ())), preferred_element_type=jnp.float32
            )
            heads = slice(head * grouped, (head + 1) * grouped)
            dq_ref[toks, heads] = near_ref[toks, heads] + (grad_query * factor).reshape(
                rows // grouped, grouped, head_dim
            )


def combine_kernel(places_ref, mine_ref, other_ref, *out_refs):
    for step, out_ref in enumerate(out_refs):
        for kind in range(2):
            for head in range(out_ref.shape[1]):
                total = None
                for i, ref in enumerate((mine_ref, other_ref)):
                    for which in range(2):
                        row = places_ref[4 + 2 * i + which:5 + 2 * i + which]
                        term = jnp.where(row == step, ref[which, kind, head].astype(jnp.float32), 0.0)
                        total = term if total is None else total + term
                out_ref[kind, head] = total.astype(out_ref.dtype)


def total_kernel(parts, near_ref, *refs):
    *blocks, dk_ref, dv_ref = refs
    count = len(blocks) // parts
    heads = dk_ref.shape[1]
    each = heads // parts
    for kind, out_ref in enumerate((dk_ref, dv_ref)):
        for head in range(heads):
            total = near_ref[kind, head]
            for ref in blocks[head // each * count:(head // each + 1) * count]:
                total += ref[kind, head % each].astype(jnp.float32)
            out_ref[:, head, :] = total


def body(queries, keys, values, grad_out, row_lse, row_delta, doc_ids, pairs):
    tokens, heads, head_dim = queries.shape
    kv_heads = keys.shape[1]
    grouped = QH // KVH
    factor = head_dim ** (-0.5)
    ring = lax.axis_size("ctx")
    subs = lax.axis_size("sub")
    rows = min(ROWS, tokens * grouped)
    cols = tokens * grouped
    parts = 1
    each = kv_heads // parts
    span_shape = (2, each, tokens, head_dim)

    def crossed(blocks):
        return [lax.ppermute(blocks[e], "ctx", [(i, i ^ e) for i in range(ring)]) for e in send_order(ring)[:-1]]

    def swapped(array):
        return lax.ppermute(array, "sub", [(i, i ^ 1) for i in range(subs)])

    def in_hbm(*arrays):
        return [pltpu.with_memory_space_constraint(array, pltpu.HBM) for array in arrays]

    params = pltpu.CompilerParams(vmem_limit_bytes=VMEM_LIMIT)
    kv = pl.pallas_call(
        pack_kernel,
        in_specs=[HBM_SPEC] * 2,
        out_specs=[VMEM_SPEC] * parts,
        out_shape=[jax.ShapeDtypeStruct(span_shape, jnp.bfloat16)] * parts,
        scratch_shapes=[pltpu.VMEM((2, *keys.shape), jnp.bfloat16), pltpu.SemaphoreType.DMA((2,))],
        compiler_params=params,
        name="pack",
    )(*in_hbm(keys, values))
    columns = [[*crossed([block] * ring), block] for block in kv]

    norm, term, docs, doc_col, places = pl.pallas_call(
        functools.partial(spread_kernel, grouped, ring, subs),
        in_specs=[HBM_SPEC] * 4,
        out_specs=[VMEM_SPEC] * 5,
        out_shape=[
            jax.ShapeDtypeStruct((kv_heads, 1, cols), jnp.float32),
            jax.ShapeDtypeStruct((kv_heads, 1, cols), jnp.float32),
            jax.ShapeDtypeStruct((1, cols), jnp.float32),
            jax.ShapeDtypeStruct((tokens, tokens), jnp.float32),
            jax.ShapeDtypeStruct((8, head_dim), jnp.int32),
        ],
        scratch_shapes=[
            pltpu.VMEM((2, heads, tokens), jnp.float32),
            pltpu.VMEM((1, tokens), jnp.int32),
            pltpu.VMEM(pairs.shape[::-1], jnp.int32),
            pltpu.SemaphoreType.DMA((4,)),
        ],
        compiler_params=params,
        name="spread",
    )(*in_hbm(row_lse.T, row_delta.T, doc_ids.reshape(1, tokens), pairs.T))

    work = 2 * tokens * tokens * heads * head_dim
    moved = 2 * queries.size * 2

    row_specs = [VMEM_SPEC] * 3
    near_kv, near_query, held = pl.pallas_call(
        functools.partial(local_kernel, factor, rows),
        in_specs=[VMEM_SPEC] * parts + [HBM_SPEC] * 2 + [VMEM_SPEC] * 4,
        out_specs=[VMEM_SPEC] * 3,
        out_shape=[
            jax.ShapeDtypeStruct((2, kv_heads, tokens, head_dim), jnp.float32),
            jax.ShapeDtypeStruct((tokens, heads, head_dim), jnp.float32),
            jax.ShapeDtypeStruct((2, kv_heads, tokens, grouped, head_dim), jnp.bfloat16),
        ],
        scratch_shapes=[pltpu.SemaphoreType.DMA((kv_heads, cols // rows, 2))],
        compiler_params=params,
        cost_estimate=pl.CostEstimate(flops=5 * work, bytes_accessed=2 * moved, transcendentals=0),
        name="local_block",
    )(*kv, *in_hbm(queries, grad_out), norm, term, docs, doc_col)

    inputs, sums = [], []
    after = near_kv
    for part, column in enumerate(columns):
        chosen = pl.pallas_call(
            choose_kernel,
            in_specs=[VMEM_SPEC] * (ring + 1) + [ANY_SPEC] * 2,
            out_specs=VMEM_SPEC,
            out_shape=jax.ShapeDtypeStruct((2, *span_shape), jnp.bfloat16),
            compiler_params=params,
            name="choose",
        )(places, *column, near_kv, after)
        other = swapped(chosen)
        inputs += [*column, other]
        far_kv = pl.pallas_call(
            functools.partial(listed_kernel, factor, rows, part * each),
            in_specs=[VMEM_SPEC] * (ring + 2) + row_specs,
            out_specs=VMEM_SPEC,
            out_shape=jax.ShapeDtypeStruct((2, *span_shape), jnp.bfloat16),
            compiler_params=params,
            cost_estimate=pl.CostEstimate(flops=8 * work // parts, bytes_accessed=moved // parts, transcendentals=0),
            name="listed_keys",
        )(places, *column, other, held, norm, term)
        other_kv = swapped(far_kv)
        blocks = pl.pallas_call(
            combine_kernel,
            in_specs=[VMEM_SPEC] * 3,
            out_specs=[VMEM_SPEC] * ring,
            out_shape=[jax.ShapeDtypeStruct(span_shape, jnp.float32)]
            + [jax.ShapeDtypeStruct(span_shape, jnp.bfloat16)] * (ring - 1),
            compiler_params=params,
            name="combine",
        )(places, far_kv, other_kv)
        sums += [blocks[0], *crossed(blocks)]
        after = blocks[0]

    grad_queries = pl.pallas_call(
        functools.partial(query_kernel, factor, rows, parts),
        in_specs=[VMEM_SPEC] * (1 + len(inputs)) + row_specs + [VMEM_SPEC, ANY_SPEC],
        out_specs=VMEM_SPEC,
        out_shape=jax.ShapeDtypeStruct((tokens, heads, head_dim), jnp.float32),
        compiler_params=params,
        cost_estimate=pl.CostEstimate(flops=6 * work, bytes_accessed=3 * moved, transcendentals=0),
        name="listed_queries",
    )(places, *inputs, held, norm, term, near_query, after)

    grad_keys, grad_values = pl.pallas_call(
        functools.partial(total_kernel, parts),
        in_specs=[VMEM_SPEC] * (parts * ring + 1),
        out_specs=[VMEM_SPEC] * 2,
        out_shape=[jax.ShapeDtypeStruct((tokens, kv_heads, head_dim), jnp.float32)] * 2,
        compiler_params=params,
        name="total",
    )(near_kv, *sums)
    return (grad_queries, grad_keys, grad_values)


def solution(mesh):
    return jax.shard_map(
        body,
        mesh=mesh,
        in_specs=(
            P(("groups", "ctx", "sub"), "head", None),
            P(("groups", "ctx", "sub"), "head", None),
            P(("groups", "ctx", "sub"), "head", None),
            P(("groups", "ctx", "sub"), "head", None),
            P(("groups", "ctx", "sub"), "head"),
            P(("groups", "ctx", "sub"), "head"),
            P(("groups", "ctx", "sub")),
            P("groups", None),
        ),
        out_specs=(
            P(("groups", "ctx", "sub"), "head", None),
            P(("groups", "ctx", "sub"), "head", None),
            P(("groups", "ctx", "sub"), "head", None),
        ),
        check_vma=False,
    )
```

```python
import functools

import jax
import jax.numpy as jnp
from jax import lax
from jax.experimental import pallas as pl
from jax.experimental.pallas import tpu as pltpu
from jax.sharding import PartitionSpec as P

QH = 64
KVH = 4
LOG2E = 1.4426950408889634
ROWS = 512
VMEM_LIMIT = 24 * 1024 * 1024

VMEM_SPEC = pl.BlockSpec(memory_space=pltpu.VMEM)
ANY_SPEC = pl.BlockSpec(memory_space=pl.ANY)
HBM_SPEC = pl.BlockSpec(memory_space=pltpu.HBM)


def rows_dot(left, right):
    return lax.dot_general(left, right, (((1,), (1,)), ((), ())), preferred_element_type=jnp.float32)


def tile_terms(key_blk, value_blk, query_blk, upstream, log_norm, row_terms, allowed, factor):
    scores = rows_dot(key_blk, query_blk)
    probs = jnp.exp2(scores * (factor * LOG2E) - log_norm)
    if allowed is not None:
        probs = jnp.where(allowed, probs, 0.0)
    grad_probs = rows_dot(value_blk, upstream)
    grad_scores = probs * (grad_probs - row_terms)
    return probs.astype(jnp.bfloat16), grad_scores.astype(jnp.bfloat16)


def chunks(tokens, grouped, rows):
    step = rows // grouped
    return [(i, slice(i * step, (i + 1) * step), slice(i * rows, (i + 1) * rows)) for i in range(tokens // step)]


def send_order(ring):
    return sorted(range(ring), key=lambda e: (-e.bit_length(), e))


def by_place(column):
    order = send_order(len(column))
    return [column[order.index(e)] for e in range(len(column))]


def start_all(sources, targets, sems):
    copies = [pltpu.make_async_copy(source, target, sems.at[i]) for i, (source, target) in enumerate(zip(sources, targets))]
    for copy in copies:
        copy.start()
    return copies


def bring_rows(query_ref, up_ref, held_ref, sems, rows):
    _, count, tokens, grouped, _ = held_ref.shape
    copies = {}
    for head in range(count):
        heads = slice(head * grouped, (head + 1) * grouped)
        for i, toks, _ in chunks(tokens, grouped, rows):
            copies[head, i] = [
                pltpu.make_async_copy(ref.at[toks, heads], held_ref.at[kind, head, toks], sems.at[head, i, kind])
                for kind, ref in enumerate((query_ref, up_ref))
            ]
            for copy in copies[head, i]:
                copy.start()
    return copies


def row_blocks(held_ref, head, rows, copies=None):
    _, _, tokens, grouped, head_dim = held_ref.shape
    for i, toks, cols in chunks(tokens, grouped, rows):
        for copy in copies[head, i] if copies else ():
            copy.wait()
        yield toks, cols, *(held_ref[kind, head, toks].reshape(rows, head_dim) for kind in range(2))


def pack_kernel(key_ref, value_ref, *refs):
    *kv_refs, held_ref, sems = refs
    each = kv_refs[0].shape[1]
    copies = start_all((key_ref, value_ref), (held_ref.at[0], held_ref.at[1]), sems)
    for kind, copy in enumerate(copies):
        copy.wait()
        for head in range(held_ref.shape[2]):
            kv_refs[head // each][kind, head % each] = held_ref[kind, :, head, :]


def spread_kernel(
    grouped, ring, subs, norm_ref, term_ref, docs_ref, pairs_ref,
    norm_row_ref, term_row_ref, docs_row_ref, doc_col_ref, places_ref,
    held_ref, held_docs, held_pairs, sems,
):
    _, heads, tokens = held_ref.shape
    copies = start_all(
        (pairs_ref, docs_ref, norm_ref, term_ref), (held_pairs, held_docs, held_ref.at[0], held_ref.at[1]), sems
    )
    cols = tokens * grouped
    column = lax.broadcasted_iota(jnp.int32, (tokens, cols), 1)
    token = lax.broadcasted_iota(jnp.int32, (tokens, cols), 0)
    pick = jnp.where(token == column // grouped, 1.0, 0.0).astype(jnp.bfloat16)
    keep = lax.broadcasted_iota(jnp.int32, (grouped, cols), 0) == (
        lax.broadcasted_iota(jnp.int32, (grouped, cols), 1) % grouped
    )
    for copy in copies:
        copy.wait()

    ctx, sub = lax.axis_index("ctx"), lax.axis_index("sub")
    pairs = held_pairs[...]
    lane = lax.broadcasted_iota(jnp.int32, pairs.shape, 1)

    def listed_by(core):
        mask = lane == ctx * subs + core
        span = jnp.sum(jnp.where(mask, pairs, 0).astype(jnp.float32), axis=1, keepdims=True)
        span = jnp.broadcast_to(span, (2, places_ref.shape[1])).astype(jnp.int32)
        return span // subs, span % subs

    (mine, mine_sub), (other, other_sub) = listed_by(sub), listed_by(1 - sub)
    places_ref[0:2] = other ^ ctx
    places_ref[2:4] = jnp.where(mine_sub == sub, mine ^ ctx, ring)
    places_ref[4:6] = places_ref[2:4]
    places_ref[6:8] = jnp.where(other_sub == sub, other ^ ctx, ring)

    pieces = []
    for value in (held_ref[0] * LOG2E, held_ref[1]):
        for _ in range(3):
            piece = value.astype(jnp.bfloat16)
            value = value - piece.astype(jnp.float32)
            pieces.append(piece)
    docs = held_docs[...].astype(jnp.float32)
    pieces.append(jnp.broadcast_to(docs, (grouped, tokens)).astype(jnp.bfloat16))
    spread = jnp.dot(jnp.concatenate(pieces, axis=0), pick, preferred_element_type=jnp.float32)
    for i, out_ref in enumerate((norm_row_ref, term_row_ref)):
        base = 3 * i * heads
        value = spread[base:base + heads] + spread[base + heads:base + 2 * heads]
        value = value + spread[base + 2 * heads:base + 3 * heads]
        for head in range(out_ref.shape[0]):
            group = value[head * grouped:(head + 1) * grouped]
            out_ref[head] = jnp.sum(jnp.where(keep, group, 0.0), axis=0, keepdims=True)
    docs_row_ref[...] = spread[6 * heads:6 * heads + 1]
    doc_col_ref[...] = jnp.broadcast_to(docs, (tokens, tokens)).T


def pick_block(sources, row):
    chosen = sources[0].astype(jnp.float32)
    for step in range(1, len(sources)):
        chosen = jnp.where(row == step, sources[step].astype(jnp.float32), chosen)
    return chosen.astype(jnp.bfloat16)


def choose_kernel(places_ref, *refs):
    *column, _, _, out_ref = refs
    for which in range(2):
        row = places_ref[which:which + 1]
        for kind in range(2):
            for head in range(out_ref.shape[2]):
                out_ref[which, kind, head] = pick_block([ref[kind, head] for ref in by_place(column)], row)


def far_blocks(places_ref, column, other_ref, head):
    return [
        jnp.concatenate(
            [
                pick_block(
                    [ref[kind, head] for ref in by_place(column)] + [other_ref[which, kind, head]],
                    places_ref[2 + which:3 + which],
                )
                for which in range(2)
            ],
            axis=0,
        )
        for kind in range(2)
    ]


def local_kernel(factor, rows, *refs):
    *kv_refs, query_ref, up_ref, norm_ref, term_ref, docs_ref, doc_col_ref, dkv_ref, dq_ref, held_ref, sems = refs
    copies = bring_rows(query_ref, up_ref, held_ref, sems, rows)
    tokens, grouped, head_dim = held_ref.shape[2:]
    each = kv_refs[0].shape[1]
    doc_col = jnp.concatenate([doc_col_ref[...]] * (rows // tokens), axis=1)
    for head in range(held_ref.shape[1]):
        key_blk, value_blk = kv_refs[head // each][0, head % each], kv_refs[head // each][1, head % each]
        grad_key = jnp.zeros((tokens, head_dim), jnp.float32)
        grad_val = jnp.zeros((tokens, head_dim), jnp.float32)
        for toks, cols, query_blk, upstream in row_blocks(held_ref, head, rows, copies):
            position = lax.broadcasted_iota(jnp.int32, (tokens, rows), 1) // grouped + toks.start
            allowed = (lax.broadcasted_iota(jnp.int32, (tokens, rows), 0) <= position) & (
                doc_col == docs_ref[:, cols]
            )
            probs, grads = tile_terms(
                key_blk, value_blk, query_blk, upstream, norm_ref[head, :, cols], term_ref[head, :, cols],
                allowed, factor,
            )
            grad_val += jnp.dot(probs, upstream, preferred_element_type=jnp.float32)
            grad_key += jnp.dot(grads, query_blk, preferred_element_type=jnp.float32)
            grad_query = lax.dot_general(
                grads, key_blk, (((0,), (0,)), ((), ())), preferred_element_type=jnp.float32
            )
            dq_ref[toks, head * grouped:(head + 1) * grouped] = (grad_query * factor).reshape(
                rows // grouped, grouped, head_dim
            )
        dkv_ref[0, head] = grad_key * factor
        dkv_ref[1, head] = grad_val


def listed_kernel(factor, rows, first, places_ref, *refs):
    *column, other_ref, held_ref, norm_ref, term_ref, dkv_ref = refs
    tokens, grouped, head_dim = held_ref.shape[2:]
    for head in range(other_ref.shape[2]):
        key_blk, value_blk = far_blocks(places_ref, column, other_ref, head)
        grad_key = jnp.zeros((2 * tokens, head_dim), jnp.float32)
        grad_val = jnp.zeros((2 * tokens, head_dim), jnp.float32)
        for toks, cols, query_blk, upstream in row_blocks(held_ref, first + head, rows):
            probs, grads = tile_terms(
                key_blk, value_blk, query_blk, upstream,
                norm_ref[first + head, :, cols], term_ref[first + head, :, cols], None, factor,
            )
            grad_val += jnp.dot(probs, upstream, preferred_element_type=jnp.float32)
            grad_key += jnp.dot(grads, query_blk, preferred_element_type=jnp.float32)
        grad_key = (grad_key * factor).astype(dkv_ref.dtype)
        grad_val = grad_val.astype(dkv_ref.dtype)
        for which in range(2):
            dkv_ref[which, 0, head] = grad_key[which * tokens:(which + 1) * tokens]
            dkv_ref[which, 1, head] = grad_val[which * tokens:(which + 1) * tokens]


def query_kernel(factor, rows, parts, places_ref, *refs):
    *inputs, held_ref, norm_ref, term_ref, near_ref, _, dq_ref = refs
    tokens, grouped, head_dim = held_ref.shape[2:]
    size = len(inputs) // parts
    each = held_ref.shape[1] // parts
    for head in range(held_ref.shape[1]):
        *column, other_ref = inputs[head // each * size:(head // each + 1) * size]
        key_blk, value_blk = far_blocks(places_ref, column, other_ref, head % each)
        for toks, cols, query_blk, upstream in row_blocks(held_ref, head, rows):
            _, grads = tile_terms(
                key_blk, value_blk, query_blk, upstream, norm_ref[head, :, cols], term_ref[head, :, cols],
                None, factor,
            )
            grad_query = lax.dot_general(
                grads, key_blk, (((0,), (0,)), ((), ())), preferred_element_type=jnp.float32
            )
            heads = slice(head * grouped, (head + 1) * grouped)
            dq_ref[toks, heads] = near_ref[toks, heads] + (grad_query * factor).reshape(
                rows // grouped, grouped, head_dim
            )


def combine_kernel(places_ref, mine_ref, other_ref, *out_refs):
    for step, out_ref in enumerate(out_refs):
        for kind in range(2):
            for head in range(out_ref.shape[1]):
                total = None
                for i, ref in enumerate((mine_ref, other_ref)):
                    for which in range(2):
                        row = places_ref[4 + 2 * i + which:5 + 2 * i + which]
                        term = jnp.where(row == step, ref[which, kind, head].astype(jnp.float32), 0.0)
                        total = term if total is None else total + term
                out_ref[kind, head] = total.astype(out_ref.dtype)


def total_kernel(parts, near_ref, *refs):
    *blocks, dk_ref, dv_ref = refs
    count = len(blocks) // parts
    heads = dk_ref.shape[1]
    each = heads // parts
    for kind, out_ref in enumerate((dk_ref, dv_ref)):
        for head in range(heads):
            total = near_ref[kind, head]
            for ref in blocks[head // each * count:(head // each + 1) * count]:
                total += ref[kind, head % each].astype(jnp.float32)
            out_ref[:, head, :] = total


def body(queries, keys, values, grad_out, row_lse, row_delta, doc_ids, pairs):
    tokens, heads, head_dim = queries.shape
    kv_heads = keys.shape[1]
    grouped = QH // KVH
    factor = head_dim ** (-0.5)
    ring = lax.axis_size("ctx")
    subs = lax.axis_size("sub")
    rows = min(ROWS, tokens * grouped)
    cols = tokens * grouped
    parts = 1
    each = kv_heads // parts
    span_shape = (2, each, tokens, head_dim)

    def crossed(blocks, order):
        return [lax.ppermute(blocks[e], "ctx", [(i, i ^ e) for i in range(ring)]) for e in order if e]

    def swapped(array):
        return lax.ppermute(array, "sub", [(i, i ^ 1) for i in range(subs)])

    def in_hbm(*arrays):
        return [pltpu.with_memory_space_constraint(array, pltpu.HBM) for array in arrays]

    params = pltpu.CompilerParams(vmem_limit_bytes=VMEM_LIMIT)
    kv = pl.pallas_call(
        pack_kernel,
        in_specs=[HBM_SPEC] * 2,
        out_specs=[VMEM_SPEC] * parts,
        out_shape=[jax.ShapeDtypeStruct(span_shape, jnp.bfloat16)] * parts,
        scratch_shapes=[pltpu.VMEM((2, *keys.shape), jnp.bfloat16), pltpu.SemaphoreType.DMA((2,))],
        compiler_params=params,
        name="pack",
    )(*in_hbm(keys, values))
    columns = [[*crossed([block] * ring, send_order(ring)), block] for block in kv]

    norm, term, docs, doc_col, places = pl.pallas_call(
        functools.partial(spread_kernel, grouped, ring, subs),
        in_specs=[HBM_SPEC] * 4,
        out_specs=[VMEM_SPEC] * 5,
        out_shape=[
            jax.ShapeDtypeStruct((kv_heads, 1, cols), jnp.float32),
            jax.ShapeDtypeStruct((kv_heads, 1, cols), jnp.float32),
            jax.ShapeDtypeStruct((1, cols), jnp.float32),
            jax.ShapeDtypeStruct((tokens, tokens), jnp.float32),
            jax.ShapeDtypeStruct((8, head_dim), jnp.int32),
        ],
        scratch_shapes=[
            pltpu.VMEM((2, heads, tokens), jnp.float32),
            pltpu.VMEM((1, tokens), jnp.int32),
            pltpu.VMEM(pairs.shape[::-1], jnp.int32),
            pltpu.SemaphoreType.DMA((4,)),
        ],
        compiler_params=params,
        name="spread",
    )(*in_hbm(row_lse.T, row_delta.T, doc_ids.reshape(1, tokens), pairs.T))

    work = 2 * tokens * tokens * heads * head_dim
    moved = 2 * queries.size * 2

    row_specs = [VMEM_SPEC] * 3
    near_kv, near_query, held = pl.pallas_call(
        functools.partial(local_kernel, factor, rows),
        in_specs=[VMEM_SPEC] * parts + [HBM_SPEC] * 2 + [VMEM_SPEC] * 4,
        out_specs=[VMEM_SPEC] * 3,
        out_shape=[
            jax.ShapeDtypeStruct((2, kv_heads, tokens, head_dim), jnp.float32),
            jax.ShapeDtypeStruct((tokens, heads, head_dim), jnp.float32),
            jax.ShapeDtypeStruct((2, kv_heads, tokens, grouped, head_dim), jnp.bfloat16),
        ],
        scratch_shapes=[pltpu.SemaphoreType.DMA((kv_heads, cols // rows, 2))],
        compiler_params=params,
        cost_estimate=pl.CostEstimate(flops=5 * work, bytes_accessed=2 * moved, transcendentals=0),
        name="local_block",
    )(*kv, *in_hbm(queries, grad_out), norm, term, docs, doc_col)

    inputs, sums = [], []
    after = near_kv
    for part, column in enumerate(columns):
        chosen = pl.pallas_call(
            choose_kernel,
            in_specs=[VMEM_SPEC] * (ring + 1) + [ANY_SPEC] * 2,
            out_specs=VMEM_SPEC,
            out_shape=jax.ShapeDtypeStruct((2, *span_shape), jnp.bfloat16),
            compiler_params=params,
            name="choose",
        )(places, *column, near_kv, after)
        other = swapped(chosen)
        inputs += [*column, other]
        far_kv = pl.pallas_call(
            functools.partial(listed_kernel, factor, rows, part * each),
            in_specs=[VMEM_SPEC] * (ring + 2) + row_specs,
            out_specs=VMEM_SPEC,
            out_shape=jax.ShapeDtypeStruct((2, *span_shape), jnp.bfloat16),
            compiler_params=params,
            cost_estimate=pl.CostEstimate(flops=8 * work // parts, bytes_accessed=moved // parts, transcendentals=0),
            name="listed_keys",
        )(places, *column, other, held, norm, term)
        other_kv = swapped(far_kv)
        blocks = pl.pallas_call(
            combine_kernel,
            in_specs=[VMEM_SPEC] * 3,
            out_specs=[VMEM_SPEC] * ring,
            out_shape=[jax.ShapeDtypeStruct(span_shape, jnp.float32)]
            + [jax.ShapeDtypeStruct(span_shape, jnp.bfloat16)] * (ring - 1),
            compiler_params=params,
            name="combine",
        )(places, far_kv, other_kv)
        sums += [blocks[0], *crossed(blocks, range(ring - 1, 0, -1))]
        after = blocks[0]

    grad_queries = pl.pallas_call(
        functools.partial(query_kernel, factor, rows, parts),
        in_specs=[VMEM_SPEC] * (1 + len(inputs)) + row_specs + [VMEM_SPEC, ANY_SPEC],
        out_specs=VMEM_SPEC,
        out_shape=jax.ShapeDtypeStruct((tokens, heads, head_dim), jnp.float32),
        compiler_params=params,
        cost_estimate=pl.CostEstimate(flops=6 * work, bytes_accessed=3 * moved, transcendentals=0),
        name="listed_queries",
    )(places, *inputs, held, norm, term, near_query, after)

    grad_keys, grad_values = pl.pallas_call(
        functools.partial(total_kernel, parts),
        in_specs=[VMEM_SPEC] * (parts * ring + 1),
        out_specs=[VMEM_SPEC] * 2,
        out_shape=[jax.ShapeDtypeStruct((tokens, kv_heads, head_dim), jnp.float32)] * 2,
        compiler_params=params,
        name="total",
    )(near_kv, *sums)
    return (grad_queries, grad_keys, grad_values)


def solution(mesh):
    return jax.shard_map(
        body,
        mesh=mesh,
        in_specs=(
            P(("groups", "ctx", "sub"), "head", None),
            P(("groups", "ctx", "sub"), "head", None),
            P(("groups", "ctx", "sub"), "head", None),
            P(("groups", "ctx", "sub"), "head", None),
            P(("groups", "ctx", "sub"), "head"),
            P(("groups", "ctx", "sub"), "head"),
            P(("groups", "ctx", "sub")),
            P("groups", None),
        ),
        out_specs=(
            P(("groups", "ctx", "sub"), "head", None),
            P(("groups", "ctx", "sub"), "head", None),
            P(("groups", "ctx", "sub"), "head", None),
        ),
        check_vma=False,
    )
```

```python
import functools

import jax
import jax.numpy as jnp
from jax import lax
from jax.experimental import pallas as pl
from jax.experimental.pallas import tpu as pltpu
from jax.sharding import PartitionSpec as P

QH = 64
KVH = 4
LOG2E = 1.4426950408889634
ROWS = 512
PARTS = 2
VMEM_LIMIT = 24 * 1024 * 1024

VMEM_SPEC = pl.BlockSpec(memory_space=pltpu.VMEM)
ANY_SPEC = pl.BlockSpec(memory_space=pl.ANY)
HBM_SPEC = pl.BlockSpec(memory_space=pltpu.HBM)


def rows_dot(left, right):
    return lax.dot_general(left, right, (((1,), (1,)), ((), ())), preferred_element_type=jnp.float32)


def tile_terms(key_blk, value_blk, query_blk, upstream, log_norm, row_terms, allowed, factor):
    scores = rows_dot(key_blk, query_blk)
    probs = jnp.exp2(scores * (factor * LOG2E) - log_norm)
    if allowed is not None:
        probs = jnp.where(allowed, probs, 0.0)
    grad_probs = rows_dot(value_blk, upstream)
    grad_scores = probs * (grad_probs - row_terms)
    return probs.astype(jnp.bfloat16), grad_scores.astype(jnp.bfloat16)


def chunks(tokens, grouped, rows):
    step = rows // grouped
    return [(i, slice(i * step, (i + 1) * step), slice(i * rows, (i + 1) * rows)) for i in range(tokens // step)]


def start_all(sources, targets, sems):
    copies = [pltpu.make_async_copy(source, target, sems.at[i]) for i, (source, target) in enumerate(zip(sources, targets))]
    for copy in copies:
        copy.start()
    return copies


def bring_rows(query_ref, up_ref, held_ref, sems, rows):
    _, count, tokens, grouped, _ = held_ref.shape
    copies = {}
    for head in range(count):
        heads = slice(head * grouped, (head + 1) * grouped)
        for i, toks, _ in chunks(tokens, grouped, rows):
            copies[head, i] = [
                pltpu.make_async_copy(ref.at[toks, heads], held_ref.at[kind, head, toks], sems.at[head, i, kind])
                for kind, ref in enumerate((query_ref, up_ref))
            ]
            for copy in copies[head, i]:
                copy.start()
    return copies


def row_blocks(held_ref, head, rows, copies=None):
    _, _, tokens, grouped, head_dim = held_ref.shape
    for i, toks, cols in chunks(tokens, grouped, rows):
        for copy in copies[head, i] if copies else ():
            copy.wait()
        yield toks, cols, *(held_ref[kind, head, toks].reshape(rows, head_dim) for kind in range(2))


def pack_kernel(key_ref, value_ref, kv_ref, held_ref, sems):
    copies = start_all((key_ref, value_ref), (held_ref.at[0], held_ref.at[1]), sems)
    for kind, copy in enumerate(copies):
        copy.wait()
        for head in range(held_ref.shape[2]):
            kv_ref[kind, head] = held_ref[kind, :, head, :]


def spread_kernel(
    grouped, ring, subs, norm_ref, term_ref, docs_ref, pairs_ref,
    norm_row_ref, term_row_ref, docs_row_ref, doc_col_ref, places_ref,
    held_ref, held_docs, held_pairs, sems,
):
    _, heads, tokens = held_ref.shape
    copies = start_all(
        (pairs_ref, docs_ref, norm_ref, term_ref), (held_pairs, held_docs, held_ref.at[0], held_ref.at[1]), sems
    )
    cols = tokens * grouped
    column = lax.broadcasted_iota(jnp.int32, (tokens, cols), 1)
    token = lax.broadcasted_iota(jnp.int32, (tokens, cols), 0)
    pick = jnp.where(token == column // grouped, 1.0, 0.0).astype(jnp.bfloat16)
    keep = lax.broadcasted_iota(jnp.int32, (grouped, cols), 0) == (
        lax.broadcasted_iota(jnp.int32, (grouped, cols), 1) % grouped
    )
    for copy in copies:
        copy.wait()

    ctx, sub = lax.axis_index("ctx"), lax.axis_index("sub")
    pairs = held_pairs[...]
    lane = lax.broadcasted_iota(jnp.int32, pairs.shape, 1)

    def listed_by(core):
        mask = lane == ctx * subs + core
        span = jnp.sum(jnp.where(mask, pairs, 0).astype(jnp.float32), axis=1, keepdims=True)
        span = jnp.broadcast_to(span, (2, places_ref.shape[1])).astype(jnp.int32)
        return span // subs, span % subs

    def around(gap):
        return jnp.where(gap < 0, gap + ring, gap)

    (mine, mine_sub), (other, other_sub) = listed_by(sub), listed_by(1 - sub)
    places_ref[0:2] = around(ctx - other)
    places_ref[2:4] = jnp.where(mine_sub == sub, around(ctx - mine), ring)
    places_ref[4:6] = jnp.where(mine_sub == sub, around(mine - ctx), ring)
    places_ref[6:8] = jnp.where(other_sub == sub, around(other - ctx), ring)

    pieces = []
    for value in (held_ref[0] * LOG2E, held_ref[1]):
        for _ in range(3):
            piece = value.astype(jnp.bfloat16)
            value = value - piece.astype(jnp.float32)
            pieces.append(piece)
    docs = held_docs[...].astype(jnp.float32)
    pieces.append(jnp.broadcast_to(docs, (grouped, tokens)).astype(jnp.bfloat16))
    spread = jnp.dot(jnp.concatenate(pieces, axis=0), pick, preferred_element_type=jnp.float32)
    for i, out_ref in enumerate((norm_row_ref, term_row_ref)):
        base = 3 * i * heads
        value = spread[base:base + heads] + spread[base + heads:base + 2 * heads]
        value = value + spread[base + 2 * heads:base + 3 * heads]
        for head in range(out_ref.shape[0]):
            group = value[head * grouped:(head + 1) * grouped]
            out_ref[head] = jnp.sum(jnp.where(keep, group, 0.0), axis=0, keepdims=True)
    docs_row_ref[...] = spread[6 * heads:6 * heads + 1]
    doc_col_ref[...] = jnp.broadcast_to(docs, (tokens, tokens)).T


def pick_block(sources, row):
    chosen = sources[0].astype(jnp.float32)
    for step in range(1, len(sources)):
        chosen = jnp.where(row == step, sources[step].astype(jnp.float32), chosen)
    return chosen.astype(jnp.bfloat16)


def choose_kernel(places_ref, *refs):
    *column, _, out_ref = refs
    for which in range(2):
        row = places_ref[which:which + 1]
        for kind in range(2):
            for head in range(out_ref.shape[2]):
                out_ref[which, kind, head] = pick_block([ref[kind, head] for ref in column], row)


def far_blocks(places_ref, column, other_ref, head):
    return [
        jnp.concatenate(
            [
                pick_block(
                    [ref[kind, head] for ref in column] + [other_ref[which, kind, head]],
                    places_ref[2 + which:3 + which],
                )
                for which in range(2)
            ],
            axis=0,
        )
        for kind in range(2)
    ]


def local_kernel(factor, rows, *refs):
    kv_ref, query_ref, up_ref, norm_ref, term_ref, docs_ref, doc_col_ref, dkv_ref, dq_ref, held_ref, sems = refs
    copies = bring_rows(query_ref, up_ref, held_ref, sems, rows)
    tokens, grouped, head_dim = held_ref.shape[2:]
    doc_col = jnp.concatenate([doc_col_ref[...]] * (rows // tokens), axis=1)
    for head in range(held_ref.shape[1]):
        key_blk, value_blk = kv_ref[0, head], kv_ref[1, head]
        grad_key = jnp.zeros((tokens, head_dim), jnp.float32)
        grad_val = jnp.zeros((tokens, head_dim), jnp.float32)
        for toks, cols, query_blk, upstream in row_blocks(held_ref, head, rows, copies):
            position = lax.broadcasted_iota(jnp.int32, (tokens, rows), 1) // grouped + toks.start
            allowed = (lax.broadcasted_iota(jnp.int32, (tokens, rows), 0) <= position) & (
                doc_col == docs_ref[:, cols]
            )
            probs, grads = tile_terms(
                key_blk, value_blk, query_blk, upstream, norm_ref[head, :, cols], term_ref[head, :, cols],
                allowed, factor,
            )
            grad_val += jnp.dot(probs, upstream, preferred_element_type=jnp.float32)
            grad_key += jnp.dot(grads, query_blk, preferred_element_type=jnp.float32)
            grad_query = lax.dot_general(
                grads, key_blk, (((0,), (0,)), ((), ())), preferred_element_type=jnp.float32
            )
            dq_ref[toks, head * grouped:(head + 1) * grouped] = (grad_query * factor).reshape(
                rows // grouped, grouped, head_dim
            )
        dkv_ref[0, head] = grad_key * factor
        dkv_ref[1, head] = grad_val


def listed_kernel(factor, rows, first, places_ref, *refs):
    *column, other_ref, held_ref, norm_ref, term_ref, _, dkv_ref = refs
    tokens, grouped, head_dim = held_ref.shape[2:]
    for head in range(dkv_ref.shape[2]):
        key_blk, value_blk = far_blocks(places_ref, column, other_ref, first + head)
        grad_key = jnp.zeros((2 * tokens, head_dim), jnp.float32)
        grad_val = jnp.zeros((2 * tokens, head_dim), jnp.float32)
        for toks, cols, query_blk, upstream in row_blocks(held_ref, first + head, rows):
            probs, grads = tile_terms(
                key_blk, value_blk, query_blk, upstream,
                norm_ref[first + head, :, cols], term_ref[first + head, :, cols], None, factor,
            )
            grad_val += jnp.dot(probs, upstream, preferred_element_type=jnp.float32)
            grad_key += jnp.dot(grads, query_blk, preferred_element_type=jnp.float32)
        grad_key = (grad_key * factor).astype(dkv_ref.dtype)
        grad_val = grad_val.astype(dkv_ref.dtype)
        for which in range(2):
            dkv_ref[which, 0, head] = grad_key[which * tokens:(which + 1) * tokens]
            dkv_ref[which, 1, head] = grad_val[which * tokens:(which + 1) * tokens]


def query_kernel(factor, rows, places_ref, *refs):
    *column, other_ref, held_ref, norm_ref, term_ref, near_ref, _, dq_ref = refs
    tokens, grouped, head_dim = held_ref.shape[2:]
    for head in range(held_ref.shape[1]):
        key_blk, value_blk = far_blocks(places_ref, column, other_ref, head)
        for toks, cols, query_blk, upstream in row_blocks(held_ref, head, rows):
            _, grads = tile_terms(
                key_blk, value_blk, query_blk, upstream, norm_ref[head, :, cols], term_ref[head, :, cols],
                None, factor,
            )
            grad_query = lax.dot_general(
                grads, key_blk, (((0,), (0,)), ((), ())), preferred_element_type=jnp.float32
            )
            heads = slice(head * grouped, (head + 1) * grouped)
            dq_ref[toks, heads] = near_ref[toks, heads] + (grad_query * factor).reshape(
                rows // grouped, grouped, head_dim
            )


def combine_kernel(places_ref, mine_ref, other_ref, *out_refs):
    for step, out_ref in enumerate(out_refs):
        for kind in range(2):
            for head in range(out_ref.shape[1]):
                total = None
                for i, ref in enumerate((mine_ref, other_ref)):
                    for which in range(2):
                        row = places_ref[4 + 2 * i + which:5 + 2 * i + which]
                        term = jnp.where(row == step, ref[which, kind, head].astype(jnp.float32), 0.0)
                        total = term if total is None else total + term
                out_ref[kind, head] = total.astype(out_ref.dtype)


def total_kernel(parts, near_ref, *refs):
    *blocks, dk_ref, dv_ref = refs
    count = len(blocks) // parts
    heads = dk_ref.shape[1]
    each = heads // parts
    for kind, out_ref in enumerate((dk_ref, dv_ref)):
        for head in range(heads):
            total = near_ref[kind, head]
            for ref in blocks[head // each * count:(head // each + 1) * count]:
                total += ref[kind, head % each].astype(jnp.float32)
            out_ref[:, head, :] = total


def body(queries, keys, values, grad_out, row_lse, row_delta, doc_ids, pairs):
    tokens, heads, head_dim = queries.shape
    kv_heads = keys.shape[1]
    grouped = QH // KVH
    factor = head_dim ** (-0.5)
    ring = lax.axis_size("ctx")
    subs = lax.axis_size("sub")
    rows = min(ROWS, tokens * grouped)
    cols = tokens * grouped
    parts = PARTS if kv_heads % PARTS == 0 else 1
    each = kv_heads // parts
    span_shape = (2, kv_heads, tokens, head_dim)
    part_shape = (2, each, tokens, head_dim)

    def shifted(array, shift):
        return lax.ppermute(array, "ctx", [(i, (i + shift) % ring) for i in range(ring)])

    def swapped(array):
        return lax.ppermute(array, "sub", [(i, i ^ 1) for i in range(subs)])

    def in_hbm(*arrays):
        return [pltpu.with_memory_space_constraint(array, pltpu.HBM) for array in arrays]

    params = pltpu.CompilerParams(vmem_limit_bytes=VMEM_LIMIT)
    kv = pl.pallas_call(
        pack_kernel,
        in_specs=[HBM_SPEC] * 2,
        out_specs=VMEM_SPEC,
        out_shape=jax.ShapeDtypeStruct(span_shape, jnp.bfloat16),
        scratch_shapes=[pltpu.VMEM((2, *keys.shape), jnp.bfloat16), pltpu.SemaphoreType.DMA((2,))],
        compiler_params=params,
        name="pack",
    )(*in_hbm(keys, values))
    column = [kv] + [shifted(kv, shift) for shift in range(1, ring)]

    norm, term, docs, doc_col, places = pl.pallas_call(
        functools.partial(spread_kernel, grouped, ring, subs),
        in_specs=[HBM_SPEC] * 4,
        out_specs=[VMEM_SPEC] * 5,
        out_shape=[
            jax.ShapeDtypeStruct((kv_heads, 1, cols), jnp.float32),
            jax.ShapeDtypeStruct((kv_heads, 1, cols), jnp.float32),
            jax.ShapeDtypeStruct((1, cols), jnp.float32),
            jax.ShapeDtypeStruct((tokens, tokens), jnp.float32),
            jax.ShapeDtypeStruct((8, head_dim), jnp.int32),
        ],
        scratch_shapes=[
            pltpu.VMEM((2, heads, tokens), jnp.float32),
            pltpu.VMEM((1, tokens), jnp.int32),
            pltpu.VMEM(pairs.shape[::-1], jnp.int32),
            pltpu.SemaphoreType.DMA((4,)),
        ],
        compiler_params=params,
        name="spread",
    )(*in_hbm(row_lse.T, row_delta.T, doc_ids.reshape(1, tokens), pairs.T))

    work = 2 * tokens * tokens * heads * head_dim
    moved = 2 * queries.size * 2

    row_specs = [VMEM_SPEC] * 3
    near_kv, near_query, held = pl.pallas_call(
        functools.partial(local_kernel, factor, rows),
        in_specs=[VMEM_SPEC] + [HBM_SPEC] * 2 + [VMEM_SPEC] * 4,
        out_specs=[VMEM_SPEC] * 3,
        out_shape=[
            jax.ShapeDtypeStruct((2, kv_heads, tokens, head_dim), jnp.float32),
            jax.ShapeDtypeStruct((tokens, heads, head_dim), jnp.float32),
            jax.ShapeDtypeStruct((2, kv_heads, tokens, grouped, head_dim), jnp.bfloat16),
        ],
        scratch_shapes=[pltpu.SemaphoreType.DMA((kv_heads, cols // rows, 2))],
        compiler_params=params,
        cost_estimate=pl.CostEstimate(flops=5 * work, bytes_accessed=2 * moved, transcendentals=0),
        name="local_block",
    )(kv, *in_hbm(queries, grad_out), norm, term, docs, doc_col)

    chosen = pl.pallas_call(
        choose_kernel,
        in_specs=[VMEM_SPEC] * (ring + 1) + [ANY_SPEC],
        out_specs=VMEM_SPEC,
        out_shape=jax.ShapeDtypeStruct((2, *span_shape), jnp.bfloat16),
        compiler_params=params,
        name="choose",
    )(places, *column, near_kv)
    other = swapped(chosen)

    sums = []
    far_kv = [near_kv]
    for part in range(parts):
        far_kv.append(
            pl.pallas_call(
                functools.partial(listed_kernel, factor, rows, part * each),
                in_specs=[VMEM_SPEC] * (ring + 2) + row_specs + [ANY_SPEC],
                out_specs=VMEM_SPEC,
                out_shape=jax.ShapeDtypeStruct((2, *part_shape), jnp.bfloat16),
                compiler_params=params,
                cost_estimate=pl.CostEstimate(
                    flops=8 * work // parts, bytes_accessed=moved // parts, transcendentals=0
                ),
                name="listed_keys",
            )(places, *column, other, held, norm, term, far_kv[-1])
        )
    for mine in far_kv[1:]:
        blocks = pl.pallas_call(
            combine_kernel,
            in_specs=[VMEM_SPEC] * 3,
            out_specs=[VMEM_SPEC] * ring,
            out_shape=[jax.ShapeDtypeStruct(part_shape, jnp.float32)]
            + [jax.ShapeDtypeStruct(part_shape, jnp.bfloat16)] * (ring - 1),
            compiler_params=params,
            name="combine",
        )(places, mine, swapped(mine))
        sums += [blocks[0]] + [shifted(blocks[shift], shift) for shift in range(1, ring)]
        after = blocks[0]

    grad_queries = pl.pallas_call(
        functools.partial(query_kernel, factor, rows),
        in_specs=[VMEM_SPEC] * (2 + ring) + row_specs + [VMEM_SPEC, ANY_SPEC],
        out_specs=VMEM_SPEC,
        out_shape=jax.ShapeDtypeStruct((tokens, heads, head_dim), jnp.float32),
        compiler_params=params,
        cost_estimate=pl.CostEstimate(flops=6 * work, bytes_accessed=3 * moved, transcendentals=0),
        name="listed_queries",
    )(places, *column, other, held, norm, term, near_query, after)

    grad_keys, grad_values = pl.pallas_call(
        functools.partial(total_kernel, parts),
        in_specs=[VMEM_SPEC] * (parts * ring + 1),
        out_specs=[VMEM_SPEC] * 2,
        out_shape=[jax.ShapeDtypeStruct((tokens, kv_heads, head_dim), jnp.float32)] * 2,
        compiler_params=params,
        name="total",
    )(near_kv, *sums)
    return (grad_queries, grad_keys, grad_values)


def solution(mesh):
    return jax.shard_map(
        body,
        mesh=mesh,
        in_specs=(
            P(("groups", "ctx", "sub"), "head", None),
            P(("groups", "ctx", "sub"), "head", None),
            P(("groups", "ctx", "sub"), "head", None),
            P(("groups", "ctx", "sub"), "head", None),
            P(("groups", "ctx", "sub"), "head"),
            P(("groups", "ctx", "sub"), "head"),
            P(("groups", "ctx", "sub")),
            P("groups", None),
        ),
        out_specs=(
            P(("groups", "ctx", "sub"), "head", None),
            P(("groups", "ctx", "sub"), "head", None),
            P(("groups", "ctx", "sub"), "head", None),
        ),
        check_vma=False,
    )
```

```python
import functools

import jax
import jax.numpy as jnp
from jax import lax
from jax.experimental import pallas as pl
from jax.experimental.pallas import tpu as pltpu
from jax.sharding import PartitionSpec as P

QH = 64
KVH = 4
LOG2E = 1.4426950408889634
ROWS = 512
PARTS = 2
VMEM_LIMIT = 24 * 1024 * 1024

VMEM_SPEC = pl.BlockSpec(memory_space=pltpu.VMEM)
ANY_SPEC = pl.BlockSpec(memory_space=pl.ANY)
HBM_SPEC = pl.BlockSpec(memory_space=pltpu.HBM)


def rows_dot(left, right):
    return lax.dot_general(left, right, (((1,), (1,)), ((), ())), preferred_element_type=jnp.float32)


def tile_terms(key_blk, value_blk, query_blk, upstream, log_norm, row_terms, allowed, factor):
    scores = rows_dot(key_blk, query_blk)
    probs = jnp.exp2(scores * (factor * LOG2E) - log_norm)
    if allowed is not None:
        probs = jnp.where(allowed, probs, 0.0)
    grad_probs = rows_dot(value_blk, upstream)
    grad_scores = probs * (grad_probs - row_terms)
    return probs.astype(jnp.bfloat16), grad_scores.astype(jnp.bfloat16)


def chunks(tokens, grouped, rows):
    step = rows // grouped
    return [(i, slice(i * step, (i + 1) * step), slice(i * rows, (i + 1) * rows)) for i in range(tokens // step)]


def start_all(sources, targets, sems):
    copies = [pltpu.make_async_copy(source, target, sems.at[i]) for i, (source, target) in enumerate(zip(sources, targets))]
    for copy in copies:
        copy.start()
    return copies


def bring_rows(query_ref, up_ref, held_ref, sems, rows):
    _, count, tokens, grouped, _ = held_ref.shape
    copies = {}
    for head in range(count):
        heads = slice(head * grouped, (head + 1) * grouped)
        for i, toks, _ in chunks(tokens, grouped, rows):
            copies[head, i] = [
                pltpu.make_async_copy(ref.at[toks, heads], held_ref.at[kind, head, toks], sems.at[head, i, kind])
                for kind, ref in enumerate((query_ref, up_ref))
            ]
            for copy in copies[head, i]:
                copy.start()
    return copies


def row_blocks(held_ref, head, rows, copies=None):
    _, _, tokens, grouped, head_dim = held_ref.shape
    for i, toks, cols in chunks(tokens, grouped, rows):
        for copy in copies[head, i] if copies else ():
            copy.wait()
        yield toks, cols, *(held_ref[kind, head, toks].reshape(rows, head_dim) for kind in range(2))


def pack_kernel(key_ref, value_ref, kv_ref, held_ref, sems):
    copies = start_all((key_ref, value_ref), (held_ref.at[0], held_ref.at[1]), sems)
    for kind, copy in enumerate(copies):
        copy.wait()
        for head in range(held_ref.shape[2]):
            kv_ref[kind, head] = held_ref[kind, :, head, :]


def spread_kernel(
    grouped, ring, subs, norm_ref, term_ref, docs_ref, pairs_ref,
    norm_row_ref, term_row_ref, docs_row_ref, doc_col_ref, places_ref,
    held_ref, held_docs, held_pairs, sems,
):
    _, heads, tokens = held_ref.shape
    copies = start_all(
        (pairs_ref, docs_ref, norm_ref, term_ref), (held_pairs, held_docs, held_ref.at[0], held_ref.at[1]), sems
    )
    cols = tokens * grouped
    column = lax.broadcasted_iota(jnp.int32, (tokens, cols), 1)
    token = lax.broadcasted_iota(jnp.int32, (tokens, cols), 0)
    pick = jnp.where(token == column // grouped, 1.0, 0.0).astype(jnp.bfloat16)
    keep = lax.broadcasted_iota(jnp.int32, (grouped, cols), 0) == (
        lax.broadcasted_iota(jnp.int32, (grouped, cols), 1) % grouped
    )
    for copy in copies:
        copy.wait()

    ctx, sub = lax.axis_index("ctx"), lax.axis_index("sub")
    pairs = held_pairs[...]
    lane = lax.broadcasted_iota(jnp.int32, pairs.shape, 1)

    def listed_by(core):
        mask = lane == ctx * subs + core
        span = jnp.sum(jnp.where(mask, pairs, 0).astype(jnp.float32), axis=1, keepdims=True)
        span = jnp.broadcast_to(span, (2, places_ref.shape[1])).astype(jnp.int32)
        return span // subs, span % subs

    def around(gap):
        return jnp.where(gap < 0, gap + ring, gap)

    (mine, mine_sub), (other, other_sub) = listed_by(sub), listed_by(1 - sub)
    places_ref[0:2] = around(ctx - other)
    places_ref[2:4] = jnp.where(mine_sub == sub, around(ctx - mine), ring)
    places_ref[4:6] = jnp.where(mine_sub == sub, around(mine - ctx), ring)
    places_ref[6:8] = jnp.where(other_sub == sub, around(other - ctx), ring)

    pieces = []
    for value in (held_ref[0] * LOG2E, held_ref[1]):
        for _ in range(3):
            piece = value.astype(jnp.bfloat16)
            value = value - piece.astype(jnp.float32)
            pieces.append(piece)
    docs = held_docs[...].astype(jnp.float32)
    pieces.append(jnp.broadcast_to(docs, (grouped, tokens)).astype(jnp.bfloat16))
    spread = jnp.dot(jnp.concatenate(pieces, axis=0), pick, preferred_element_type=jnp.float32)
    for i, out_ref in enumerate((norm_row_ref, term_row_ref)):
        base = 3 * i * heads
        value = spread[base:base + heads] + spread[base + heads:base + 2 * heads]
        value = value + spread[base + 2 * heads:base + 3 * heads]
        for head in range(out_ref.shape[0]):
            group = value[head * grouped:(head + 1) * grouped]
            out_ref[head] = jnp.sum(jnp.where(keep, group, 0.0), axis=0, keepdims=True)
    docs_row_ref[...] = spread[6 * heads:6 * heads + 1]
    doc_col_ref[...] = jnp.broadcast_to(docs, (tokens, tokens)).T


def pick_block(sources, row):
    chosen = sources[0].astype(jnp.float32)
    for step in range(1, len(sources)):
        chosen = jnp.where(row == step, sources[step].astype(jnp.float32), chosen)
    return chosen.astype(jnp.bfloat16)


def choose_kernel(places_ref, *refs):
    *column, _, out_ref = refs
    for which in range(2):
        row = places_ref[which:which + 1]
        for kind in range(2):
            for head in range(out_ref.shape[2]):
                out_ref[which, kind, head] = pick_block([ref[kind, head] for ref in column], row)


def far_blocks(places_ref, column, other_ref, head):
    return [
        jnp.concatenate(
            [
                pick_block(
                    [ref[kind, head] for ref in column] + [other_ref[which, kind, head]],
                    places_ref[2 + which:3 + which],
                )
                for which in range(2)
            ],
            axis=0,
        )
        for kind in range(2)
    ]


def local_kernel(factor, rows, *refs):
    kv_ref, query_ref, up_ref, norm_ref, term_ref, docs_ref, doc_col_ref, dkv_ref, dq_ref, held_ref, sems = refs
    copies = bring_rows(query_ref, up_ref, held_ref, sems, rows)
    tokens, grouped, head_dim = held_ref.shape[2:]
    doc_col = jnp.concatenate([doc_col_ref[...]] * (rows // tokens), axis=1)
    for head in range(held_ref.shape[1]):
        key_blk, value_blk = kv_ref[0, head], kv_ref[1, head]
        grad_key = jnp.zeros((tokens, head_dim), jnp.float32)
        grad_val = jnp.zeros((tokens, head_dim), jnp.float32)
        for toks, cols, query_blk, upstream in row_blocks(held_ref, head, rows, copies):
            position = lax.broadcasted_iota(jnp.int32, (tokens, rows), 1) // grouped + toks.start
            allowed = (lax.broadcasted_iota(jnp.int32, (tokens, rows), 0) <= position) & (
                doc_col == docs_ref[:, cols]
            )
            probs, grads = tile_terms(
                key_blk, value_blk, query_blk, upstream, norm_ref[head, :, cols], term_ref[head, :, cols],
                allowed, factor,
            )
            grad_val += jnp.dot(probs, upstream, preferred_element_type=jnp.float32)
            grad_key += jnp.dot(grads, query_blk, preferred_element_type=jnp.float32)
            grad_query = lax.dot_general(
                grads, key_blk, (((0,), (0,)), ((), ())), preferred_element_type=jnp.float32
            )
            dq_ref[toks, head * grouped:(head + 1) * grouped] = (grad_query * factor).reshape(
                rows // grouped, grouped, head_dim
            )
        dkv_ref[0, head] = grad_key * factor
        dkv_ref[1, head] = grad_val


def listed_kernel(factor, rows, first, places_ref, *refs):
    *column, other_ref, held_ref, norm_ref, term_ref, _, dkv_ref = refs
    tokens, grouped, head_dim = held_ref.shape[2:]
    for head in range(dkv_ref.shape[2]):
        key_blk, value_blk = far_blocks(places_ref, column, other_ref, first + head)
        grad_key = jnp.zeros((2 * tokens, head_dim), jnp.float32)
        grad_val = jnp.zeros((2 * tokens, head_dim), jnp.float32)
        for toks, cols, query_blk, upstream in row_blocks(held_ref, first + head, rows):
            probs, grads = tile_terms(
                key_blk, value_blk, query_blk, upstream,
                norm_ref[first + head, :, cols], term_ref[first + head, :, cols], None, factor,
            )
            grad_val += jnp.dot(probs, upstream, preferred_element_type=jnp.float32)
            grad_key += jnp.dot(grads, query_blk, preferred_element_type=jnp.float32)
        grad_key = (grad_key * factor).astype(dkv_ref.dtype)
        grad_val = grad_val.astype(dkv_ref.dtype)
        for which in range(2):
            dkv_ref[which, 0, head] = grad_key[which * tokens:(which + 1) * tokens]
            dkv_ref[which, 1, head] = grad_val[which * tokens:(which + 1) * tokens]


def query_kernel(factor, rows, places_ref, *refs):
    *column, other_ref, held_ref, norm_ref, term_ref, near_ref, _, dq_ref = refs
    tokens, grouped, head_dim = held_ref.shape[2:]
    for head in range(held_ref.shape[1]):
        key_blk, value_blk = far_blocks(places_ref, column, other_ref, head)
        for toks, cols, query_blk, upstream in row_blocks(held_ref, head, rows):
            _, grads = tile_terms(
                key_blk, value_blk, query_blk, upstream, norm_ref[head, :, cols], term_ref[head, :, cols],
                None, factor,
            )
            grad_query = lax.dot_general(
                grads, key_blk, (((0,), (0,)), ((), ())), preferred_element_type=jnp.float32
            )
            heads = slice(head * grouped, (head + 1) * grouped)
            dq_ref[toks, heads] = near_ref[toks, heads] + (grad_query * factor).reshape(
                rows // grouped, grouped, head_dim
            )


def combine_kernel(places_ref, mine_ref, other_ref, *out_refs):
    for step, out_ref in enumerate(out_refs):
        for kind in range(2):
            for head in range(out_ref.shape[1]):
                total = None
                for i, ref in enumerate((mine_ref, other_ref)):
                    for which in range(2):
                        row = places_ref[4 + 2 * i + which:5 + 2 * i + which]
                        term = jnp.where(row == step, ref[which, kind, head].astype(jnp.float32), 0.0)
                        total = term if total is None else total + term
                out_ref[kind, head] = total.astype(out_ref.dtype)


def total_kernel(parts, near_ref, *refs):
    *blocks, dk_ref, dv_ref = refs
    count = len(blocks) // parts
    heads = dk_ref.shape[1]
    each = heads // parts
    for kind, out_ref in enumerate((dk_ref, dv_ref)):
        for head in range(heads):
            total = near_ref[kind, head]
            for ref in blocks[head // each * count:(head // each + 1) * count]:
                total += ref[kind, head % each].astype(jnp.float32)
            out_ref[:, head, :] = total


def body(queries, keys, values, grad_out, row_lse, row_delta, doc_ids, pairs):
    tokens, heads, head_dim = queries.shape
    kv_heads = keys.shape[1]
    grouped = QH // KVH
    factor = head_dim ** (-0.5)
    ring = lax.axis_size("ctx")
    subs = lax.axis_size("sub")
    rows = min(ROWS, tokens * grouped)
    cols = tokens * grouped
    parts = PARTS if kv_heads % PARTS == 0 else 1
    each = kv_heads // parts
    span_shape = (2, kv_heads, tokens, head_dim)
    part_shape = (2, each, tokens, head_dim)

    def shifted(array, shift):
        return lax.ppermute(array, "ctx", [(i, (i + shift) % ring) for i in range(ring)])

    def swapped(array):
        return lax.ppermute(array, "sub", [(i, i ^ 1) for i in range(subs)])

    def in_hbm(*arrays):
        return [pltpu.with_memory_space_constraint(array, pltpu.HBM) for array in arrays]

    params = pltpu.CompilerParams(vmem_limit_bytes=VMEM_LIMIT)
    kv = pl.pallas_call(
        pack_kernel,
        in_specs=[HBM_SPEC] * 2,
        out_specs=VMEM_SPEC,
        out_shape=jax.ShapeDtypeStruct(span_shape, jnp.bfloat16),
        scratch_shapes=[pltpu.VMEM((2, *keys.shape), jnp.bfloat16), pltpu.SemaphoreType.DMA((2,))],
        compiler_params=params,
        name="pack",
    )(*in_hbm(keys, values))
    column = [kv] + [shifted(kv, shift) for shift in range(1, ring)]

    norm, term, docs, doc_col, places = pl.pallas_call(
        functools.partial(spread_kernel, grouped, ring, subs),
        in_specs=[HBM_SPEC] * 4,
        out_specs=[VMEM_SPEC] * 5,
        out_shape=[
            jax.ShapeDtypeStruct((kv_heads, 1, cols), jnp.float32),
            jax.ShapeDtypeStruct((kv_heads, 1, cols), jnp.float32),
            jax.ShapeDtypeStruct((1, cols), jnp.float32),
            jax.ShapeDtypeStruct((tokens, tokens), jnp.float32),
            jax.ShapeDtypeStruct((8, head_dim), jnp.int32),
        ],
        scratch_shapes=[
            pltpu.VMEM((2, heads, tokens), jnp.float32),
            pltpu.VMEM((1, tokens), jnp.int32),
            pltpu.VMEM(pairs.shape[::-1], jnp.int32),
            pltpu.SemaphoreType.DMA((4,)),
        ],
        compiler_params=params,
        name="spread",
    )(*in_hbm(row_lse.T, row_delta.T, doc_ids.reshape(1, tokens), pairs.T))

    work = 2 * tokens * tokens * heads * head_dim
    moved = 2 * queries.size * 2

    row_specs = [VMEM_SPEC] * 3
    near_kv, near_query, held = pl.pallas_call(
        functools.partial(local_kernel, factor, rows),
        in_specs=[VMEM_SPEC] + [HBM_SPEC] * 2 + [VMEM_SPEC] * 4,
        out_specs=[VMEM_SPEC] * 3,
        out_shape=[
            jax.ShapeDtypeStruct((2, kv_heads, tokens, head_dim), jnp.float32),
            jax.ShapeDtypeStruct((tokens, heads, head_dim), jnp.float32),
            jax.ShapeDtypeStruct((2, kv_heads, tokens, grouped, head_dim), jnp.bfloat16),
        ],
        scratch_shapes=[pltpu.SemaphoreType.DMA((kv_heads, cols // rows, 2))],
        compiler_params=params,
        cost_estimate=pl.CostEstimate(flops=5 * work, bytes_accessed=2 * moved, transcendentals=0),
        name="local_block",
    )(kv, *in_hbm(queries, grad_out), norm, term, docs, doc_col)

    chosen = pl.pallas_call(
        choose_kernel,
        in_specs=[VMEM_SPEC] * (ring + 1) + [ANY_SPEC],
        out_specs=VMEM_SPEC,
        out_shape=jax.ShapeDtypeStruct((2, *span_shape), jnp.bfloat16),
        compiler_params=params,
        name="choose",
    )(places, *column, near_kv)
    other = swapped(chosen)

    sums = []
    far_kv = [near_kv]
    for part in range(parts):
        far_kv.append(
            pl.pallas_call(
                functools.partial(listed_kernel, factor, rows, part * each),
                in_specs=[VMEM_SPEC] * (ring + 2) + row_specs + [ANY_SPEC],
                out_specs=VMEM_SPEC,
                out_shape=jax.ShapeDtypeStruct((2, *part_shape), jnp.bfloat16),
                compiler_params=params,
                cost_estimate=pl.CostEstimate(
                    flops=8 * work // parts, bytes_accessed=moved // parts, transcendentals=0
                ),
                name="listed_keys",
            )(places, *column, other, held, norm, term, far_kv[-1])
        )
    for mine in far_kv[1:]:
        blocks = pl.pallas_call(
            combine_kernel,
            in_specs=[VMEM_SPEC] * 3,
            out_specs=[VMEM_SPEC] * ring,
            out_shape=[jax.ShapeDtypeStruct(part_shape, jnp.float32)]
            + [jax.ShapeDtypeStruct(part_shape, jnp.bfloat16)] * (ring - 1),
            compiler_params=params,
            name="combine",
        )(places, mine, swapped(mine))
        order = [*range(1, ring)] if mine is far_kv[1] else [ring - 1, *range(1, ring - 1)]
        sums += [blocks[0]] + [shifted(blocks[shift], shift) for shift in order]
        after = blocks[0]

    grad_queries = pl.pallas_call(
        functools.partial(query_kernel, factor, rows),
        in_specs=[VMEM_SPEC] * (2 + ring) + row_specs + [VMEM_SPEC, ANY_SPEC],
        out_specs=VMEM_SPEC,
        out_shape=jax.ShapeDtypeStruct((tokens, heads, head_dim), jnp.float32),
        compiler_params=params,
        cost_estimate=pl.CostEstimate(flops=6 * work, bytes_accessed=3 * moved, transcendentals=0),
        name="listed_queries",
    )(places, *column, other, held, norm, term, near_query, after)

    grad_keys, grad_values = pl.pallas_call(
        functools.partial(total_kernel, parts),
        in_specs=[VMEM_SPEC] * (parts * ring + 1),
        out_specs=[VMEM_SPEC] * 2,
        out_shape=[jax.ShapeDtypeStruct((tokens, kv_heads, head_dim), jnp.float32)] * 2,
        compiler_params=params,
        name="total",
    )(near_kv, *sums)
    return (grad_queries, grad_keys, grad_values)


def solution(mesh):
    return jax.shard_map(
        body,
        mesh=mesh,
        in_specs=(
            P(("groups", "ctx", "sub"), "head", None),
            P(("groups", "ctx", "sub"), "head", None),
            P(("groups", "ctx", "sub"), "head", None),
            P(("groups", "ctx", "sub"), "head", None),
            P(("groups", "ctx", "sub"), "head"),
            P(("groups", "ctx", "sub"), "head"),
            P(("groups", "ctx", "sub")),
            P("groups", None),
        ),
        out_specs=(
            P(("groups", "ctx", "sub"), "head", None),
            P(("groups", "ctx", "sub"), "head", None),
            P(("groups", "ctx", "sub"), "head", None),
        ),
        check_vma=False,
    )
```

```python
import functools

import jax
import jax.numpy as jnp
from jax import lax
from jax.experimental import pallas as pl
from jax.experimental.pallas import tpu as pltpu
from jax.sharding import PartitionSpec as P

QH = 64
KVH = 4
LOG2E = 1.4426950408889634
ROWS = 1024
PARTS = 2
VMEM_LIMIT = 24 * 1024 * 1024

VMEM_SPEC = pl.BlockSpec(memory_space=pltpu.VMEM)
ANY_SPEC = pl.BlockSpec(memory_space=pl.ANY)
HBM_SPEC = pl.BlockSpec(memory_space=pltpu.HBM)


def rows_dot(left, right):
    return lax.dot_general(left, right, (((1,), (1,)), ((), ())), preferred_element_type=jnp.float32)


def tile_terms(key_blk, value_blk, query_blk, upstream, log_norm, row_terms, allowed, factor):
    scores = rows_dot(key_blk, query_blk)
    probs = jnp.exp2(scores * (factor * LOG2E) - log_norm)
    if allowed is not None:
        probs = jnp.where(allowed, probs, 0.0)
    grad_probs = rows_dot(value_blk, upstream)
    grad_scores = probs * (grad_probs - row_terms)
    return probs.astype(jnp.bfloat16), grad_scores.astype(jnp.bfloat16)


def chunks(tokens, grouped, rows):
    step = rows // grouped
    return [(i, slice(i * step, (i + 1) * step), slice(i * rows, (i + 1) * rows)) for i in range(tokens // step)]


def start_all(sources, targets, sems):
    copies = [pltpu.make_async_copy(source, target, sems.at[i]) for i, (source, target) in enumerate(zip(sources, targets))]
    for copy in copies:
        copy.start()
    return copies


def bring_rows(query_ref, up_ref, held_ref, sems, rows):
    _, count, tokens, grouped, _ = held_ref.shape
    copies = {}
    for head in range(count):
        heads = slice(head * grouped, (head + 1) * grouped)
        for i, toks, _ in chunks(tokens, grouped, rows):
            copies[head, i] = [
                pltpu.make_async_copy(ref.at[toks, heads], held_ref.at[kind, head, toks], sems.at[head, i, kind])
                for kind, ref in enumerate((query_ref, up_ref))
            ]
            for copy in copies[head, i]:
                copy.start()
    return copies


def row_blocks(held_ref, head, rows, copies=None):
    _, _, tokens, grouped, head_dim = held_ref.shape
    for i, toks, cols in chunks(tokens, grouped, rows):
        for copy in copies[head, i] if copies else ():
            copy.wait()
        yield toks, cols, *(held_ref[kind, head, toks].reshape(rows, head_dim) for kind in range(2))


def pack_kernel(key_ref, value_ref, kv_ref, held_ref, sems):
    copies = start_all((key_ref, value_ref), (held_ref.at[0], held_ref.at[1]), sems)
    for kind, copy in enumerate(copies):
        copy.wait()
        for head in range(held_ref.shape[2]):
            kv_ref[kind, head] = held_ref[kind, :, head, :]


def spread_kernel(
    grouped, ring, subs, norm_ref, term_ref, docs_ref, pairs_ref,
    norm_row_ref, term_row_ref, docs_row_ref, doc_col_ref, places_ref,
    held_ref, held_docs, held_pairs, sems,
):
    _, heads, tokens = held_ref.shape
    copies = start_all(
        (pairs_ref, docs_ref, norm_ref, term_ref), (held_pairs, held_docs, held_ref.at[0], held_ref.at[1]), sems
    )
    cols = tokens * grouped
    column = lax.broadcasted_iota(jnp.int32, (tokens, cols), 1)
    token = lax.broadcasted_iota(jnp.int32, (tokens, cols), 0)
    pick = jnp.where(token == column // grouped, 1.0, 0.0).astype(jnp.bfloat16)
    keep = lax.broadcasted_iota(jnp.int32, (grouped, cols), 0) == (
        lax.broadcasted_iota(jnp.int32, (grouped, cols), 1) % grouped
    )
    for copy in copies:
        copy.wait()

    ctx, sub = lax.axis_index("ctx"), lax.axis_index("sub")
    pairs = held_pairs[...]
    lane = lax.broadcasted_iota(jnp.int32, pairs.shape, 1)

    def listed_by(core):
        mask = lane == ctx * subs + core
        span = jnp.sum(jnp.where(mask, pairs, 0).astype(jnp.float32), axis=1, keepdims=True)
        span = jnp.broadcast_to(span, (2, places_ref.shape[1])).astype(jnp.int32)
        return span // subs, span % subs

    def around(gap):
        return jnp.where(gap < 0, gap + ring, gap)

    (mine, mine_sub), (other, other_sub) = listed_by(sub), listed_by(1 - sub)
    places_ref[0:2] = around(ctx - other)
    places_ref[2:4] = jnp.where(mine_sub == sub, around(ctx - mine), ring)
    places_ref[4:6] = jnp.where(mine_sub == sub, around(mine - ctx), ring)
    places_ref[6:8] = jnp.where(other_sub == sub, around(other - ctx), ring)

    pieces = []
    for value in (held_ref[0] * LOG2E, held_ref[1]):
        for _ in range(3):
            piece = value.astype(jnp.bfloat16)
            value = value - piece.astype(jnp.float32)
            pieces.append(piece)
    docs = held_docs[...].astype(jnp.float32)
    pieces.append(jnp.broadcast_to(docs, (grouped, tokens)).astype(jnp.bfloat16))
    spread = jnp.dot(jnp.concatenate(pieces, axis=0), pick, preferred_element_type=jnp.float32)
    for i, out_ref in enumerate((norm_row_ref, term_row_ref)):
        base = 3 * i * heads
        value = spread[base:base + heads] + spread[base + heads:base + 2 * heads]
        value = value + spread[base + 2 * heads:base + 3 * heads]
        for head in range(out_ref.shape[0]):
            group = value[head * grouped:(head + 1) * grouped]
            out_ref[head] = jnp.sum(jnp.where(keep, group, 0.0), axis=0, keepdims=True)
    docs_row_ref[...] = spread[6 * heads:6 * heads + 1]
    doc_col_ref[...] = jnp.broadcast_to(docs, (tokens, tokens)).T


def pick_block(sources, row):
    chosen = sources[0].astype(jnp.float32)
    for step in range(1, len(sources)):
        chosen = jnp.where(row == step, sources[step].astype(jnp.float32), chosen)
    return chosen.astype(jnp.bfloat16)


def choose_kernel(places_ref, *refs):
    *column, _, out_ref = refs
    for which in range(2):
        row = places_ref[which:which + 1]
        for kind in range(2):
            for head in range(out_ref.shape[2]):
                out_ref[which, kind, head] = pick_block([ref[kind, head] for ref in column], row)


def far_blocks(places_ref, column, other_ref, head):
    return [
        jnp.concatenate(
            [
                pick_block(
                    [ref[kind, head] for ref in column] + [other_ref[which, kind, head]],
                    places_ref[2 + which:3 + which],
                )
                for which in range(2)
            ],
            axis=0,
        )
        for kind in range(2)
    ]


def local_kernel(factor, rows, *refs):
    kv_ref, query_ref, up_ref, norm_ref, term_ref, docs_ref, doc_col_ref, dkv_ref, dq_ref, held_ref, sems = refs
    copies = bring_rows(query_ref, up_ref, held_ref, sems, rows)
    tokens, grouped, head_dim = held_ref.shape[2:]
    doc_col = jnp.concatenate([doc_col_ref[...]] * (rows // tokens), axis=1)
    for head in range(held_ref.shape[1]):
        key_blk, value_blk = kv_ref[0, head], kv_ref[1, head]
        grad_key = jnp.zeros((tokens, head_dim), jnp.float32)
        grad_val = jnp.zeros((tokens, head_dim), jnp.float32)
        for toks, cols, query_blk, upstream in row_blocks(held_ref, head, rows, copies):
            position = lax.broadcasted_iota(jnp.int32, (tokens, rows), 1) // grouped + toks.start
            allowed = (lax.broadcasted_iota(jnp.int32, (tokens, rows), 0) <= position) & (
                doc_col == docs_ref[:, cols]
            )
            probs, grads = tile_terms(
                key_blk, value_blk, query_blk, upstream, norm_ref[head, :, cols], term_ref[head, :, cols],
                allowed, factor,
            )
            grad_val += jnp.dot(probs, upstream, preferred_element_type=jnp.float32)
            grad_key += jnp.dot(grads, query_blk, preferred_element_type=jnp.float32)
            grad_query = lax.dot_general(
                grads, key_blk, (((0,), (0,)), ((), ())), preferred_element_type=jnp.float32
            )
            dq_ref[toks, head * grouped:(head + 1) * grouped] = (grad_query * factor).reshape(
                rows // grouped, grouped, head_dim
            )
        dkv_ref[0, head] = grad_key * factor
        dkv_ref[1, head] = grad_val


def listed_kernel(factor, rows, first, places_ref, *refs):
    *column, other_ref, held_ref, norm_ref, term_ref, _, dkv_ref = refs
    tokens, grouped, head_dim = held_ref.shape[2:]
    for head in range(dkv_ref.shape[2]):
        key_blk, value_blk = far_blocks(places_ref, column, other_ref, first + head)
        grad_key = jnp.zeros((2 * tokens, head_dim), jnp.float32)
        grad_val = jnp.zeros((2 * tokens, head_dim), jnp.float32)
        for toks, cols, query_blk, upstream in row_blocks(held_ref, first + head, rows):
            probs, grads = tile_terms(
                key_blk, value_blk, query_blk, upstream,
                norm_ref[first + head, :, cols], term_ref[first + head, :, cols], None, factor,
            )
            grad_val += jnp.dot(probs, upstream, preferred_element_type=jnp.float32)
            grad_key += jnp.dot(grads, query_blk, preferred_element_type=jnp.float32)
        grad_key = (grad_key * factor).astype(dkv_ref.dtype)
        grad_val = grad_val.astype(dkv_ref.dtype)
        for which in range(2):
            dkv_ref[which, 0, head] = grad_key[which * tokens:(which + 1) * tokens]
            dkv_ref[which, 1, head] = grad_val[which * tokens:(which + 1) * tokens]


def query_kernel(factor, rows, places_ref, *refs):
    *column, other_ref, held_ref, norm_ref, term_ref, near_ref, _, dq_ref = refs
    tokens, grouped, head_dim = held_ref.shape[2:]
    for head in range(held_ref.shape[1]):
        key_blk, value_blk = far_blocks(places_ref, column, other_ref, head)
        for toks, cols, query_blk, upstream in row_blocks(held_ref, head, rows):
            _, grads = tile_terms(
                key_blk, value_blk, query_blk, upstream, norm_ref[head, :, cols], term_ref[head, :, cols],
                None, factor,
            )
            grad_query = lax.dot_general(
                grads, key_blk, (((0,), (0,)), ((), ())), preferred_element_type=jnp.float32
            )
            heads = slice(head * grouped, (head + 1) * grouped)
            dq_ref[toks, heads] = near_ref[toks, heads] + (grad_query * factor).reshape(
                rows // grouped, grouped, head_dim
            )


def combine_kernel(places_ref, mine_ref, other_ref, *out_refs):
    for step, out_ref in enumerate(out_refs):
        for kind in range(2):
            for head in range(out_ref.shape[1]):
                total = None
                for i, ref in enumerate((mine_ref, other_ref)):
                    for which in range(2):
                        row = places_ref[4 + 2 * i + which:5 + 2 * i + which]
                        term = jnp.where(row == step, ref[which, kind, head].astype(jnp.float32), 0.0)
                        total = term if total is None else total + term
                out_ref[kind, head] = total.astype(out_ref.dtype)


def total_kernel(parts, near_ref, *refs):
    *blocks, dk_ref, dv_ref = refs
    count = len(blocks) // parts
    heads = dk_ref.shape[1]
    each = heads // parts
    for kind, out_ref in enumerate((dk_ref, dv_ref)):
        for head in range(heads):
            total = near_ref[kind, head]
            for ref in blocks[head // each * count:(head // each + 1) * count]:
                total += ref[kind, head % each].astype(jnp.float32)
            out_ref[:, head, :] = total


def body(queries, keys, values, grad_out, row_lse, row_delta, doc_ids, pairs):
    tokens, heads, head_dim = queries.shape
    kv_heads = keys.shape[1]
    grouped = QH // KVH
    factor = head_dim ** (-0.5)
    ring = lax.axis_size("ctx")
    subs = lax.axis_size("sub")
    rows = min(ROWS, tokens * grouped)
    cols = tokens * grouped
    parts = PARTS if kv_heads % PARTS == 0 else 1
    each = kv_heads // parts
    span_shape = (2, kv_heads, tokens, head_dim)
    part_shape = (2, each, tokens, head_dim)

    def shifted(array, shift):
        return lax.ppermute(array, "ctx", [(i, (i + shift) % ring) for i in range(ring)])

    def swapped(array):
        return lax.ppermute(array, "sub", [(i, i ^ 1) for i in range(subs)])

    def in_hbm(*arrays):
        return [pltpu.with_memory_space_constraint(array, pltpu.HBM) for array in arrays]

    params = pltpu.CompilerParams(vmem_limit_bytes=VMEM_LIMIT)
    kv = pl.pallas_call(
        pack_kernel,
        in_specs=[HBM_SPEC] * 2,
        out_specs=VMEM_SPEC,
        out_shape=jax.ShapeDtypeStruct(span_shape, jnp.bfloat16),
        scratch_shapes=[pltpu.VMEM((2, *keys.shape), jnp.bfloat16), pltpu.SemaphoreType.DMA((2,))],
        compiler_params=params,
        name="pack",
    )(*in_hbm(keys, values))
    column = [kv] + [shifted(kv, shift) for shift in range(1, ring)]

    norm, term, docs, doc_col, places = pl.pallas_call(
        functools.partial(spread_kernel, grouped, ring, subs),
        in_specs=[HBM_SPEC] * 4,
        out_specs=[VMEM_SPEC] * 5,
        out_shape=[
            jax.ShapeDtypeStruct((kv_heads, 1, cols), jnp.float32),
            jax.ShapeDtypeStruct((kv_heads, 1, cols), jnp.float32),
            jax.ShapeDtypeStruct((1, cols), jnp.float32),
            jax.ShapeDtypeStruct((tokens, tokens), jnp.float32),
            jax.ShapeDtypeStruct((8, head_dim), jnp.int32),
        ],
        scratch_shapes=[
            pltpu.VMEM((2, heads, tokens), jnp.float32),
            pltpu.VMEM((1, tokens), jnp.int32),
            pltpu.VMEM(pairs.shape[::-1], jnp.int32),
            pltpu.SemaphoreType.DMA((4,)),
        ],
        compiler_params=params,
        name="spread",
    )(*in_hbm(row_lse.T, row_delta.T, doc_ids.reshape(1, tokens), pairs.T))

    work = 2 * tokens * tokens * heads * head_dim
    moved = 2 * queries.size * 2

    row_specs = [VMEM_SPEC] * 3
    near_kv, near_query, held = pl.pallas_call(
        functools.partial(local_kernel, factor, rows),
        in_specs=[VMEM_SPEC] + [HBM_SPEC] * 2 + [VMEM_SPEC] * 4,
        out_specs=[VMEM_SPEC] * 3,
        out_shape=[
            jax.ShapeDtypeStruct((2, kv_heads, tokens, head_dim), jnp.float32),
            jax.ShapeDtypeStruct((tokens, heads, head_dim), jnp.float32),
            jax.ShapeDtypeStruct((2, kv_heads, tokens, grouped, head_dim), jnp.bfloat16),
        ],
        scratch_shapes=[pltpu.SemaphoreType.DMA((kv_heads, cols // rows, 2))],
        compiler_params=params,
        cost_estimate=pl.CostEstimate(flops=5 * work, bytes_accessed=2 * moved, transcendentals=0),
        name="local_block",
    )(kv, *in_hbm(queries, grad_out), norm, term, docs, doc_col)

    chosen = pl.pallas_call(
        choose_kernel,
        in_specs=[VMEM_SPEC] * (ring + 1) + [ANY_SPEC],
        out_specs=VMEM_SPEC,
        out_shape=jax.ShapeDtypeStruct((2, *span_shape), jnp.bfloat16),
        compiler_params=params,
        name="choose",
    )(places, *column, near_kv)
    other = swapped(chosen)

    sums = []
    far_kv = [near_kv]
    for part in range(parts):
        far_kv.append(
            pl.pallas_call(
                functools.partial(listed_kernel, factor, rows, part * each),
                in_specs=[VMEM_SPEC] * (ring + 2) + row_specs + [ANY_SPEC],
                out_specs=VMEM_SPEC,
                out_shape=jax.ShapeDtypeStruct((2, *part_shape), jnp.bfloat16),
                compiler_params=params,
                cost_estimate=pl.CostEstimate(
                    flops=8 * work // parts, bytes_accessed=moved // parts, transcendentals=0
                ),
                name="listed_keys",
            )(places, *column, other, held, norm, term, far_kv[-1])
        )
    for mine in far_kv[1:]:
        blocks = pl.pallas_call(
            combine_kernel,
            in_specs=[VMEM_SPEC] * 3,
            out_specs=[VMEM_SPEC] * ring,
            out_shape=[jax.ShapeDtypeStruct(part_shape, jnp.float32)]
            + [jax.ShapeDtypeStruct(part_shape, jnp.bfloat16)] * (ring - 1),
            compiler_params=params,
            name="combine",
        )(places, mine, swapped(mine))
        order = [*range(1, ring)] if mine is far_kv[1] else [ring - 1, *range(1, ring - 1)]
        sums += [blocks[0]] + [shifted(blocks[shift], shift) for shift in order]
        after = blocks[0]

    grad_queries = pl.pallas_call(
        functools.partial(query_kernel, factor, rows),
        in_specs=[VMEM_SPEC] * (2 + ring) + row_specs + [VMEM_SPEC, ANY_SPEC],
        out_specs=VMEM_SPEC,
        out_shape=jax.ShapeDtypeStruct((tokens, heads, head_dim), jnp.float32),
        compiler_params=params,
        cost_estimate=pl.CostEstimate(flops=6 * work, bytes_accessed=3 * moved, transcendentals=0),
        name="listed_queries",
    )(places, *column, other, held, norm, term, near_query, after)

    grad_keys, grad_values = pl.pallas_call(
        functools.partial(total_kernel, parts),
        in_specs=[VMEM_SPEC] * (parts * ring + 1),
        out_specs=[VMEM_SPEC] * 2,
        out_shape=[jax.ShapeDtypeStruct((tokens, kv_heads, head_dim), jnp.float32)] * 2,
        compiler_params=params,
        name="total",
    )(near_kv, *sums)
    return (grad_queries, grad_keys, grad_values)


def solution(mesh):
    return jax.shard_map(
        body,
        mesh=mesh,
        in_specs=(
            P(("groups", "ctx", "sub"), "head", None),
            P(("groups", "ctx", "sub"), "head", None),
            P(("groups", "ctx", "sub"), "head", None),
            P(("groups", "ctx", "sub"), "head", None),
            P(("groups", "ctx", "sub"), "head"),
            P(("groups", "ctx", "sub"), "head"),
            P(("groups", "ctx", "sub")),
            P("groups", None),
        ),
        out_specs=(
            P(("groups", "ctx", "sub"), "head", None),
            P(("groups", "ctx", "sub"), "head", None),
            P(("groups", "ctx", "sub"), "head", None),
        ),
        check_vma=False,
    )
```

```python
import functools

import jax
import jax.numpy as jnp
from jax import lax
from jax.experimental import pallas as pl
from jax.experimental.pallas import tpu as pltpu
from jax.sharding import PartitionSpec as P

QH = 64
KVH = 4
LOG2E = 1.4426950408889634
ROWS = 2048
PARTS = 2
VMEM_LIMIT = 24 * 1024 * 1024

VMEM_SPEC = pl.BlockSpec(memory_space=pltpu.VMEM)
ANY_SPEC = pl.BlockSpec(memory_space=pl.ANY)
HBM_SPEC = pl.BlockSpec(memory_space=pltpu.HBM)


def rows_dot(left, right):
    return lax.dot_general(left, right, (((1,), (1,)), ((), ())), preferred_element_type=jnp.float32)


def tile_terms(key_blk, value_blk, query_blk, upstream, log_norm, row_terms, allowed, factor):
    scores = rows_dot(key_blk, query_blk)
    probs = jnp.exp2(scores * (factor * LOG2E) - log_norm)
    if allowed is not None:
        probs = jnp.where(allowed, probs, 0.0)
    grad_probs = rows_dot(value_blk, upstream)
    grad_scores = probs * (grad_probs - row_terms)
    return probs.astype(jnp.bfloat16), grad_scores.astype(jnp.bfloat16)


def chunks(tokens, grouped, rows):
    step = rows // grouped
    return [(i, slice(i * step, (i + 1) * step), slice(i * rows, (i + 1) * rows)) for i in range(tokens // step)]


def start_all(sources, targets, sems):
    copies = [pltpu.make_async_copy(source, target, sems.at[i]) for i, (source, target) in enumerate(zip(sources, targets))]
    for copy in copies:
        copy.start()
    return copies


def bring_rows(query_ref, up_ref, held_ref, sems, rows):
    _, count, tokens, grouped, _ = held_ref.shape
    copies = {}
    for head in range(count):
        heads = slice(head * grouped, (head + 1) * grouped)
        for i, toks, _ in chunks(tokens, grouped, rows):
            copies[head, i] = [
                pltpu.make_async_copy(ref.at[toks, heads], held_ref.at[kind, head, toks], sems.at[head, i, kind])
                for kind, ref in enumerate((query_ref, up_ref))
            ]
            for copy in copies[head, i]:
                copy.start()
    return copies


def row_blocks(held_ref, head, rows, copies=None):
    _, _, tokens, grouped, head_dim = held_ref.shape
    for i, toks, cols in chunks(tokens, grouped, rows):
        for copy in copies[head, i] if copies else ():
            copy.wait()
        yield toks, cols, *(held_ref[kind, head, toks].reshape(rows, head_dim) for kind in range(2))


def pack_kernel(key_ref, value_ref, kv_ref, held_ref, sems):
    copies = start_all((key_ref, value_ref), (held_ref.at[0], held_ref.at[1]), sems)
    for kind, copy in enumerate(copies):
        copy.wait()
        for head in range(held_ref.shape[2]):
            kv_ref[kind, head] = held_ref[kind, :, head, :]


def spread_kernel(
    grouped, ring, subs, norm_ref, term_ref, docs_ref, pairs_ref,
    norm_row_ref, term_row_ref, docs_row_ref, doc_col_ref, places_ref,
    held_ref, held_docs, held_pairs, sems,
):
    _, heads, tokens = held_ref.shape
    copies = start_all(
        (pairs_ref, docs_ref, norm_ref, term_ref), (held_pairs, held_docs, held_ref.at[0], held_ref.at[1]), sems
    )
    cols = tokens * grouped
    column = lax.broadcasted_iota(jnp.int32, (tokens, cols), 1)
    token = lax.broadcasted_iota(jnp.int32, (tokens, cols), 0)
    pick = jnp.where(token == column // grouped, 1.0, 0.0).astype(jnp.bfloat16)
    keep = lax.broadcasted_iota(jnp.int32, (grouped, cols), 0) == (
        lax.broadcasted_iota(jnp.int32, (grouped, cols), 1) % grouped
    )
    for copy in copies:
        copy.wait()

    ctx, sub = lax.axis_index("ctx"), lax.axis_index("sub")
    pairs = held_pairs[...]
    lane = lax.broadcasted_iota(jnp.int32, pairs.shape, 1)

    def listed_by(core):
        mask = lane == ctx * subs + core
        span = jnp.sum(jnp.where(mask, pairs, 0).astype(jnp.float32), axis=1, keepdims=True)
        span = jnp.broadcast_to(span, (2, places_ref.shape[1])).astype(jnp.int32)
        return span // subs, span % subs

    def around(gap):
        return jnp.where(gap < 0, gap + ring, gap)

    (mine, mine_sub), (other, other_sub) = listed_by(sub), listed_by(1 - sub)
    places_ref[0:2] = around(ctx - other)
    places_ref[2:4] = jnp.where(mine_sub == sub, around(ctx - mine), ring)
    places_ref[4:6] = jnp.where(mine_sub == sub, around(mine - ctx), ring)
    places_ref[6:8] = jnp.where(other_sub == sub, around(other - ctx), ring)

    pieces = []
    for value in (held_ref[0] * LOG2E, held_ref[1]):
        for _ in range(3):
            piece = value.astype(jnp.bfloat16)
            value = value - piece.astype(jnp.float32)
            pieces.append(piece)
    docs = held_docs[...].astype(jnp.float32)
    pieces.append(jnp.broadcast_to(docs, (grouped, tokens)).astype(jnp.bfloat16))
    spread = jnp.dot(jnp.concatenate(pieces, axis=0), pick, preferred_element_type=jnp.float32)
    for i, out_ref in enumerate((norm_row_ref, term_row_ref)):
        base = 3 * i * heads
        value = spread[base:base + heads] + spread[base + heads:base + 2 * heads]
        value = value + spread[base + 2 * heads:base + 3 * heads]
        for head in range(out_ref.shape[0]):
            group = value[head * grouped:(head + 1) * grouped]
            out_ref[head] = jnp.sum(jnp.where(keep, group, 0.0), axis=0, keepdims=True)
    docs_row_ref[...] = spread[6 * heads:6 * heads + 1]
    doc_col_ref[...] = jnp.broadcast_to(docs, (tokens, tokens)).T


def pick_block(sources, row):
    chosen = sources[0].astype(jnp.float32)
    for step in range(1, len(sources)):
        chosen = jnp.where(row == step, sources[step].astype(jnp.float32), chosen)
    return chosen.astype(jnp.bfloat16)


def choose_kernel(places_ref, *refs):
    *column, _, out_ref = refs
    for which in range(2):
        row = places_ref[which:which + 1]
        for kind in range(2):
            for head in range(out_ref.shape[2]):
                out_ref[which, kind, head] = pick_block([ref[kind, head] for ref in column], row)


def far_blocks(places_ref, column, other_ref, head):
    return [
        jnp.concatenate(
            [
                pick_block(
                    [ref[kind, head] for ref in column] + [other_ref[which, kind, head]],
                    places_ref[2 + which:3 + which],
                )
                for which in range(2)
            ],
            axis=0,
        )
        for kind in range(2)
    ]


def local_kernel(factor, rows, *refs):
    kv_ref, query_ref, up_ref, norm_ref, term_ref, docs_ref, doc_col_ref, dkv_ref, dq_ref, held_ref, sems = refs
    copies = bring_rows(query_ref, up_ref, held_ref, sems, rows)
    tokens, grouped, head_dim = held_ref.shape[2:]
    doc_col = jnp.concatenate([doc_col_ref[...]] * (rows // tokens), axis=1)
    for head in range(held_ref.shape[1]):
        key_blk, value_blk = kv_ref[0, head], kv_ref[1, head]
        grad_key = jnp.zeros((tokens, head_dim), jnp.float32)
        grad_val = jnp.zeros((tokens, head_dim), jnp.float32)
        for toks, cols, query_blk, upstream in row_blocks(held_ref, head, rows, copies):
            position = lax.broadcasted_iota(jnp.int32, (tokens, rows), 1) // grouped + toks.start
            allowed = (lax.broadcasted_iota(jnp.int32, (tokens, rows), 0) <= position) & (
                doc_col == docs_ref[:, cols]
            )
            probs, grads = tile_terms(
                key_blk, value_blk, query_blk, upstream, norm_ref[head, :, cols], term_ref[head, :, cols],
                allowed, factor,
            )
            grad_val += jnp.dot(probs, upstream, preferred_element_type=jnp.float32)
            grad_key += jnp.dot(grads, query_blk, preferred_element_type=jnp.float32)
            grad_query = lax.dot_general(
                grads, key_blk, (((0,), (0,)), ((), ())), preferred_element_type=jnp.float32
            )
            dq_ref[toks, head * grouped:(head + 1) * grouped] = (grad_query * factor).reshape(
                rows // grouped, grouped, head_dim
            )
        dkv_ref[0, head] = grad_key * factor
        dkv_ref[1, head] = grad_val


def listed_kernel(factor, rows, first, places_ref, *refs):
    *column, other_ref, held_ref, norm_ref, term_ref, _, dkv_ref = refs
    tokens, grouped, head_dim = held_ref.shape[2:]
    for head in range(dkv_ref.shape[2]):
        key_blk, value_blk = far_blocks(places_ref, column, other_ref, first + head)
        grad_key = jnp.zeros((2 * tokens, head_dim), jnp.float32)
        grad_val = jnp.zeros((2 * tokens, head_dim), jnp.float32)
        for toks, cols, query_blk, upstream in row_blocks(held_ref, first + head, rows):
            probs, grads = tile_terms(
                key_blk, value_blk, query_blk, upstream,
                norm_ref[first + head, :, cols], term_ref[first + head, :, cols], None, factor,
            )
            grad_val += jnp.dot(probs, upstream, preferred_element_type=jnp.float32)
            grad_key += jnp.dot(grads, query_blk, preferred_element_type=jnp.float32)
        grad_key = (grad_key * factor).astype(dkv_ref.dtype)
        grad_val = grad_val.astype(dkv_ref.dtype)
        for which in range(2):
            dkv_ref[which, 0, head] = grad_key[which * tokens:(which + 1) * tokens]
            dkv_ref[which, 1, head] = grad_val[which * tokens:(which + 1) * tokens]


def query_kernel(factor, rows, places_ref, *refs):
    *column, other_ref, held_ref, norm_ref, term_ref, near_ref, _, dq_ref = refs
    tokens, grouped, head_dim = held_ref.shape[2:]
    for head in range(held_ref.shape[1]):
        key_blk, value_blk = far_blocks(places_ref, column, other_ref, head)
        for toks, cols, query_blk, upstream in row_blocks(held_ref, head, rows):
            _, grads = tile_terms(
                key_blk, value_blk, query_blk, upstream, norm_ref[head, :, cols], term_ref[head, :, cols],
                None, factor,
            )
            grad_query = lax.dot_general(
                grads, key_blk, (((0,), (0,)), ((), ())), preferred_element_type=jnp.float32
            )
            heads = slice(head * grouped, (head + 1) * grouped)
            dq_ref[toks, heads] = near_ref[toks, heads] + (grad_query * factor).reshape(
                rows // grouped, grouped, head_dim
            )


def combine_kernel(places_ref, mine_ref, other_ref, *out_refs):
    for step, out_ref in enumerate(out_refs):
        for kind in range(2):
            for head in range(out_ref.shape[1]):
                total = None
                for i, ref in enumerate((mine_ref, other_ref)):
                    for which in range(2):
                        row = places_ref[4 + 2 * i + which:5 + 2 * i + which]
                        term = jnp.where(row == step, ref[which, kind, head].astype(jnp.float32), 0.0)
                        total = term if total is None else total + term
                out_ref[kind, head] = total.astype(out_ref.dtype)


def total_kernel(parts, near_ref, *refs):
    *blocks, dk_ref, dv_ref = refs
    count = len(blocks) // parts
    heads = dk_ref.shape[1]
    each = heads // parts
    for kind, out_ref in enumerate((dk_ref, dv_ref)):
        for head in range(heads):
            total = near_ref[kind, head]
            for ref in blocks[head // each * count:(head // each + 1) * count]:
                total += ref[kind, head % each].astype(jnp.float32)
            out_ref[:, head, :] = total


def body(queries, keys, values, grad_out, row_lse, row_delta, doc_ids, pairs):
    tokens, heads, head_dim = queries.shape
    kv_heads = keys.shape[1]
    grouped = QH // KVH
    factor = head_dim ** (-0.5)
    ring = lax.axis_size("ctx")
    subs = lax.axis_size("sub")
    rows = min(ROWS, tokens * grouped)
    cols = tokens * grouped
    parts = PARTS if kv_heads % PARTS == 0 else 1
    each = kv_heads // parts
    span_shape = (2, kv_heads, tokens, head_dim)
    part_shape = (2, each, tokens, head_dim)

    def shifted(array, shift):
        return lax.ppermute(array, "ctx", [(i, (i + shift) % ring) for i in range(ring)])

    def swapped(array):
        return lax.ppermute(array, "sub", [(i, i ^ 1) for i in range(subs)])

    def in_hbm(*arrays):
        return [pltpu.with_memory_space_constraint(array, pltpu.HBM) for array in arrays]

    params = pltpu.CompilerParams(vmem_limit_bytes=VMEM_LIMIT)
    kv = pl.pallas_call(
        pack_kernel,
        in_specs=[HBM_SPEC] * 2,
        out_specs=VMEM_SPEC,
        out_shape=jax.ShapeDtypeStruct(span_shape, jnp.bfloat16),
        scratch_shapes=[pltpu.VMEM((2, *keys.shape), jnp.bfloat16), pltpu.SemaphoreType.DMA((2,))],
        compiler_params=params,
        name="pack",
    )(*in_hbm(keys, values))
    column = [kv] + [shifted(kv, shift) for shift in range(1, ring)]

    norm, term, docs, doc_col, places = pl.pallas_call(
        functools.partial(spread_kernel, grouped, ring, subs),
        in_specs=[HBM_SPEC] * 4,
        out_specs=[VMEM_SPEC] * 5,
        out_shape=[
            jax.ShapeDtypeStruct((kv_heads, 1, cols), jnp.float32),
            jax.ShapeDtypeStruct((kv_heads, 1, cols), jnp.float32),
            jax.ShapeDtypeStruct((1, cols), jnp.float32),
            jax.ShapeDtypeStruct((tokens, tokens), jnp.float32),
            jax.ShapeDtypeStruct((8, head_dim), jnp.int32),
        ],
        scratch_shapes=[
            pltpu.VMEM((2, heads, tokens), jnp.float32),
            pltpu.VMEM((1, tokens), jnp.int32),
            pltpu.VMEM(pairs.shape[::-1], jnp.int32),
            pltpu.SemaphoreType.DMA((4,)),
        ],
        compiler_params=params,
        name="spread",
    )(*in_hbm(row_lse.T, row_delta.T, doc_ids.reshape(1, tokens), pairs.T))

    work = 2 * tokens * tokens * heads * head_dim
    moved = 2 * queries.size * 2

    row_specs = [VMEM_SPEC] * 3
    near_kv, near_query, held = pl.pallas_call(
        functools.partial(local_kernel, factor, rows),
        in_specs=[VMEM_SPEC] + [HBM_SPEC] * 2 + [VMEM_SPEC] * 4,
        out_specs=[VMEM_SPEC] * 3,
        out_shape=[
            jax.ShapeDtypeStruct((2, kv_heads, tokens, head_dim), jnp.float32),
            jax.ShapeDtypeStruct((tokens, heads, head_dim), jnp.float32),
            jax.ShapeDtypeStruct((2, kv_heads, tokens, grouped, head_dim), jnp.bfloat16),
        ],
        scratch_shapes=[pltpu.SemaphoreType.DMA((kv_heads, cols // rows, 2))],
        compiler_params=params,
        cost_estimate=pl.CostEstimate(flops=5 * work, bytes_accessed=2 * moved, transcendentals=0),
        name="local_block",
    )(kv, *in_hbm(queries, grad_out), norm, term, docs, doc_col)

    chosen = pl.pallas_call(
        choose_kernel,
        in_specs=[VMEM_SPEC] * (ring + 1) + [ANY_SPEC],
        out_specs=VMEM_SPEC,
        out_shape=jax.ShapeDtypeStruct((2, *span_shape), jnp.bfloat16),
        compiler_params=params,
        name="choose",
    )(places, *column, near_kv)
    other = swapped(chosen)

    sums = []
    far_kv = [near_kv]
    for part in range(parts):
        far_kv.append(
            pl.pallas_call(
                functools.partial(listed_kernel, factor, rows, part * each),
                in_specs=[VMEM_SPEC] * (ring + 2) + row_specs + [ANY_SPEC],
                out_specs=VMEM_SPEC,
                out_shape=jax.ShapeDtypeStruct((2, *part_shape), jnp.bfloat16),
                compiler_params=params,
                cost_estimate=pl.CostEstimate(
                    flops=8 * work // parts, bytes_accessed=moved // parts, transcendentals=0
                ),
                name="listed_keys",
            )(places, *column, other, held, norm, term, far_kv[-1])
        )
    for mine in far_kv[1:]:
        blocks = pl.pallas_call(
            combine_kernel,
            in_specs=[VMEM_SPEC] * 3,
            out_specs=[VMEM_SPEC] * ring,
            out_shape=[jax.ShapeDtypeStruct(part_shape, jnp.float32)]
            + [jax.ShapeDtypeStruct(part_shape, jnp.bfloat16)] * (ring - 1),
            compiler_params=params,
            name="combine",
        )(places, mine, swapped(mine))
        order = [*range(1, ring)] if mine is far_kv[1] else [ring - 1, *range(1, ring - 1)]
        sums += [blocks[0]] + [shifted(blocks[shift], shift) for shift in order]
        after = blocks[0]

    grad_queries = pl.pallas_call(
        functools.partial(query_kernel, factor, rows),
        in_specs=[VMEM_SPEC] * (2 + ring) + row_specs + [VMEM_SPEC, ANY_SPEC],
        out_specs=VMEM_SPEC,
        out_shape=jax.ShapeDtypeStruct((tokens, heads, head_dim), jnp.float32),
        compiler_params=params,
        cost_estimate=pl.CostEstimate(flops=6 * work, bytes_accessed=3 * moved, transcendentals=0),
        name="listed_queries",
    )(places, *column, other, held, norm, term, near_query, after)

    grad_keys, grad_values = pl.pallas_call(
        functools.partial(total_kernel, parts),
        in_specs=[VMEM_SPEC] * (parts * ring + 1),
        out_specs=[VMEM_SPEC] * 2,
        out_shape=[jax.ShapeDtypeStruct((tokens, kv_heads, head_dim), jnp.float32)] * 2,
        compiler_params=params,
        name="total",
    )(near_kv, *sums)
    return (grad_queries, grad_keys, grad_values)


def solution(mesh):
    return jax.shard_map(
        body,
        mesh=mesh,
        in_specs=(
            P(("groups", "ctx", "sub"), "head", None),
            P(("groups", "ctx", "sub"), "head", None),
            P(("groups", "ctx", "sub"), "head", None),
            P(("groups", "ctx", "sub"), "head", None),
            P(("groups", "ctx", "sub"), "head"),
            P(("groups", "ctx", "sub"), "head"),
            P(("groups", "ctx", "sub")),
            P("groups", None),
        ),
        out_specs=(
            P(("groups", "ctx", "sub"), "head", None),
            P(("groups", "ctx", "sub"), "head", None),
            P(("groups", "ctx", "sub"), "head", None),
        ),
        check_vma=False,
    )
```

```python
import functools

import jax
import jax.numpy as jnp
from jax import lax
from jax.experimental import pallas as pl
from jax.experimental.pallas import tpu as pltpu
from jax.sharding import PartitionSpec as P

QH = 64
KVH = 4
LOG2E = 1.4426950408889634
ROWS = 1024
PARTS = 1
VMEM_LIMIT = 24 * 1024 * 1024

VMEM_SPEC = pl.BlockSpec(memory_space=pltpu.VMEM)
ANY_SPEC = pl.BlockSpec(memory_space=pl.ANY)
HBM_SPEC = pl.BlockSpec(memory_space=pltpu.HBM)


def rows_dot(left, right):
    return lax.dot_general(left, right, (((1,), (1,)), ((), ())), preferred_element_type=jnp.float32)


def tile_terms(key_blk, value_blk, query_blk, upstream, log_norm, row_terms, allowed, factor):
    scores = rows_dot(key_blk, query_blk)
    probs = jnp.exp2(scores * (factor * LOG2E) - log_norm)
    if allowed is not None:
        probs = jnp.where(allowed, probs, 0.0)
    grad_probs = rows_dot(value_blk, upstream)
    grad_scores = probs * (grad_probs - row_terms)
    return probs.astype(jnp.bfloat16), grad_scores.astype(jnp.bfloat16)


def chunks(tokens, grouped, rows):
    step = rows // grouped
    return [(i, slice(i * step, (i + 1) * step), slice(i * rows, (i + 1) * rows)) for i in range(tokens // step)]


def start_all(sources, targets, sems):
    copies = [pltpu.make_async_copy(source, target, sems.at[i]) for i, (source, target) in enumerate(zip(sources, targets))]
    for copy in copies:
        copy.start()
    return copies


def bring_rows(query_ref, up_ref, held_ref, sems, rows):
    _, count, tokens, grouped, _ = held_ref.shape
    copies = {}
    for head in range(count):
        heads = slice(head * grouped, (head + 1) * grouped)
        for i, toks, _ in chunks(tokens, grouped, rows):
            copies[head, i] = [
                pltpu.make_async_copy(ref.at[toks, heads], held_ref.at[kind, head, toks], sems.at[head, i, kind])
                for kind, ref in enumerate((query_ref, up_ref))
            ]
            for copy in copies[head, i]:
                copy.start()
    return copies


def row_blocks(held_ref, head, rows, copies=None):
    _, _, tokens, grouped, head_dim = held_ref.shape
    for i, toks, cols in chunks(tokens, grouped, rows):
        for copy in copies[head, i] if copies else ():
            copy.wait()
        yield toks, cols, *(held_ref[kind, head, toks].reshape(rows, head_dim) for kind in range(2))


def pack_kernel(key_ref, value_ref, kv_ref, held_ref, sems):
    copies = start_all((key_ref, value_ref), (held_ref.at[0], held_ref.at[1]), sems)
    for kind, copy in enumerate(copies):
        copy.wait()
        for head in range(held_ref.shape[2]):
            kv_ref[kind, head] = held_ref[kind, :, head, :]


def spread_kernel(
    grouped, ring, subs, norm_ref, term_ref, docs_ref, pairs_ref,
    norm_row_ref, term_row_ref, docs_row_ref, doc_col_ref, places_ref,
    held_ref, held_docs, held_pairs, sems,
):
    _, heads, tokens = held_ref.shape
    copies = start_all(
        (pairs_ref, docs_ref, norm_ref, term_ref), (held_pairs, held_docs, held_ref.at[0], held_ref.at[1]), sems
    )
    cols = tokens * grouped
    column = lax.broadcasted_iota(jnp.int32, (tokens, cols), 1)
    token = lax.broadcasted_iota(jnp.int32, (tokens, cols), 0)
    pick = jnp.where(token == column // grouped, 1.0, 0.0).astype(jnp.bfloat16)
    keep = lax.broadcasted_iota(jnp.int32, (grouped, cols), 0) == (
        lax.broadcasted_iota(jnp.int32, (grouped, cols), 1) % grouped
    )
    for copy in copies:
        copy.wait()

    ctx, sub = lax.axis_index("ctx"), lax.axis_index("sub")
    pairs = held_pairs[...]
    lane = lax.broadcasted_iota(jnp.int32, pairs.shape, 1)

    def listed_by(core):
        mask = lane == ctx * subs + core
        span = jnp.sum(jnp.where(mask, pairs, 0).astype(jnp.float32), axis=1, keepdims=True)
        span = jnp.broadcast_to(span, (2, places_ref.shape[1])).astype(jnp.int32)
        return span // subs, span % subs

    def around(gap):
        return jnp.where(gap < 0, gap + ring, gap)

    (mine, mine_sub), (other, other_sub) = listed_by(sub), listed_by(1 - sub)
    places_ref[0:2] = around(ctx - other)
    places_ref[2:4] = jnp.where(mine_sub == sub, around(ctx - mine), ring)
    places_ref[4:6] = jnp.where(mine_sub == sub, around(mine - ctx), ring)
    places_ref[6:8] = jnp.where(other_sub == sub, around(other - ctx), ring)

    pieces = []
    for value in (held_ref[0] * LOG2E, held_ref[1]):
        for _ in range(3):
            piece = value.astype(jnp.bfloat16)
            value = value - piece.astype(jnp.float32)
            pieces.append(piece)
    docs = held_docs[...].astype(jnp.float32)
    pieces.append(jnp.broadcast_to(docs, (grouped, tokens)).astype(jnp.bfloat16))
    spread = jnp.dot(jnp.concatenate(pieces, axis=0), pick, preferred_element_type=jnp.float32)
    for i, out_ref in enumerate((norm_row_ref, term_row_ref)):
        base = 3 * i * heads
        value = spread[base:base + heads] + spread[base + heads:base + 2 * heads]
        value = value + spread[base + 2 * heads:base + 3 * heads]
        for head in range(out_ref.shape[0]):
            group = value[head * grouped:(head + 1) * grouped]
            out_ref[head] = jnp.sum(jnp.where(keep, group, 0.0), axis=0, keepdims=True)
    docs_row_ref[...] = spread[6 * heads:6 * heads + 1]
    doc_col_ref[...] = jnp.broadcast_to(docs, (tokens, tokens)).T


def pick_block(sources, row):
    chosen = sources[0].astype(jnp.float32)
    for step in range(1, len(sources)):
        chosen = jnp.where(row == step, sources[step].astype(jnp.float32), chosen)
    return chosen.astype(jnp.bfloat16)


def choose_kernel(places_ref, *refs):
    *column, _, out_ref = refs
    for which in range(2):
        row = places_ref[which:which + 1]
        for kind in range(2):
            for head in range(out_ref.shape[2]):
                out_ref[which, kind, head] = pick_block([ref[kind, head] for ref in column], row)


def far_blocks(places_ref, column, other_ref, head):
    return [
        jnp.concatenate(
            [
                pick_block(
                    [ref[kind, head] for ref in column] + [other_ref[which, kind, head]],
                    places_ref[2 + which:3 + which],
                )
                for which in range(2)
            ],
            axis=0,
        )
        for kind in range(2)
    ]


def local_kernel(factor, rows, *refs):
    kv_ref, query_ref, up_ref, norm_ref, term_ref, docs_ref, doc_col_ref, dkv_ref, dq_ref, held_ref, sems = refs
    copies = bring_rows(query_ref, up_ref, held_ref, sems, rows)
    tokens, grouped, head_dim = held_ref.shape[2:]
    doc_col = jnp.concatenate([doc_col_ref[...]] * (rows // tokens), axis=1)
    for head in range(held_ref.shape[1]):
        key_blk, value_blk = kv_ref[0, head], kv_ref[1, head]
        grad_key = jnp.zeros((tokens, head_dim), jnp.float32)
        grad_val = jnp.zeros((tokens, head_dim), jnp.float32)
        for toks, cols, query_blk, upstream in row_blocks(held_ref, head, rows, copies):
            position = lax.broadcasted_iota(jnp.int32, (tokens, rows), 1) // grouped + toks.start
            allowed = (lax.broadcasted_iota(jnp.int32, (tokens, rows), 0) <= position) & (
                doc_col == docs_ref[:, cols]
            )
            probs, grads = tile_terms(
                key_blk, value_blk, query_blk, upstream, norm_ref[head, :, cols], term_ref[head, :, cols],
                allowed, factor,
            )
            grad_val += jnp.dot(probs, upstream, preferred_element_type=jnp.float32)
            grad_key += jnp.dot(grads, query_blk, preferred_element_type=jnp.float32)
            grad_query = lax.dot_general(
                grads, key_blk, (((0,), (0,)), ((), ())), preferred_element_type=jnp.float32
            )
            dq_ref[toks, head * grouped:(head + 1) * grouped] = (grad_query * factor).reshape(
                rows // grouped, grouped, head_dim
            )
        dkv_ref[0, head] = grad_key * factor
        dkv_ref[1, head] = grad_val


def listed_kernel(factor, rows, first, places_ref, *refs):
    *column, other_ref, held_ref, norm_ref, term_ref, _, dkv_ref = refs
    tokens, grouped, head_dim = held_ref.shape[2:]
    for head in range(dkv_ref.shape[2]):
        key_blk, value_blk = far_blocks(places_ref, column, other_ref, first + head)
        grad_key = jnp.zeros((2 * tokens, head_dim), jnp.float32)
        grad_val = jnp.zeros((2 * tokens, head_dim), jnp.float32)
        for toks, cols, query_blk, upstream in row_blocks(held_ref, first + head, rows):
            probs, grads = tile_terms(
                key_blk, value_blk, query_blk, upstream,
                norm_ref[first + head, :, cols], term_ref[first + head, :, cols], None, factor,
            )
            grad_val += jnp.dot(probs, upstream, preferred_element_type=jnp.float32)
            grad_key += jnp.dot(grads, query_blk, preferred_element_type=jnp.float32)
        grad_key = (grad_key * factor).astype(dkv_ref.dtype)
        grad_val = grad_val.astype(dkv_ref.dtype)
        for which in range(2):
            dkv_ref[which, 0, head] = grad_key[which * tokens:(which + 1) * tokens]
            dkv_ref[which, 1, head] = grad_val[which * tokens:(which + 1) * tokens]


def query_kernel(factor, rows, places_ref, *refs):
    *column, other_ref, held_ref, norm_ref, term_ref, near_ref, _, dq_ref = refs
    tokens, grouped, head_dim = held_ref.shape[2:]
    for head in range(held_ref.shape[1]):
        key_blk, value_blk = far_blocks(places_ref, column, other_ref, head)
        for toks, cols, query_blk, upstream in row_blocks(held_ref, head, rows):
            _, grads = tile_terms(
                key_blk, value_blk, query_blk, upstream, norm_ref[head, :, cols], term_ref[head, :, cols],
                None, factor,
            )
            grad_query = lax.dot_general(
                grads, key_blk, (((0,), (0,)), ((), ())), preferred_element_type=jnp.float32
            )
            heads = slice(head * grouped, (head + 1) * grouped)
            dq_ref[toks, heads] = near_ref[toks, heads] + (grad_query * factor).reshape(
                rows // grouped, grouped, head_dim
            )


def combine_kernel(places_ref, mine_ref, other_ref, *out_refs):
    for step, out_ref in enumerate(out_refs):
        for kind in range(2):
            for head in range(out_ref.shape[1]):
                total = None
                for i, ref in enumerate((mine_ref, other_ref)):
                    for which in range(2):
                        row = places_ref[4 + 2 * i + which:5 + 2 * i + which]
                        term = jnp.where(row == step, ref[which, kind, head].astype(jnp.float32), 0.0)
                        total = term if total is None else total + term
                out_ref[kind, head] = total.astype(out_ref.dtype)


def total_kernel(parts, near_ref, *refs):
    *blocks, dk_ref, dv_ref = refs
    count = len(blocks) // parts
    heads = dk_ref.shape[1]
    each = heads // parts
    for kind, out_ref in enumerate((dk_ref, dv_ref)):
        for head in range(heads):
            total = near_ref[kind, head]
            for ref in blocks[head // each * count:(head // each + 1) * count]:
                total += ref[kind, head % each].astype(jnp.float32)
            out_ref[:, head, :] = total


def body(queries, keys, values, grad_out, row_lse, row_delta, doc_ids, pairs):
    tokens, heads, head_dim = queries.shape
    kv_heads = keys.shape[1]
    grouped = QH // KVH
    factor = head_dim ** (-0.5)
    ring = lax.axis_size("ctx")
    subs = lax.axis_size("sub")
    rows = min(ROWS, tokens * grouped)
    cols = tokens * grouped
    parts = PARTS if kv_heads % PARTS == 0 else 1
    each = kv_heads // parts
    span_shape = (2, kv_heads, tokens, head_dim)
    part_shape = (2, each, tokens, head_dim)

    def shifted(array, shift):
        return lax.ppermute(array, "ctx", [(i, (i + shift) % ring) for i in range(ring)])

    def swapped(array):
        return lax.ppermute(array, "sub", [(i, i ^ 1) for i in range(subs)])

    def in_hbm(*arrays):
        return [pltpu.with_memory_space_constraint(array, pltpu.HBM) for array in arrays]

    params = pltpu.CompilerParams(vmem_limit_bytes=VMEM_LIMIT)
    kv = pl.pallas_call(
        pack_kernel,
        in_specs=[HBM_SPEC] * 2,
        out_specs=VMEM_SPEC,
        out_shape=jax.ShapeDtypeStruct(span_shape, jnp.bfloat16),
        scratch_shapes=[pltpu.VMEM((2, *keys.shape), jnp.bfloat16), pltpu.SemaphoreType.DMA((2,))],
        compiler_params=params,
        name="pack",
    )(*in_hbm(keys, values))
    column = [kv] + [shifted(kv, shift) for shift in range(1, ring)]

    norm, term, docs, doc_col, places = pl.pallas_call(
        functools.partial(spread_kernel, grouped, ring, subs),
        in_specs=[HBM_SPEC] * 4,
        out_specs=[VMEM_SPEC] * 5,
        out_shape=[
            jax.ShapeDtypeStruct((kv_heads, 1, cols), jnp.float32),
            jax.ShapeDtypeStruct((kv_heads, 1, cols), jnp.float32),
            jax.ShapeDtypeStruct((1, cols), jnp.float32),
            jax.ShapeDtypeStruct((tokens, tokens), jnp.float32),
            jax.ShapeDtypeStruct((8, head_dim), jnp.int32),
        ],
        scratch_shapes=[
            pltpu.VMEM((2, heads, tokens), jnp.float32),
            pltpu.VMEM((1, tokens), jnp.int32),
            pltpu.VMEM(pairs.shape[::-1], jnp.int32),
            pltpu.SemaphoreType.DMA((4,)),
        ],
        compiler_params=params,
        name="spread",
    )(*in_hbm(row_lse.T, row_delta.T, doc_ids.reshape(1, tokens), pairs.T))

    work = 2 * tokens * tokens * heads * head_dim
    moved = 2 * queries.size * 2

    row_specs = [VMEM_SPEC] * 3
    near_kv, near_query, held = pl.pallas_call(
        functools.partial(local_kernel, factor, rows),
        in_specs=[VMEM_SPEC] + [HBM_SPEC] * 2 + [VMEM_SPEC] * 4,
        out_specs=[VMEM_SPEC] * 3,
        out_shape=[
            jax.ShapeDtypeStruct((2, kv_heads, tokens, head_dim), jnp.float32),
            jax.ShapeDtypeStruct((tokens, heads, head_dim), jnp.float32),
            jax.ShapeDtypeStruct((2, kv_heads, tokens, grouped, head_dim), jnp.bfloat16),
        ],
        scratch_shapes=[pltpu.SemaphoreType.DMA((kv_heads, cols // rows, 2))],
        compiler_params=params,
        cost_estimate=pl.CostEstimate(flops=5 * work, bytes_accessed=2 * moved, transcendentals=0),
        name="local_block",
    )(kv, *in_hbm(queries, grad_out), norm, term, docs, doc_col)

    chosen = pl.pallas_call(
        choose_kernel,
        in_specs=[VMEM_SPEC] * (ring + 1) + [ANY_SPEC],
        out_specs=VMEM_SPEC,
        out_shape=jax.ShapeDtypeStruct((2, *span_shape), jnp.bfloat16),
        compiler_params=params,
        name="choose",
    )(places, *column, near_kv)
    other = swapped(chosen)

    sums = []
    far_kv = [near_kv]
    for part in range(parts):
        far_kv.append(
            pl.pallas_call(
                functools.partial(listed_kernel, factor, rows, part * each),
                in_specs=[VMEM_SPEC] * (ring + 2) + row_specs + [ANY_SPEC],
                out_specs=VMEM_SPEC,
                out_shape=jax.ShapeDtypeStruct((2, *part_shape), jnp.bfloat16),
                compiler_params=params,
                cost_estimate=pl.CostEstimate(
                    flops=8 * work // parts, bytes_accessed=moved // parts, transcendentals=0
                ),
                name="listed_keys",
            )(places, *column, other, held, norm, term, far_kv[-1])
        )
    for mine in far_kv[1:]:
        blocks = pl.pallas_call(
            combine_kernel,
            in_specs=[VMEM_SPEC] * 3,
            out_specs=[VMEM_SPEC] * ring,
            out_shape=[jax.ShapeDtypeStruct(part_shape, jnp.float32)]
            + [jax.ShapeDtypeStruct(part_shape, jnp.bfloat16)] * (ring - 1),
            compiler_params=params,
            name="combine",
        )(places, mine, swapped(mine))
        order = [*range(1, ring)] if mine is far_kv[1] else [ring - 1, *range(1, ring - 1)]
        sums += [blocks[0]] + [shifted(blocks[shift], shift) for shift in order]
        after = blocks[0]

    grad_queries = pl.pallas_call(
        functools.partial(query_kernel, factor, rows),
        in_specs=[VMEM_SPEC] * (2 + ring) + row_specs + [VMEM_SPEC, ANY_SPEC],
        out_specs=VMEM_SPEC,
        out_shape=jax.ShapeDtypeStruct((tokens, heads, head_dim), jnp.float32),
        compiler_params=params,
        cost_estimate=pl.CostEstimate(flops=6 * work, bytes_accessed=3 * moved, transcendentals=0),
        name="listed_queries",
    )(places, *column, other, held, norm, term, near_query, after)

    grad_keys, grad_values = pl.pallas_call(
        functools.partial(total_kernel, parts),
        in_specs=[VMEM_SPEC] * (parts * ring + 1),
        out_specs=[VMEM_SPEC] * 2,
        out_shape=[jax.ShapeDtypeStruct((tokens, kv_heads, head_dim), jnp.float32)] * 2,
        compiler_params=params,
        name="total",
    )(near_kv, *sums)
    return (grad_queries, grad_keys, grad_values)


def solution(mesh):
    return jax.shard_map(
        body,
        mesh=mesh,
        in_specs=(
            P(("groups", "ctx", "sub"), "head", None),
            P(("groups", "ctx", "sub"), "head", None),
            P(("groups", "ctx", "sub"), "head", None),
            P(("groups", "ctx", "sub"), "head", None),
            P(("groups", "ctx", "sub"), "head"),
            P(("groups", "ctx", "sub"), "head"),
            P(("groups", "ctx", "sub")),
            P("groups", None),
        ),
        out_specs=(
            P(("groups", "ctx", "sub"), "head", None),
            P(("groups", "ctx", "sub"), "head", None),
            P(("groups", "ctx", "sub"), "head", None),
        ),
        check_vma=False,
    )
```
